128 devices in a mesh: slide: 16 (over y, x), seq: 8 (over z, core).
Axes of the slice: x: 4, y: 4, z: 4, core: 2. Of those that a mesh axis runs over, the one named last changes fastest.
Arguments:
- tile_feats: bfloat16 [49152, 1536], P(('slide', 'seq')), may hold values from -6 to 6
- norm_gain: float32 [1536], replicated, may hold values from 0.1 to 1.9
- w_embed: bfloat16 [1536, 768], replicated, may hold values from -0.15625 to 0.15625
- slide_of_tile: int32 [49152, 1], P(('slide', 'seq')), may hold values from 0 to 15; in each aligned block of 384 rows (0 to 383, 384 to 767, ...) at most 48 rows name the same one
- w_qkv: bfloat16 [768, 2304], replicated, may hold values from -2 to 2
- w_out: bfloat16 [768, 768], replicated, may hold values from -0.21875 to 0.21875
- cotangent: bfloat16 [16, 6144, 768], P('slide', 'seq'), may hold values from -6 to 6
Outputs:
- attended: bfloat16 [16, 6144, 768], P('slide', 'seq')
- grad_qkv: float32 [768, 2304], P(('slide', 'seq'))
- grad_out: float32 [768, 768], P(('slide', 'seq'))
The draws below stay inside these ranges and needn't reach their ends.
Inputs may be any that keep to these rules, and one draw needn't show every extreme that they name: `slide_of_tile`: among one device's 384 tiles at most 48 name the same slide, a bound that some block reaches of them.
All inputs are finite; a program needn't handle non-finite values.
Results may differ from the reference program's by a relative error of at most 0.03.
The reference program's roundings to bfloat16 on the way count: a program that leaves them out, or rounds other values in their place, can miss the bound.
Values may be sent and summed in bfloat16 or wider, within the bound.
A program may use at most 128 MiB of HBM per device.

```python
import math
import jax
import jax.numpy as jnp
import numpy as np
from jax import lax

WIDE = 1536
D = 768
HEADS = 12
TILE_DEV = 384
CAP = 48
RATE = 8
SLIDES = 16
L_DEV = 768
SEQ_LEN = 6144
TILES = 49152
N_SLIDE = 16
N_SEQ = 8


def draw_w_qkv(key, part):
    key = jax.random.fold_in(key, 7)
    base_key = jax.random.fold_in(key, 0)
    entries = jax.random.truncated_normal(base_key, -6.0, 6.0, (D, 3 * D), jnp.float32) * D ** (-0.5)
    return entries.astype(jnp.bfloat16)


def levels(own_key, shape, cuts, low, high):
    factor_of, own = 1.0, jax.random.fold_in(own_key, 6)
    for position, parts in cuts:
        heights = jnp.exp(jax.random.uniform(jax.random.fold_in(own, position), (parts,), jnp.float32, low / len(cuts), high / len(cuts)))
        factor_of = factor_of * jnp.repeat(heights, shape[position] // parts).reshape([-1 if axis == position else 1 for axis in range(len(shape))])
    return factor_of


def assign_block(stream_key, own, number, rows, count, top, most, slope):
    sequence = jax.random.permutation(stream_key, count)
    heavy_load, ordinary = load_shares(count, rows * top, most, slope, True), load_shares(count, rows * top, most, slope, False)
    places = jnp.arange(count)

    def named(lengths, rotation):
        used = int((lengths > 0).sum())
        fixed = max(1, used // 4)
        moved = fixed + (places - fixed + rotation * (used - fixed)) % max(1, count - fixed)
        return jnp.zeros((count,), jnp.int32).at[sequence[jnp.where(places < fixed, places, moved)]].set(jnp.asarray(lengths, jnp.int32))

    lengths = jnp.where(number % 4 == 0, named(heavy_load, number // 4), named(ordinary, number - number // 4 - 1))
    mixed = jax.random.permutation(jax.random.fold_in(own, 3), count)
    giver, taker = mixed[0:count // 2 * 2:2], mixed[1:count // 2 * 2:2]
    slack = jnp.minimum(lengths[giver] - 1, most - lengths[taker]) // 2
    slack = jnp.where((giver == sequence[0]) | (taker == sequence[0]) | (lengths[taker] == 0), 0, jnp.maximum(slack, 0))
    moved = jax.random.randint(jax.random.fold_in(own, 4), (count // 2,), 0, 1 << 20) % (slack + 1)
    lengths = lengths.at[giver].add(-moved).at[taker].add(moved)
    items = jnp.searchsorted(jnp.cumsum(lengths), jnp.arange(rows * top), side="right").astype(jnp.int32)
    table = items.reshape(top, rows).T
    table = table[jax.random.permutation(jax.random.fold_in(own, 1), rows)]
    rotation = jax.random.randint(jax.random.fold_in(own, 2), (rows, 1), 0, top)
    return jnp.take_along_axis(table, (jnp.arange(top)[None, :] + rotation) % top, axis=1)


def load_shares(count, total, bound, lean, full):
    loads = [(1 << 20) // math.isqrt(standing ** lean) + 1 for standing in range(1, count + 1)]
    largest = bound if full else min(bound, max(-(-total // count), total * loads[0] // sum(loads)))
    least = 1 if total - largest >= count - 1 else 0
    given, surplus = [largest] + [least] * (count - 1), total - largest - least * (count - 1)
    while surplus > 0:
        free = [i for i in range(1, count) if given[i] < largest] or [i for i in range(1, count) if given[i] < bound]
        whole, remaining = sum([loads[i] for i in free]), surplus
        for i in free:
            extra = min(bound - given[i], max(1, remaining * loads[i] // whole), surplus)
            given[i] = given[i] + extra
            surplus = surplus - extra
    return np.array(given)


def gaussian(rng, extent, scale, bound, cuts=(), kind=jnp.bfloat16):
    loudness = levels(rng, extent, cuts, -0.22, 0.18) if cuts else 1.0
    drawn = jax.random.normal(rng, extent, jnp.float32) * scale * loudness
    return jnp.minimum(jnp.maximum(drawn, -bound), bound).astype(kind)


def setup_inputs(seed: int = 0) -> dict:
    streams_of = jax.random.split(jax.random.key(seed), 8)
    tile_feats = gaussian(streams_of[0], (TILES, WIDE), 1.0, 6.0, ((0, 128),))
    norm_gain = jnp.clip(1.0 + 0.18 * jax.random.normal(streams_of[1], (WIDE,), jnp.float32), 0.1, 1.9)
    w_embed = gaussian(streams_of[2], (WIDE, D), WIDE ** -0.5, 0.15625)
    slide_of_tile_keys = jax.random.split(jax.random.fold_in(streams_of[3], 1), TILES // TILE_DEV)
    slide_of_tile_turns = jax.random.permutation(jax.random.fold_in(streams_of[3], 3), TILES // TILE_DEV)
    slide_of_tile = jax.vmap(lambda own, number: assign_block(jax.random.fold_in(streams_of[3], 2), own, number, TILE_DEV, SLIDES, 1, CAP, 2))(slide_of_tile_keys, slide_of_tile_turns).reshape((TILES, 1))
    w_qkv = draw_w_qkv(jax.random.fold_in(streams_of[7], 71), 0)
    w_out = gaussian(streams_of[5], (D, D), D ** -0.5, 0.21875)
    cotangent = gaussian(streams_of[6], (SLIDES, SEQ_LEN, D), 1.0, 6.0, ((0, 16), (1, 8)))
    return {"tile_feats": tile_feats, "norm_gain": norm_gain, "w_embed": w_embed, "slide_of_tile": slide_of_tile, "w_qkv": w_qkv, "w_out": w_out, "cotangent": cotangent}


masked_value = -1e+30

def embed_tiles(feats, norm_gain, w_embed):
    values = feats.astype(jnp.float32)
    center = lax.optimization_barrier(jnp.mean(values, axis=-1, keepdims=True))
    spread = lax.optimization_barrier(jnp.mean((values - center) ** 2, axis=-1, keepdims=True))
    normed = ((values - center) * lax.rsqrt(spread + 1e-06) * norm_gain).astype(jnp.bfloat16)
    return jnp.dot(normed, w_embed, preferred_element_type=jnp.float32).astype(jnp.bfloat16)

def place_tiles(embedded, targets, slides):
    one_hot = (targets[:, None] == jnp.arange(slides, dtype=jnp.int32)[None, :]).astype(jnp.int32)
    order_rank = lax.optimization_barrier(jnp.sum((jnp.cumsum(one_hot, axis=0) - 1) * one_hot, axis=1))
    slot_index = (targets * CAP + order_rank).astype(jnp.int32)
    placing = (jnp.arange(slides * CAP, dtype=jnp.int32)[:, None] == slot_index[None, :]).astype(jnp.bfloat16)
    buffer = jnp.dot(placing, embedded, preferred_element_type=jnp.float32).astype(jnp.bfloat16)
    return (buffer, lax.optimization_barrier(jnp.sum(one_hot, axis=0)).astype(jnp.int32))

def head_pass(query, local_keys, local_values, far_keys, far_values, d_head, key_mask):
    scale = query.shape[-1] ** (-0.5)
    keys_all = jnp.concatenate([local_keys, far_keys], axis=0)
    values_all = jnp.concatenate([local_values, far_values], axis=0)
    scores = jnp.dot(query, keys_all.T, preferred_element_type=jnp.float32) * scale
    scores = jnp.where(key_mask[None, :], scores, masked_value)
    peak = lax.optimization_barrier(jnp.max(scores, axis=-1, keepdims=True))
    raw_weights = jnp.exp(scores - peak)
    prob_exact = raw_weights / lax.optimization_barrier(jnp.sum(raw_weights, axis=-1, keepdims=True))
    prob_bf16 = prob_exact.astype(jnp.bfloat16)
    head_output = jnp.dot(prob_bf16, values_all, preferred_element_type=jnp.float32).astype(jnp.bfloat16)
    grad_p = jnp.dot(d_head, values_all.T, preferred_element_type=jnp.float32)
    row_delta = lax.optimization_barrier(jnp.sum(d_head.astype(jnp.float32) * head_output.astype(jnp.float32), axis=-1, keepdims=True))
    grad_s = (prob_exact * (grad_p - row_delta)).astype(jnp.bfloat16)
    grad_query = (jnp.dot(grad_s, keys_all, preferred_element_type=jnp.float32) * scale).astype(jnp.bfloat16)
    grad_key = jnp.dot(grad_s.T, query, preferred_element_type=jnp.float32) * scale
    grad_value = jnp.dot(prob_bf16.T, d_head, preferred_element_type=jnp.float32)
    local_count = local_keys.shape[0]
    return (head_output, grad_query, grad_key[:local_count].astype(jnp.bfloat16), grad_value[:local_count].astype(jnp.bfloat16), grad_key[local_count:], grad_value[local_count:])

def block_pass(rows_in, valid, qkv, kv_dilated, valid_dilated, grad_rows, w_out):
    width = rows_in.shape[1]
    head_size = width // HEADS

    def to_heads(array):
        return array.reshape(array.shape[0], HEADS, head_size).transpose(1, 0, 2)

    def from_heads(array):
        return array.transpose(1, 0, 2).reshape(array.shape[1], HEADS * head_size)
    masked_grad = (grad_rows.astype(jnp.float32) * valid[:, None]).astype(jnp.bfloat16)
    d_heads = jnp.dot(masked_grad, w_out.T, preferred_element_type=jnp.float32).astype(jnp.bfloat16)
    key_mask = jnp.concatenate([valid, valid_dilated]) > 0.5
    results = lax.map(lambda group: head_pass(*group, key_mask), (to_heads(qkv[:, :width]), to_heads(qkv[:, width:2 * width]), to_heads(qkv[:, 2 * width:]), to_heads(kv_dilated[:, :width]), to_heads(kv_dilated[:, width:]), to_heads(d_heads)))
    heads_out = from_heads(results[0])
    mixed = rows_in.astype(jnp.float32) + jnp.dot(heads_out, w_out, preferred_element_type=jnp.float32)
    output = (mixed * valid[:, None]).astype(jnp.bfloat16)
    grad_mix = jnp.dot(heads_out.T, masked_grad, preferred_element_type=jnp.float32)
    local_grads = jnp.concatenate([from_heads(results[1]), from_heads(results[2]), from_heads(results[3])], axis=1)
    grad_proj = jnp.dot(rows_in.T, local_grads, preferred_element_type=jnp.float32)
    dilated_grad = jnp.concatenate([from_heads(results[4]), from_heads(results[5])], axis=1)
    return (output, grad_proj, grad_mix, dilated_grad)

def reference(tile_feats, norm_gain, w_embed, slide_of_tile, w_qkv, w_out, cotangent):
    embedded = embed_tiles(tile_feats, norm_gain, w_embed).reshape(N_SLIDE, N_SEQ, TILE_DEV, D)
    targets = slide_of_tile[:, 0].reshape(N_SLIDE, N_SEQ, TILE_DEV)
    buffers, counts = jax.vmap(jax.vmap(lambda rows, aims: place_tiles(rows, aims, N_SLIDE)))(embedded, targets)
    seq_x = buffers.reshape(N_SLIDE, N_SEQ, N_SLIDE, CAP, D).transpose(2, 1, 0, 3, 4).reshape(SLIDES, SEQ_LEN, D)
    counts_owner = counts.transpose(2, 1, 0)
    valid_all = (jnp.arange(CAP, dtype=jnp.int32)[None, None, None, :] < counts_owner[..., None]).astype(jnp.float32)
    valid_all = valid_all.reshape(SLIDES, SEQ_LEN)
    factor = (SLIDES * SEQ_LEN) ** (-0.5)

    def per_slide(carry, inputs):
        rows_in, valid, grad_rows = inputs
        qkv = jnp.dot(rows_in, w_qkv, preferred_element_type=jnp.float32).astype(jnp.bfloat16)
        kv_dilated = qkv[::RATE, D:]
        valid_dilated = valid[::RATE]
        rows_dilated = rows_in[::RATE]
        results = lax.map(lambda group: block_pass(group[0], group[1], group[2], kv_dilated, valid_dilated, group[3], w_out), (rows_in.reshape(N_SEQ, L_DEV, D), valid.reshape(N_SEQ, L_DEV), qkv.reshape(N_SEQ, L_DEV, 3 * D), grad_rows.reshape(N_SEQ, L_DEV, D)))
        grad_proj = lax.optimization_barrier(jnp.sum(results[1], axis=0))
        grad_mix = lax.optimization_barrier(jnp.sum(results[2], axis=0))
        dilated_grad = lax.optimization_barrier(jnp.sum(results[3], axis=0))
        dilated_term = jnp.dot(rows_dilated.astype(jnp.float32).T, dilated_grad, precision=lax.Precision.HIGHEST)
        grad_proj = jnp.concatenate([grad_proj[:, :D], grad_proj[:, D:] + dilated_term], axis=1)
        return ((carry[0] + grad_proj, carry[1] + grad_mix), results[0].reshape(SEQ_LEN, D))
    start = (jnp.zeros((D, 3 * D), jnp.float32), jnp.zeros((D, D), jnp.float32))
    totals, attended = lax.scan(per_slide, start, (seq_x, valid_all, cotangent))
    return (attended, totals[0] * factor, totals[1] * factor)
```

```python
import functools

import jax
import jax.numpy as jnp
import numpy as np
from jax import lax
from jax.experimental import pallas as pl
from jax.experimental.pallas import tpu as pltpu
from jax.sharding import PartitionSpec as P

HEADS = 12
CAP = 48
RATE = 8
WIDTH = 768
SLOTS = 768
KEYS = 1536
BLOCK = 256
SIDE = 4
THIRD = 1024
MASKED = -1e30
BF16 = jnp.bfloat16
F32 = jnp.float32
MESH = pl.DeviceIdType.MESH
ORDERS = (("x", "y", "z"), ("y", "z", "x"), ("z", "x", "y"))
NT = (((1,), (1,)), ((), ()))


def embed_tiles(feats, norm_gain, w_embed):
    values = feats.astype(F32)
    center = jnp.mean(values, axis=-1, keepdims=True)
    spread = jnp.mean((values - center) ** 2, axis=-1, keepdims=True)
    normed = ((values - center) * lax.rsqrt(spread + 1e-06) * norm_gain).astype(BF16)
    return jnp.dot(normed, w_embed, preferred_element_type=F32).astype(BF16)


def place_tiles(embedded, targets, slides):
    one_hot = (targets[:, None] == jnp.arange(slides, dtype=jnp.int32)[None, :]).astype(jnp.int32)
    order_rank = jnp.sum((jnp.cumsum(one_hot, axis=0) - 1) * one_hot, axis=1)
    slot_index = targets * CAP + order_rank
    placing = (jnp.arange(slides * CAP, dtype=jnp.int32)[:, None] == slot_index[None, :]).astype(BF16)
    buffer = jnp.dot(placing, embedded, preferred_element_type=F32).astype(BF16)
    return (buffer, jnp.sum(one_hot, axis=0))


def row_orders():
    feature = np.arange(WIDTH)
    device, inner = feature // 6, feature % 6
    at = {"core": device % 2, "z": device // 2 % 4, "x": device // 8 % 4, "y": device // 32}
    places = [
        at["core"] * 384 + at[a] * 96 + at[b] * 24 + at[c] * 6 + inner for a, b, c in ORDERS
    ]
    return np.broadcast_to(np.stack(places)[:, None, :], (3, 8, WIDTH)).astype(np.int32)


def dot(a, b):
    return jnp.dot(a, b, preferred_element_type=F32)


def layer_kernel(
    x_ref, xd_ref, val_ref, cot_ref, wqkv_ref, wout_ref, place_ref, att_ref, g_ref,
    q_tok, k_tok, v_tok, do_tok, q_t, k_t, v_t, do_t, mg, o_t, dq_t, dq_tok, dkv,
    scores, prob, grad, perm, xp_t, op_t, filler,
):
    mg_val = val_ref[:SLOTS, :].astype(BF16)
    for c in range(6):
        cols = slice(c * 128, c * 128 + 128)
        mg[:, cols] = cot_ref[:, cols] * mg_val
    row = lax.broadcasted_iota(jnp.int32, (64, SLOTS), 0)
    filler[...] = jnp.where(row == 0, 1.0, 0.0).astype(BF16)

    @pl.loop(0, 3)
    def _(c):
        start = pl.multiple_of(c * BLOCK, BLOCK)
        cols = pl.ds(start, BLOCK)
        query = dot(x_ref[...], wqkv_ref[:, cols]).astype(BF16) * BF16(0.125)
        q_tok[:, cols] = query
        q_t[cols, :] = query.T
        for base, tok, turned in ((WIDTH, k_tok, k_t), (2 * WIDTH, v_tok, v_t)):
            w_cols = pl.ds(pl.multiple_of(start + base, BLOCK), BLOCK)
            for first, rows_ref in ((0, x_ref), (SLOTS, xd_ref)):
                part = dot(rows_ref[...], wqkv_ref[:, w_cols]).astype(BF16)
                tok[first : first + SLOTS, cols] = part
                turned[cols, first : first + SLOTS] = part.T
        d_heads = lax.dot_general(mg[...], wout_ref[cols, :], NT, preferred_element_type=F32).astype(BF16)
        do_tok[:, cols] = d_heads
        do_t[cols, :] = d_heads.T

    @pl.loop(0, HEADS // 2)
    def _(pair):
        lanes = pl.ds(pl.multiple_of(pair * 128, 128), 128)
        k2, v2 = k_tok[:, lanes], v_tok[:, lanes]
        bias = jnp.where(val_ref[...] > 0.5, 0.0, MASKED).astype(BF16)
        lane = lax.broadcasted_iota(jnp.int32, (KEYS, 128), 1)
        keys, q_rows, do_rows, zeros = [], [], [], jnp.zeros((64, SLOTS), BF16)
        for a in range(2):
            rows = pl.ds(pl.multiple_of(pair * 128 + a * 64, 64), 64)
            own = lane < 64 if a == 0 else lane >= 64
            keys.append(jnp.where(own, k2, bias))
            q_part, do_part = q_t[rows, :], do_t[rows, :]
            halves = (q_part, filler[...]) if a == 0 else (filler[...], q_part)
            q_rows.append(jnp.concatenate(halves, axis=0))
            halves = (do_part, zeros) if a == 0 else (zeros, do_part)
            do_rows.append(jnp.concatenate(halves, axis=0))

        for step in range(6):
            a, block = step // 3, step % 3
            cols = slice(block * BLOCK, block * BLOCK + BLOCK)
            rows = pl.ds(pl.multiple_of(pair * 128 + a * 64, 64), 64)
            slot = step % 2
            out_cols = slice(a * SLOTS + block * BLOCK, a * SLOTS + block * BLOCK + BLOCK)
            s = dot(keys[a], q_rows[a][:, cols])
            peak = jnp.max(s, axis=0, keepdims=True)
            raw = jnp.exp(s - peak)
            scores[slot] = raw
            inverse = 1.0 / jnp.sum(raw, axis=0, keepdims=True)
            p = (scores[slot] * inverse).astype(BF16)
            prob[:, out_cols] = p
            out = dot(v_t[rows, :], p).astype(BF16)
            o_t[rows, cols] = out
            delta = jnp.sum(do_t[rows, cols].astype(F32) * out.astype(F32), axis=0, keepdims=True)
            grad_p = dot(v2, do_rows[a][:, cols])
            ds = (scores[slot] * inverse * (grad_p - delta)).astype(BF16)
            grad[:, out_cols] = ds
            dq_t[rows, cols] = (dot(k_t[rows, :], ds) * 0.125).astype(BF16)

        lane_q = lax.broadcasted_iota(jnp.int32, (SLOTS, 128), 1)
        q2, do2 = q_tok[:, lanes], do_tok[:, lanes]
        nothing = jnp.zeros((SLOTS, 128), BF16)
        q_cat = jnp.concatenate([jnp.where(lane_q < 64, q2, nothing), jnp.where(lane_q < 64, nothing, q2)], axis=0)
        do_cat = jnp.concatenate([jnp.where(lane_q < 64, do2, nothing), jnp.where(lane_q < 64, nothing, do2)], axis=0)
        dkv[:, lanes] = dot(grad[...], q_cat).astype(BF16)
        dkv[:, pl.ds(pl.multiple_of(pair * 128 + WIDTH, 128), 128)] = dot(prob[...], do_cat).astype(BF16)
        dq_tok[:, lanes] = dq_t[lanes, :].T

    @pl.loop(0, 3)
    def _(c):
        cols = pl.ds(pl.multiple_of(c * BLOCK, BLOCK), BLOCK)
        mixed = x_ref[:, cols].astype(F32) + lax.dot_general(
            o_t[...], wout_ref[:, cols], (((0,), (0,)), ((), ())), preferred_element_type=F32
        )
        att_ref[:, cols] = (mixed * val_ref[:SLOTS, :1]).astype(BF16)

    for t in range(3):
        place = place_ref[t][:1, :]
        perm[...] = (lax.broadcasted_iota(jnp.int32, (WIDTH, WIDTH), 0) == place).astype(BF16)

        @pl.loop(0, 3)
        def _(c):
            start = pl.multiple_of(c * BLOCK, BLOCK)
            rows = pl.ds(start, BLOCK)
            xp_t[:, rows] = lax.dot_general(perm[...], x_ref[rows, :], NT, preferred_element_type=F32).astype(BF16)
            far = pl.ds(pl.multiple_of(start + SLOTS, BLOCK), BLOCK)
            xp_t[:, far] = lax.dot_general(perm[...], xd_ref[rows, :], NT, preferred_element_type=F32).astype(BF16)
            if t == 2:
                op_t[:, rows] = dot(perm[...], o_t[:, rows]).astype(BF16)

        for n in range(4):
            chunk = t * 4 + n
            cols = slice(n * BLOCK, n * BLOCK + BLOCK)
            if chunk < 3:
                part = dot(xp_t[:, :SLOTS], dq_tok[:, chunk * BLOCK : chunk * BLOCK + BLOCK])
            elif chunk < 9:
                part = dot(xp_t[...], dkv[:, chunk * BLOCK - WIDTH : chunk * BLOCK - WIDTH + BLOCK])
            else:
                part = dot(op_t[...], mg[:, chunk * BLOCK - 2304 : chunk * BLOCK - 2304 + BLOCK])
            g_ref[t, :, cols] = part.astype(BF16)


def layer(x, xd, val, cot, w_qkv, w_out):
    tall, wide = (KEYS, WIDTH), (WIDTH, KEYS)
    square = (SLOTS, WIDTH)
    vmem = pl.BlockSpec(memory_space=pltpu.VMEM)
    shapes = [
        square, tall, tall, square, square, wide, wide, square, square, square, square, square, (KEYS, KEYS),
    ]
    scratch = [pltpu.VMEM(s, BF16) for s in shapes]
    scratch += [
        pltpu.VMEM((2, KEYS, BLOCK), F32),
        pltpu.VMEM((KEYS, KEYS), BF16),
        pltpu.VMEM((KEYS, KEYS), BF16),
        pltpu.VMEM(square, BF16),
        pltpu.VMEM(wide, BF16),
        pltpu.VMEM(square, BF16),
        pltpu.VMEM((64, SLOTS), BF16),
    ]
    return pl.pallas_call(
        layer_kernel,
        out_shape=(
            jax.ShapeDtypeStruct((SLOTS, WIDTH), BF16),
            jax.ShapeDtypeStruct((3, WIDTH, THIRD), BF16),
        ),
        in_specs=[vmem] * 7,
        out_specs=(vmem, vmem),
        scratch_shapes=scratch,
        compiler_params=pltpu.CompilerParams(vmem_limit_bytes=62 * 1024 * 1024),
        cost_estimate=pl.CostEstimate(flops=28_000_000_000, bytes_accessed=16_000_000, transcendentals=14_000_000),
        name="layer",
    )(x, xd, val, cot, w_qkv, w_out, jnp.asarray(row_orders()))


def sum_kernel(factor, g_ref, oq_ref, oo_ref, half, pair_sum, from_a, owned, from_b, spread, from_c,
               send0, recv0, send_a, recv_a, send_b, recv_b, send_c, recv_c):
    slide, seq = lax.axis_index("slide"), lax.axis_index("seq")
    at = {"y": slide // SIDE, "x": slide % SIDE, "z": seq // 2}
    core = seq % 2

    def peer(axis, distance):
        moved = dict(at)
        moved[axis] = lax.rem(at[axis] + distance, SIDE)
        return moved[axis], (moved["y"] * SIDE + moved["x"], moved["z"] * 2 + core)

    sibling = (slide, at["z"] * 2 + 1 - core)
    barrier = pltpu.get_barrier_semaphore()
    others = [sibling] + [peer(axis, d)[1] for axis in "xyz" for d in (1, 2, 3)]
    for other in others:
        pl.semaphore_signal(barrier, inc=1, device_id=other, device_id_type=MESH)
    pl.semaphore_wait(barrier, len(others))

    def remote(src, dst, send, recv, device):
        copy = pltpu.make_async_remote_copy(
            src_ref=src, dst_ref=dst, send_sem=send, recv_sem=recv, device_id=device, device_id_type=MESH
        )
        copy.start()
        return copy

    started = []
    own_half = pl.multiple_of(core * 384, 384)
    its_half = pl.multiple_of((1 - core) * 384, 384)
    zero = [
        remote(g_ref.at[t, pl.ds(its_half, 384), :], half.at[t], send0.at[t], recv0.at[t], sibling) for t in range(3)
    ]
    stage_a = []
    for t in range(3):
        zero[t].wait_recv()
        pair_sum[t] = (g_ref[t, pl.ds(own_half, 384), :].astype(F32) + half[t].astype(F32)).astype(BF16)
        row = []
        for d in (2, 1, 3):
            there, device = peer(ORDERS[t][0], d)
            src = pair_sum.at[t, pl.ds(pl.multiple_of(there * 96, 96), 96), :]
            row.append(remote(src, from_a.at[t, d - 1], send_a.at[t, d - 1], recv_a.at[t, d - 1], device))
        stage_a.append(row)
    stage_b = []
    for t in range(3):
        mine = pl.multiple_of(at[ORDERS[t][0]] * 96, 96)
        total = g_ref[t, pl.ds(pl.multiple_of(own_half + mine, 96), 96), :].astype(F32)
        total = total + half[t, pl.ds(mine, 96), :].astype(F32)
        for copy in stage_a[t]:
            copy.wait_recv()
        for d in range(3):
            total = total + from_a[t, d].astype(F32)
        owned[t] = total
        row = []
        for d in (2, 1, 3):
            there, device = peer(ORDERS[t][1], d)
            src = owned.at[t, pl.ds(pl.multiple_of(there * 24, 24), 24), :]
            row.append(remote(src, from_b.at[t, d - 1], send_b.at[t, d - 1], recv_b.at[t, d - 1], device))
        stage_b.append(row)
    stage_c = []
    for t in range(3):
        mine = pl.multiple_of(at[ORDERS[t][1]] * 24, 24)
        total = owned[t, pl.ds(mine, 24), :]
        for copy in stage_b[t]:
            copy.wait_recv()
        for d in range(3):
            total = total + from_b[t, d]
        for c in range(SIDE):
            spread[t, c, :6, :] = total[c * 6 : c * 6 + 6]
            spread[t, c, 6:, :] = jnp.zeros((2, THIRD), F32)
        row = []
        for d in (2, 1, 3):
            there, device = peer(ORDERS[t][2], d)
            row.append(remote(spread.at[t, there], from_c.at[t, d - 1], send_c.at[t, d - 1], recv_c.at[t, d - 1], device))
        stage_c.append(row)
    for t in range(3):
        total = spread[t, at[ORDERS[t][2]]]
        for copy in stage_c[t]:
            copy.wait_recv()
        for d in range(3):
            total = total + from_c[t, d]
        total = total[:6] * factor
        if t < 2:
            oq_ref[:, t * THIRD : t * THIRD + THIRD] = total
        else:
            oq_ref[:, 2 * THIRD :] = total[:, :BLOCK]
            oo_ref[...] = total[:, BLOCK:]
    for copy in zero:
        copy.wait_send()
    for stage in (stage_a, stage_b, stage_c):
        for row in stage:
            for copy in row:
                copy.wait_send()


def sum_gradients(g, factor):
    vmem = pl.BlockSpec(memory_space=pltpu.VMEM)
    return pl.pallas_call(
        functools.partial(sum_kernel, factor),
        out_shape=(jax.ShapeDtypeStruct((6, 3 * WIDTH), F32), jax.ShapeDtypeStruct((6, WIDTH), F32)),
        in_specs=[vmem],
        out_specs=(vmem, vmem),
        scratch_shapes=[
            pltpu.VMEM((3, 384, THIRD), BF16),
            pltpu.VMEM((3, 384, THIRD), BF16),
            pltpu.VMEM((3, 3, 96, THIRD), BF16),
            pltpu.VMEM((3, 96, THIRD), F32),
            pltpu.VMEM((3, 3, 24, THIRD), F32),
            pltpu.VMEM((3, SIDE, 8, THIRD), F32),
            pltpu.VMEM((3, 3, 8, THIRD), F32),
            pltpu.SemaphoreType.DMA((3,)),
            pltpu.SemaphoreType.DMA((3,)),
        ] + [pltpu.SemaphoreType.DMA((3, 3))] * 6,
        compiler_params=pltpu.CompilerParams(
            collective_id=1, has_side_effects=True, vmem_limit_bytes=48 * 1024 * 1024
        ),
        cost_estimate=pl.CostEstimate(flops=10_000_000, bytes_accessed=5_000_000, transcendentals=0),
        name="sum_gradients",
    )(g)


def shards(tile_feats, norm_gain, w_embed, slide_of_tile, w_qkv, w_out, cotangent):
    width = w_out.shape[0]
    slides = lax.axis_size("slide")
    blocks = lax.axis_size("seq")
    embedded = embed_tiles(tile_feats, norm_gain, w_embed)
    buffer, counts = place_tiles(embedded, slide_of_tile[:, 0], slides)
    received, arrived = (
        lax.all_to_all(
            buffer.reshape(slides, CAP, width), "slide", split_axis=0, concat_axis=0, tiled=True
        ),
        lax.all_to_all(counts.reshape(slides, 1), "slide", split_axis=0, concat_axis=0, tiled=True),
    )
    rows_in = received.reshape(slides * CAP, width)
    valid = (jnp.arange(CAP, dtype=jnp.int32)[None, :] < arrived).astype(F32).reshape(slides * CAP)
    rows_far, valid_far = (
        lax.all_gather(rows_in[::RATE], "seq", axis=0, tiled=True),
        lax.all_gather(valid[::RATE].astype(BF16), "seq", axis=0, tiled=True),
    )
    val = jnp.broadcast_to(jnp.concatenate([valid, valid_far.astype(F32)])[:, None], (KEYS, 128))
    output, partial = layer(rows_in, rows_far, val, cotangent[0], w_qkv, w_out)
    factor = (slides * blocks * rows_in.shape[0]) ** (-0.5)
    grad_qkv, grad_out = sum_gradients(partial, factor)
    return (output[None], grad_qkv, grad_out)


def solution(mesh):
    return jax.shard_map(
        shards,
        mesh=mesh,
        in_specs=(
            P(("slide", "seq"), None),
            P(),
            P(),
            P(("slide", "seq"), None),
            P(),
            P(),
            P("slide", "seq", None),
        ),
        out_specs=(P("slide", "seq", None), P(("slide", "seq"), None), P(("slide", "seq"), None)),
        check_vma=False,
    )
```

```python
import functools

import jax
import jax.numpy as jnp
import numpy as np
from jax import lax
from jax.experimental import pallas as pl
from jax.experimental.pallas import tpu as pltpu
from jax.sharding import PartitionSpec as P

HEADS = 12
CAP = 48
RATE = 8
WIDTH = 768
WIDE = 1536
TILES = 384
SLOTS = 768
KEYS = 1536
BLOCK = 256
PART = 512
SIDE = 4
THIRD = 1024
MASKED = -1e30
BF16 = jnp.bfloat16
F32 = jnp.float32
MESH = pl.DeviceIdType.MESH
ORDERS = (("x", "y", "z"), ("y", "z", "x"), ("z", "x", "y"))
NT = (((1,), (1,)), ((), ()))


def front_kernel(
    feats_ref, gain_ref, we_ref, target_ref, x_ref, xd_ref, near_ref, far_ref,
    normed, embedded, placed, tally, near_all, own_far, mine16,
    send_x, recv_x, send_n, recv_n, send_f, recv_f, send_z, recv_z, send_s, recv_s, local,
):
    slide, seq = lax.axis_index("slide"), lax.axis_index("seq")
    z, core = seq // 2, seq % 2
    slides = [(lax.rem(slide + k, 16), seq) for k in range(1, 16)]
    blocks = [(slide, lax.rem(seq + k, 8)) for k in range(1, 8)]
    barrier = pltpu.get_barrier_semaphore()
    for device in slides + blocks:
        pl.semaphore_signal(barrier, inc=1, device_id=device, device_id_type=MESH)

    def remote(src, dst, send, recv, device):
        copy = pltpu.make_async_remote_copy(
            src_ref=src, dst_ref=dst, send_sem=send, recv_sem=recv, device_id=device, device_id_type=MESH
        )
        copy.start()
        return copy

    target = target_ref[...]
    named = lax.broadcasted_iota(jnp.int32, (16, TILES), 0) == target
    one_hot = jnp.where(named, 1.0, 0.0)
    earlier = (
        lax.broadcasted_iota(jnp.int32, (TILES, TILES), 0) < lax.broadcasted_iota(jnp.int32, (TILES, TILES), 1)
    ).astype(BF16)
    before = dot(one_hot.astype(BF16), earlier)
    rank = jnp.sum(one_hot * before, axis=0, keepdims=True)
    slot = target * CAP + rank.astype(jnp.int32)
    placing = (lax.broadcasted_iota(jnp.int32, (SLOTS, TILES), 0) == slot).astype(BF16)
    total = jnp.sum(one_hot, axis=1, keepdims=True)
    for d in range(16):
        tally[d] = jnp.broadcast_to(total[d : d + 1], (8, 128))

    @pl.loop(0, 4)
    def _(c):
        rows = pl.ds(pl.multiple_of(c * 96, 96), 96)
        values = feats_ref[rows, :].astype(F32)
        center = jnp.mean(values, axis=-1, keepdims=True)
        moved = values - center
        spread = jnp.mean(moved * moved, axis=-1, keepdims=True)
        normed[rows, :] = (moved * lax.rsqrt(spread + 1e-06) * gain_ref[...]).astype(BF16)

    pl.semaphore_wait(barrier, 22)
    near_copies = [
        remote(tally.at[dev[0]], near_all.at[slide], send_n.at[k], recv_n.at[k], dev) for k, dev in enumerate(slides)
    ]
    near_all[slide] = tally[slide]
    x_copies = []
    for half in range(2):
        cols = slice(half * 384, half * 384 + 384)
        embedded[...] = dot(normed[...], we_ref[:, cols]).astype(BF16)
        placed[:, cols] = dot(placing, embedded[...]).astype(BF16)
        for k in (7, 8, 6, 9, 5, 10, 4, 11, 3, 12, 2, 13, 1, 14, 0):
            dev = slides[k]
            src = placed.at[pl.ds(pl.multiple_of(dev[0] * CAP, CAP), CAP), cols]
            dst = x_ref.at[pl.ds(pl.multiple_of(slide * CAP, CAP), CAP), cols]
            x_copies.append(remote(src, dst, send_x.at[half, k], recv_x.at[half, k], dev))
    own = pl.ds(pl.multiple_of(slide * CAP, CAP), CAP)
    x_ref[own, :] = placed[own, :]

    for copy in near_copies:
        copy.wait_recv()
    for i in range(16):
        mine16[i : i + 1, :] = near_all[i][:1]
    near_ref[...] = mine16[...]
    far_copies = [remote(mine16, far_ref.at[seq], send_f.at[k], recv_f.at[k], dev) for k, dev in enumerate(blocks)]
    far_ref[seq] = mine16[...]

    row = lax.broadcasted_iota(jnp.int32, (96, SLOTS), 0)
    pick = lax.broadcasted_iota(jnp.int32, (96, SLOTS), 1) == (row % 16) * CAP + (row // 16) * RATE
    pick = pick.astype(BF16)
    for copy in x_copies:
        copy.wait_recv()
    rows = dot(pick, x_ref[...]).astype(BF16)
    for m in range(6):
        own_far[m] = rows[m * 16 : m * 16 + 16]

    sibling = (slide, z * 2 + 1 - core)
    up = (slide, lax.rem(z + 1, SIDE) * 2 + core)
    down = (slide, lax.rem(z + 3, SIDE) * 2 + core)
    to_up = remote(own_far, xd_ref.at[:, seq], send_z.at[0], recv_z.at[0], up)
    to_down = remote(own_far, xd_ref.at[:, seq], send_z.at[1], recv_z.at[1], down)
    to_side = [remote(own_far, xd_ref.at[:, seq], send_s.at[0], recv_s.at[0], sibling)]
    keep = pltpu.make_async_copy(own_far, xd_ref.at[:, seq], local)
    keep.start()
    to_up.wait_recv()
    relay_up = remote(xd_ref.at[pl.ds(0, 3), down[1]], xd_ref.at[pl.ds(0, 3), down[1]], send_z.at[2], recv_z.at[2], up)
    to_side.append(remote(xd_ref.at[:, down[1]], xd_ref.at[:, down[1]], send_s.at[1], recv_s.at[1], sibling))
    to_down.wait_recv()
    relay_down = remote(xd_ref.at[pl.ds(3, 3), up[1]], xd_ref.at[pl.ds(3, 3), up[1]], send_z.at[3], recv_z.at[3], down)
    to_side.append(remote(xd_ref.at[:, up[1]], xd_ref.at[:, up[1]], send_s.at[2], recv_s.at[2], sibling))
    relay_up.wait_recv()
    relay_down.wait_recv()
    across = lax.rem(z + 2, SIDE) * 2 + core
    to_side.append(remote(xd_ref.at[:, across], xd_ref.at[:, across], send_s.at[3], recv_s.at[3], sibling))
    for copy in to_side + far_copies:
        copy.wait_recv()
    keep.wait()
    for copy in to_side + far_copies + near_copies + x_copies + [to_up, to_down, relay_up, relay_down]:
        copy.wait_send()


def front(feats, gain, w_embed, target):
    vmem = pl.BlockSpec(memory_space=pltpu.VMEM)
    dma = pltpu.SemaphoreType.DMA
    return pl.pallas_call(
        front_kernel,
        out_shape=(
            jax.ShapeDtypeStruct((SLOTS, WIDTH), BF16),
            jax.ShapeDtypeStruct((6, 8, 16, WIDTH), BF16),
            jax.ShapeDtypeStruct((16, 128), F32),
            jax.ShapeDtypeStruct((8, 16, 128), F32),
        ),
        in_specs=[vmem] * 4,
        out_specs=(vmem,) * 4,
        scratch_shapes=[
            pltpu.VMEM((TILES, WIDE), BF16),
            pltpu.VMEM((TILES, WIDTH // 2), BF16),
            pltpu.VMEM((SLOTS, WIDTH), BF16),
            pltpu.VMEM((16, 8, 128), F32),
            pltpu.VMEM((16, 8, 128), F32),
            pltpu.VMEM((6, 16, WIDTH), BF16),
            pltpu.VMEM((16, 128), F32),
            dma((2, 15)), dma((2, 15)), dma((15,)), dma((15,)), dma((7,)), dma((7,)),
            dma((4,)), dma((4,)), dma((4,)), dma((4,)), dma,
        ],
        compiler_params=pltpu.CompilerParams(
            collective_id=2, has_side_effects=True, vmem_limit_bytes=40 * 1024 * 1024
        ),
        cost_estimate=pl.CostEstimate(flops=2_000_000_000, bytes_accessed=8_000_000, transcendentals=0),
        name="front",
    )(feats, gain, w_embed, target)


def row_orders():
    feature = np.arange(WIDTH)
    device, inner = feature // 6, feature % 6
    at = {"core": device % 2, "z": device // 2 % 4, "x": device // 8 % 4, "y": device // 32}
    places = [
        at["core"] * 384 + at[a] * 96 + at[b] * 24 + at[c] * 6 + inner for a, b, c in ORDERS
    ]
    return np.broadcast_to(np.stack(places)[:, None, :], (3, 8, WIDTH)).astype(np.int32)


def dot(a, b):
    return jnp.dot(a, b, preferred_element_type=F32)


def layer_kernel(
    x_ref, xd_ref, near_ref, far_ref, cot_ref, wqkv_ref, wout_ref, place_ref, att_ref, g_ref,
    val, bias, q_tok, k_tok, v_tok, do_tok, q_t, k_t, v_t, do_t, x_t, mg, o_t, dq_t, dq_tok, dkv,
    score_0, score_1, grad_p, prob_0, prob_1, grad_0, grad_1, key_0, key_1, q_0, q_1, do_0, do_1,
    qc_0, qc_1, dc_0, dc_1,
):
    scores, prob, grad = (score_0, score_1), (prob_0, prob_1), (grad_0, grad_1)
    keys, q_rows, do_rows = (key_0, key_1), (q_0, q_1), (do_0, do_1)
    q_cat, do_cat = (qc_0, qc_1), (dc_0, dc_1)

    place_in = lax.broadcasted_iota(jnp.int32, (CAP, 128), 0).astype(F32)
    for i in range(16):
        val[i * CAP : i * CAP + CAP, :] = jnp.where(place_in < near_ref[i : i + 1, :], 1.0, 0.0)
    for m in range(6):
        for j in range(8):
            first = SLOTS + m * 128 + j * 16
            val[first : first + 16, :] = jnp.where(far_ref[j] > m * RATE, 1.0, 0.0)
    bias[...] = jnp.where(val[...] > 0.5, 0.0, MASKED).astype(BF16)
    mg_val = val[:SLOTS, :].astype(BF16)
    for c in range(6):
        cols = slice(c * 128, c * 128 + 128)
        mg[:, cols] = cot_ref[:, cols] * mg_val
    row = lax.broadcasted_iota(jnp.int32, (64, SLOTS), 0)
    filler = jnp.where(row == 0, 1.0, 0.0).astype(BF16)
    zeros = jnp.zeros((64, SLOTS), BF16)
    q_0[64:, :], q_1[:64, :] = filler, filler
    do_0[64:, :], do_1[:64, :] = zeros, zeros

    @pl.loop(0, 3)
    def _(c):
        start = pl.multiple_of(c * BLOCK, BLOCK)
        cols = pl.ds(start, BLOCK)
        query = dot(x_ref[...], wqkv_ref[:, cols]).astype(BF16) * BF16(0.125)
        q_tok[:, cols] = query
        q_t[cols, :] = query.T
        for first, rows_ref in ((0, x_ref), (SLOTS, xd_ref)):
            x_t[cols, first : first + SLOTS] = rows_ref[:, cols].T
        for base, tok, turned in ((WIDTH, k_tok, k_t), (2 * WIDTH, v_tok, v_t)):
            w_cols = pl.ds(pl.multiple_of(start + base, BLOCK), BLOCK)
            for first, rows_ref in ((0, x_ref), (SLOTS, xd_ref)):
                part = dot(rows_ref[...], wqkv_ref[:, w_cols]).astype(BF16)
                tok[first : first + SLOTS, cols] = part
                turned[cols, first : first + SLOTS] = part.T
        d_heads = lax.dot_general(mg[...], wout_ref[cols, :], NT, preferred_element_type=F32).astype(BF16)
        do_tok[:, cols] = d_heads
        do_t[cols, :] = d_heads.T

    def lanes_of(pair):
        return pl.ds(pl.multiple_of(pair * 128, 128), 128)

    def close_keys(pair, a, third):
        rows = slice(third * PART, third * PART + PART)
        mine = lax.broadcasted_iota(jnp.int32, (PART, 128), 1) // 64 == a
        for offset, left, right in ((0, grad[a], q_cat[a]), (WIDTH, prob[a], do_cat[a])):
            lanes = pl.ds(pl.multiple_of(pair * 128 + offset, 128), 128)
            part = dot(left[rows, :], right[...]).astype(BF16)
            dkv[rows, lanes] = jnp.where(mine, part, dkv[rows, lanes])

    @pl.loop(0, HEADS // 2)
    def _(pair):
        lanes = lanes_of(pair)
        before = lax.max(pair - 1, 0)
        lane = lax.broadcasted_iota(jnp.int32, (KEYS, 128), 1)
        lane_q = lax.broadcasted_iota(jnp.int32, (SLOTS, 128), 1)
        nothing = jnp.zeros((SLOTS, 128), BF16)

        def head_rows(a):
            return pl.ds(pl.multiple_of(pair * 128 + a * 64, 64), 64)

        def open_head(a):
            own = slice(a * 64, a * 64 + 64)
            keys[a][...] = jnp.where(lane // 64 == a, k_tok[:, lanes], bias[...])
            q_rows[a][own, :] = q_t[head_rows(a), :]
            do_rows[a][own, :] = do_t[head_rows(a), :]

        def score_part(step, part):
            a, block = step // 3, step % 3
            rows = slice(part * PART, part * PART + PART)
            cols = slice(block * BLOCK, block * BLOCK + BLOCK)
            s = dot(keys[a][rows, :], q_rows[a][:, cols])
            scores[step % 2][rows, :] = s
            return jnp.max(s, axis=0, keepdims=True)

        def top(parts):
            return jnp.maximum(jnp.maximum(parts[0], parts[1]), parts[2])

        open_head(0)
        peak = top([score_part(0, part) for part in range(3)])
        open_head(1)
        for step in range(6):
            a, block = step // 3, step % 3
            cols = slice(block * BLOCK, block * BLOCK + BLOCK)
            score = scores[step % 2]
            peaks, sums = [], []
            for part in range(3):
                rows = slice(part * PART, part * PART + PART)
                if step < 5:
                    peaks.append(score_part(step + 1, part))
                raw = jnp.exp(score[rows, :] - peak)
                score[rows, :] = raw
                sums.append(jnp.sum(raw, axis=0, keepdims=True))
            inverse = 1.0 / (sums[0] + sums[1] + sums[2])
            for part in range(3):
                rows = slice(part * PART, part * PART + PART)
                grad_p[rows, :] = dot(v_tok[rows, lanes], do_rows[a][:, cols])
                p = score[rows, :] * inverse
                score[rows, :] = p
                prob[a][rows, cols] = p.astype(BF16)
            out = dot(v_t[head_rows(a), :], prob[a][:, cols]).astype(BF16)
            o_t[head_rows(a), cols] = out
            if a == 0:
                close_keys(before, 1, block)
            else:
                close_keys(pair, 0, block)
            delta = jnp.sum(do_t[head_rows(a), cols].astype(F32) * out.astype(F32), axis=0, keepdims=True)
            for part in range(3):
                rows = slice(part * PART, part * PART + PART)
                grad[a][rows, cols] = (score[rows, :] * (grad_p[rows, :] - delta)).astype(BF16)
            dq_t[head_rows(a), cols] = (dot(k_t[head_rows(a), :], grad[a][:, cols]) * 0.125).astype(BF16)
            if step < 5:
                peak = top(peaks)
            if block == 2:
                half = lane_q // 64 == a
                q_cat[a][...] = jnp.where(half, q_tok[:, lanes], nothing)
                do_cat[a][...] = jnp.where(half, do_tok[:, lanes], nothing)
        dq_tok[:, lanes] = dq_t[lanes, :].T

    for third in range(3):
        close_keys(HEADS // 2 - 1, 1, third)

    @pl.loop(0, 3)
    def _(c):
        cols = pl.ds(pl.multiple_of(c * BLOCK, BLOCK), BLOCK)
        mixed = x_ref[:, cols].astype(F32) + lax.dot_general(
            o_t[...], wout_ref[:, cols], (((0,), (0,)), ((), ())), preferred_element_type=F32
        )
        att_ref[:, cols] = (mixed * val[:SLOTS, :1]).astype(BF16)

    perm = prob_0
    for t in range(3):
        place = place_ref[t][:1, :]
        perm[:WIDTH, :] = (lax.broadcasted_iota(jnp.int32, (WIDTH, WIDTH), 0) == place).astype(BF16)
        for n in range(4):
            chunk = t * 4 + n
            cols = slice(n * BLOCK, n * BLOCK + BLOCK)
            if chunk < 3:
                part = dot(x_t[:, :SLOTS], dq_tok[:, chunk * BLOCK : chunk * BLOCK + BLOCK])
            elif chunk < 9:
                part = dot(x_t[...], dkv[:, chunk * BLOCK - WIDTH : chunk * BLOCK - WIDTH + BLOCK])
            else:
                part = dot(o_t[...], mg[:, chunk * BLOCK - 2304 : chunk * BLOCK - 2304 + BLOCK])
            g_ref[t, :, cols] = dot(perm[:WIDTH, :], part.astype(BF16)).astype(BF16)


def layer(x, xd, near, far, cot, w_qkv, w_out):
    tall, wide = (KEYS, WIDTH), (WIDTH, KEYS)
    square = (SLOTS, WIDTH)
    vmem = pl.BlockSpec(memory_space=pltpu.VMEM)
    scratch = [pltpu.VMEM((KEYS, 128), F32), pltpu.VMEM((KEYS, 128), BF16)]
    shapes = [
        square, tall, tall, square, square, wide, wide, square, wide, square, square, square, square, (KEYS, KEYS),
    ]
    scratch += [pltpu.VMEM(s, BF16) for s in shapes]
    scratch += [pltpu.VMEM((KEYS, BLOCK), F32)] * 3
    scratch += [pltpu.VMEM(tall, BF16)] * 4
    scratch += [pltpu.VMEM((KEYS, 128), BF16)] * 2
    scratch += [pltpu.VMEM((128, SLOTS), BF16)] * 4
    scratch += [pltpu.VMEM((SLOTS, 128), BF16)] * 4
    return pl.pallas_call(
        layer_kernel,
        out_shape=(
            jax.ShapeDtypeStruct((SLOTS, WIDTH), BF16),
            jax.ShapeDtypeStruct((3, WIDTH, THIRD), BF16),
        ),
        in_specs=[vmem] * 8,
        out_specs=(vmem, vmem),
        scratch_shapes=scratch,
        compiler_params=pltpu.CompilerParams(vmem_limit_bytes=62 * 1024 * 1024),
        cost_estimate=pl.CostEstimate(flops=28_000_000_000, bytes_accessed=16_000_000, transcendentals=14_000_000),
        name="layer",
    )(x, xd, near, far, cot, w_qkv, w_out, jnp.asarray(row_orders()))


def sum_kernel(factor, g_ref, oq_ref, oo_ref, half, pair_sum, from_a, owned, from_b, spread, from_c,
               send0, recv0, send_a, recv_a, send_b, recv_b, send_c, recv_c):
    slide, seq = lax.axis_index("slide"), lax.axis_index("seq")
    at = {"y": slide // SIDE, "x": slide % SIDE, "z": seq // 2}
    core = seq % 2

    def peer(axis, distance):
        moved = dict(at)
        moved[axis] = lax.rem(at[axis] + distance, SIDE)
        return moved[axis], (moved["y"] * SIDE + moved["x"], moved["z"] * 2 + core)

    sibling = (slide, at["z"] * 2 + 1 - core)
    barrier = pltpu.get_barrier_semaphore()
    others = [sibling] + [peer(axis, d)[1] for axis in "xyz" for d in (1, 2, 3)]
    for other in others:
        pl.semaphore_signal(barrier, inc=1, device_id=other, device_id_type=MESH)
    pl.semaphore_wait(barrier, len(others))

    def remote(src, dst, send, recv, device):
        copy = pltpu.make_async_remote_copy(
            src_ref=src, dst_ref=dst, send_sem=send, recv_sem=recv, device_id=device, device_id_type=MESH
        )
        copy.start()
        return copy

    started = []
    own_half = pl.multiple_of(core * 384, 384)
    its_half = pl.multiple_of((1 - core) * 384, 384)
    zero = [
        remote(g_ref.at[t, pl.ds(its_half, 384), :], half.at[t], send0.at[t], recv0.at[t], sibling) for t in range(3)
    ]
    stage_a = []
    for t in range(3):
        zero[t].wait_recv()
        pair_sum[t] = (g_ref[t, pl.ds(own_half, 384), :].astype(F32) + half[t].astype(F32)).astype(BF16)
        row = []
        for d in (2, 1, 3):
            there, device = peer(ORDERS[t][0], d)
            src = pair_sum.at[t, pl.ds(pl.multiple_of(there * 96, 96), 96), :]
            row.append(remote(src, from_a.at[t, d - 1], send_a.at[t, d - 1], recv_a.at[t, d - 1], device))
        stage_a.append(row)
    stage_b = []
    for t in range(3):
        mine = pl.multiple_of(at[ORDERS[t][0]] * 96, 96)
        total = g_ref[t, pl.ds(pl.multiple_of(own_half + mine, 96), 96), :].astype(F32)
        total = total + half[t, pl.ds(mine, 96), :].astype(F32)
        for copy in stage_a[t]:
            copy.wait_recv()
        for d in range(3):
            total = total + from_a[t, d].astype(F32)
        owned[t] = total
        row = []
        for d in (2, 1, 3):
            there, device = peer(ORDERS[t][1], d)
            src = owned.at[t, pl.ds(pl.multiple_of(there * 24, 24), 24), :]
            row.append(remote(src, from_b.at[t, d - 1], send_b.at[t, d - 1], recv_b.at[t, d - 1], device))
        stage_b.append(row)
    stage_c = []
    for t in range(3):
        mine = pl.multiple_of(at[ORDERS[t][1]] * 24, 24)
        total = owned[t, pl.ds(mine, 24), :]
        for copy in stage_b[t]:
            copy.wait_recv()
        for d in range(3):
            total = total + from_b[t, d]
        for c in range(SIDE):
            spread[t, c, :6, :] = total[c * 6 : c * 6 + 6]
            spread[t, c, 6:, :] = jnp.zeros((2, THIRD), F32)
        row = []
        for d in (2, 1, 3):
            there, device = peer(ORDERS[t][2], d)
            row.append(remote(spread.at[t, there], from_c.at[t, d - 1], send_c.at[t, d - 1], recv_c.at[t, d - 1], device))
        stage_c.append(row)
    for t in range(3):
        total = spread[t, at[ORDERS[t][2]]]
        for copy in stage_c[t]:
            copy.wait_recv()
        for d in range(3):
            total = total + from_c[t, d]
        total = total[:6] * factor
        if t < 2:
            oq_ref[:, t * THIRD : t * THIRD + THIRD] = total
        else:
            oq_ref[:, 2 * THIRD :] = total[:, :BLOCK]
            oo_ref[...] = total[:, BLOCK:]
    for copy in zero:
        copy.wait_send()
    for stage in (stage_a, stage_b, stage_c):
        for row in stage:
            for copy in row:
                copy.wait_send()


def sum_gradients(g, factor):
    vmem = pl.BlockSpec(memory_space=pltpu.VMEM)
    return pl.pallas_call(
        functools.partial(sum_kernel, factor),
        out_shape=(jax.ShapeDtypeStruct((6, 3 * WIDTH), F32), jax.ShapeDtypeStruct((6, WIDTH), F32)),
        in_specs=[vmem],
        out_specs=(vmem, vmem),
        scratch_shapes=[
            pltpu.VMEM((3, 384, THIRD), BF16),
            pltpu.VMEM((3, 384, THIRD), BF16),
            pltpu.VMEM((3, 3, 96, THIRD), BF16),
            pltpu.VMEM((3, 96, THIRD), F32),
            pltpu.VMEM((3, 3, 24, THIRD), F32),
            pltpu.VMEM((3, SIDE, 8, THIRD), F32),
            pltpu.VMEM((3, 3, 8, THIRD), F32),
            pltpu.SemaphoreType.DMA((3,)),
            pltpu.SemaphoreType.DMA((3,)),
        ] + [pltpu.SemaphoreType.DMA((3, 3))] * 6,
        compiler_params=pltpu.CompilerParams(
            collective_id=1, has_side_effects=True, vmem_limit_bytes=48 * 1024 * 1024
        ),
        cost_estimate=pl.CostEstimate(flops=10_000_000, bytes_accessed=5_000_000, transcendentals=0),
        name="sum_gradients",
    )(g)


def shards(tile_feats, norm_gain, w_embed, slide_of_tile, w_qkv, w_out, cotangent):
    x, xd, near, far = front(tile_feats, norm_gain.reshape(1, WIDE), w_embed, slide_of_tile.reshape(1, TILES))
    output, partial = layer(x, xd.reshape(SLOTS, WIDTH), near, far, cotangent[0], w_qkv, w_out)
    factor = (lax.axis_size("slide") * lax.axis_size("seq") * SLOTS) ** (-0.5)
    grad_qkv, grad_out = sum_gradients(partial, factor)
    return (output[None], grad_qkv, grad_out)


def solution(mesh):
    return jax.shard_map(
        shards,
        mesh=mesh,
        in_specs=(
            P(("slide", "seq"), None),
            P(),
            P(),
            P(("slide", "seq"), None),
            P(),
            P(),
            P("slide", "seq", None),
        ),
        out_specs=(P("slide", "seq", None), P(("slide", "seq"), None), P(("slide", "seq"), None)),
        check_vma=False,
    )
```

```python
import functools

import jax
import jax.numpy as jnp
import numpy as np
from jax import lax
from jax.experimental import pallas as pl
from jax.experimental.pallas import tpu as pltpu
from jax.sharding import PartitionSpec as P

HEADS = 12
CAP = 48
RATE = 8
WIDTH = 768
WIDE = 1536
TILES = 384
SLOTS = 768
KEYS = 1536
BLOCK = 256
PART = 512
SIDE = 4
MASKED = -1e30
BF16 = jnp.bfloat16
F32 = jnp.float32
MESH = pl.DeviceIdType.MESH
ORDERS = (("x", "y", "z"), ("y", "z", "x"), ("z", "x", "y"))
NT = (((1,), (1,)), ((), ()))


def row_orders():
    feature = np.arange(WIDTH)
    device, inner = feature // 6, feature % 6
    at = {"core": device % 2, "z": device // 2 % 4, "x": device // 8 % 4, "y": device // 32}
    places = [
        at["core"] * 384 + at[a] * 96 + at[b] * 24 + at[c] * 6 + inner for a, b, c in ORDERS
    ]
    return np.broadcast_to(np.stack(places)[:, None, :], (3, 8, WIDTH)).astype(np.int32)


def dot(a, b):
    return jnp.dot(a, b, preferred_element_type=F32)


def whole_kernel(
    factor,
    feats_ref, gain_ref, we_ref, target_ref, cot_ref, wqkv_ref, wout_ref, place_ref,
    att_ref, oq_ref, oo_ref,
    x, xd, val, bias, q_tok, k_tok, v_tok, do_tok, q_t, k_t, v_t, do_t, x_t, mg, o_t, wout,
    dq_t, dq_round, dkv, score_0, score_1, grad_p, prob_0, prob_1, grad_0, grad_1,
    key_0, key_1, q_0, q_1, do_0, do_1, qc_0, qc_1, dc_0, dc_1, perm,
    tally, near_all, near, far, own_far,
    g, half, pair_sum, from_a, owned, from_b, spread, from_c,
    load, send_x, recv_x, send_n, recv_n, send_f, recv_f, send_z, recv_z, send_s, recv_s,
    send0, recv0, send_a, recv_a, send_b, recv_b, send_c, recv_c,
):
    scores, prob, grad = (score_0, score_1), (prob_0, prob_1), (grad_0, grad_1)
    keys, q_rows, do_rows = (key_0, key_1), (q_0, q_1), (do_0, do_1)
    q_cat, do_cat = (qc_0, qc_1), (dc_0, dc_1)
    slide, seq = lax.axis_index("slide"), lax.axis_index("seq")
    at = {"y": slide // SIDE, "x": slide % SIDE, "z": seq // 2}
    z, core = at["z"], seq % 2
    sibling = (slide, z * 2 + 1 - core)
    slides = [(lax.rem(slide + k, 16), seq) for k in range(1, 16)]
    blocks = [(slide, lax.rem(seq + k, 8)) for k in range(1, 8)]

    barrier = pltpu.get_barrier_semaphore()
    for device in slides + blocks:
        pl.semaphore_signal(barrier, inc=1, device_id=device, device_id_type=MESH)

    def remote(src, dst, send, recv, device):
        return pltpu.make_async_remote_copy(
            src_ref=src, dst_ref=dst, send_sem=send, recv_sem=recv, device_id=device, device_id_type=MESH
        )

    def begin(*args):
        copy = remote(*args)
        copy.start()
        return copy

    feats, normed, placed, w_e, w_q, w_k, w_v = (
        grad_0.at[:SLOTS], grad_1.at[:SLOTS], grad_1.at[SLOTS:], prob_1,
        prob_0.at[:SLOTS], prob_0.at[SLOTS:], grad_0.at[SLOTS:],
    )
    sources = [
        (feats_ref.at[:, :WIDTH], feats.at[:TILES]), (feats_ref.at[:, WIDTH:], feats.at[TILES:]),
        (we_ref, w_e), (cot_ref, mg), (wout_ref, wout),
        (wqkv_ref.at[:, :WIDTH], w_q), (wqkv_ref.at[:, WIDTH : 2 * WIDTH], w_k), (wqkv_ref.at[:, 2 * WIDTH :], w_v),
    ]
    loads = [pltpu.make_async_copy(src, dst, load.at[n]) for n, (src, dst) in enumerate(sources)]
    for copy in loads:
        copy.start()

    target = target_ref[...]
    named = lax.broadcasted_iota(jnp.int32, (16, TILES), 0) == target
    one_hot = jnp.where(named, 1.0, 0.0)
    earlier = (
        lax.broadcasted_iota(jnp.int32, (TILES, TILES), 0) < lax.broadcasted_iota(jnp.int32, (TILES, TILES), 1)
    ).astype(BF16)
    before_it = dot(one_hot.astype(BF16), earlier)
    rank = jnp.sum(one_hot * before_it, axis=0, keepdims=True)
    slot = target * CAP + rank.astype(jnp.int32)
    placing = x_t.at[:, :TILES]
    placing[...] = (lax.broadcasted_iota(jnp.int32, (SLOTS, TILES), 0) == slot).astype(BF16)
    total = jnp.sum(one_hot, axis=1, keepdims=True)
    for d in range(16):
        tally[d] = jnp.broadcast_to(total[d : d + 1], (8, 128))
    loads[0].wait()
    loads[1].wait()

    @pl.loop(0, 4)
    def _(c):
        low = pl.ds(pl.multiple_of(c * 96, 96), 96)
        high = pl.ds(pl.multiple_of(c * 96 + TILES, 96), 96)
        values = [feats[low, :].astype(F32), feats[high, :].astype(F32)]
        center = sum(jnp.sum(v, axis=-1, keepdims=True) for v in values) * (1.0 / WIDE)
        moved = [v - center for v in values]
        spread_sq = sum(jnp.sum(v * v, axis=-1, keepdims=True) for v in moved) * (1.0 / WIDE)
        scale = lax.rsqrt(spread_sq + 1e-06)
        normed[low, :] = (moved[0] * scale * gain_ref[:, :WIDTH]).astype(BF16)
        normed[high, :] = (moved[1] * scale * gain_ref[:, WIDTH:]).astype(BF16)

    pl.semaphore_wait(barrier, 22)
    near_copies = [
        begin(tally.at[dev[0]], near_all.at[slide], send_n.at[k], recv_n.at[k], dev) for k, dev in enumerate(slides)
    ]
    near_all[slide] = tally[slide]
    loads[2].wait()
    x_copies = []
    for part in range(2):
        cols = slice(part * 384, part * 384 + 384)
        embedded = dot(normed[:TILES, :], w_e[:WIDTH, cols]) + dot(normed[TILES:, :], w_e[WIDTH:, cols])
        o_t[:TILES, cols] = embedded.astype(BF16)
        placed[:, cols] = dot(placing[...], o_t[:TILES, cols]).astype(BF16)
        for k in (7, 8, 6, 9, 5, 10, 4, 11, 3, 12, 2, 13, 1, 14, 0):
            dev = slides[k]
            src = placed.at[pl.ds(pl.multiple_of(dev[0] * CAP, CAP), CAP), cols]
            dst = x.at[pl.ds(pl.multiple_of(slide * CAP, CAP), CAP), cols]
            x_copies.append(begin(src, dst, send_x.at[part, k], recv_x.at[part, k], dev))
    own = pl.ds(pl.multiple_of(slide * CAP, CAP), CAP)
    x[own, :] = placed[own, :]

    for copy in near_copies:
        copy.wait_recv()
    for i in range(16):
        near[i : i + 1, :] = near_all[i][:1]
    far_copies = [begin(near, far.at[seq], send_f.at[k], recv_f.at[k], dev) for k, dev in enumerate(blocks)]
    far[seq] = near[...]
    place_in = lax.broadcasted_iota(jnp.int32, (CAP, 128), 0).astype(F32)
    for i in range(16):
        val[i * CAP : i * CAP + CAP, :] = jnp.where(place_in < near[i : i + 1, :], 1.0, 0.0)
    for t in range(3):
        perm[t] = (lax.broadcasted_iota(jnp.int32, (WIDTH, WIDTH), 0) == place_ref[t][:1, :]).astype(BF16)
    row = lax.broadcasted_iota(jnp.int32, (64, SLOTS), 0)
    filler = jnp.where(row == 0, 1.0, 0.0).astype(BF16)
    zeros = jnp.zeros((64, SLOTS), BF16)
    q_0[64:, :], q_1[:64, :] = filler, filler
    do_0[64:, :], do_1[:64, :] = zeros, zeros
    for copy in loads[3:]:
        copy.wait()
    mg_val = val[:SLOTS, :].astype(BF16)
    for c in range(6):
        cols = slice(c * 128, c * 128 + 128)
        mg[:, cols] = mg[:, cols] * mg_val

    @pl.loop(0, 3)
    def _(c):
        cols = pl.ds(pl.multiple_of(c * BLOCK, BLOCK), BLOCK)
        d_heads = lax.dot_general(mg[...], wout[cols, :], NT, preferred_element_type=F32).astype(BF16)
        do_tok[:, cols] = d_heads
        do_t[cols, :] = d_heads.T

    row = lax.broadcasted_iota(jnp.int32, (96, SLOTS), 0)
    pick = lax.broadcasted_iota(jnp.int32, (96, SLOTS), 1) == (row % 16) * CAP + (row // 16) * RATE
    pick = pick.astype(BF16)
    for copy in x_copies:
        copy.wait_recv()
    rows = dot(pick, x[...]).astype(BF16)
    for m in range(6):
        own_far[m] = rows[m * 16 : m * 16 + 16]

    up = (slide, lax.rem(z + 1, SIDE) * 2 + core)
    down = (slide, lax.rem(z + 3, SIDE) * 2 + core)
    across = lax.rem(z + 2, SIDE) * 2 + core
    to_up = begin(own_far, xd.at[:, seq], send_z.at[0], recv_z.at[0], up)
    to_down = begin(own_far, xd.at[:, seq], send_z.at[1], recv_z.at[1], down)
    to_side = [begin(own_far, xd.at[:, seq], send_s.at[0], recv_s.at[0], sibling)]
    xd[:, seq] = own_far[...]

    def project(first, rows_of):
        @pl.loop(0, 3)
        def _(c):
            cols = pl.ds(pl.multiple_of(c * BLOCK, BLOCK), BLOCK)
            x_t[cols, first : first + SLOTS] = rows_of(cols).T
            for w, tok, turned in ((w_k, k_tok, k_t), (w_v, v_tok, v_t)):
                part = dot(rows_of(slice(None)), w[:, cols]).astype(BF16)
                tok[first : first + SLOTS, cols] = part
                turned[cols, first : first + SLOTS] = part.T

    @pl.loop(0, 3)
    def _(c):
        cols = pl.ds(pl.multiple_of(c * BLOCK, BLOCK), BLOCK)
        query = dot(x[...], w_q[:, cols]).astype(BF16) * BF16(0.125)
        q_tok[:, cols] = query
        q_t[cols, :] = query.T

    to_up.wait_recv()
    relay_up = begin(xd.at[pl.ds(0, 3), down[1]], xd.at[pl.ds(0, 3), down[1]], send_z.at[2], recv_z.at[2], up)
    to_side.append(begin(xd.at[:, down[1]], xd.at[:, down[1]], send_s.at[1], recv_s.at[1], sibling))
    to_down.wait_recv()
    relay_down = begin(xd.at[pl.ds(3, 3), up[1]], xd.at[pl.ds(3, 3), up[1]], send_z.at[3], recv_z.at[3], down)
    to_side.append(begin(xd.at[:, up[1]], xd.at[:, up[1]], send_s.at[2], recv_s.at[2], sibling))

    project(0, lambda cols: x[:, cols])

    relay_up.wait_recv()
    relay_down.wait_recv()
    to_side.append(begin(xd.at[:, across], xd.at[:, across], send_s.at[3], recv_s.at[3], sibling))
    for copy in far_copies:
        copy.wait_recv()
    for m in range(6):
        for j in range(8):
            first = SLOTS + m * 128 + j * 16
            val[first : first + 16, :] = jnp.where(far[j] > m * RATE, 1.0, 0.0)
    bias[...] = jnp.where(val[...] > 0.5, 0.0, MASKED).astype(BF16)
    for copy in to_side:
        copy.wait_recv()

    project(SLOTS, lambda cols: xd[:, :, :, cols].reshape(SLOTS, WIDTH if isinstance(cols, slice) else BLOCK))

    for copy in to_side + far_copies + near_copies + x_copies + [to_up, to_down, relay_up, relay_down]:
        copy.wait_send()

    def close_keys(pair, a, third):
        rows = slice(third * PART, third * PART + PART)
        mine = lax.broadcasted_iota(jnp.int32, (PART, 128), 1) // 64 == a
        slot = lax.rem(pair // 2, 2)
        for offset, left, right in ((0, grad[a], q_cat[a]), (BLOCK, prob[a], do_cat[a])):
            lanes = pl.ds(pl.multiple_of(lax.rem(pair, 2) * 128 + offset, 128), 128)
            part = dot(left[rows, :], right[...]).astype(BF16)
            dkv[slot, rows, lanes] = jnp.where(mine, part, dkv[slot, rows, lanes])

    own_half = pl.multiple_of(core * 384, 384)
    its_half = pl.multiple_of((1 - core) * 384, 384)

    def parity(r):
        return r % 2 if isinstance(r, int) else lax.rem(r, 2)

    def axis_copies(r, t, axis, source, landing, send, recv, height):
        copies = []
        for d in (2, 1, 3):
            moved = dict(at)
            moved[axis] = lax.rem(at[axis] + d, SIDE)
            device = (moved["y"] * SIDE + moved["x"], moved["z"] * 2 + core)
            if height:
                src = source.at[r, t, pl.ds(pl.multiple_of(moved[axis] * height, height), height), :]
            else:
                src = source.at[r, t, moved[axis]]
            copies.append(remote(src, landing.at[r, t, d - 1], send.at[r, t, d - 1], recv.at[r, t, d - 1], device))
        return copies

    def pair_copy(r, t):
        src = g.at[parity(r), t, pl.ds(its_half, 384), :]
        return remote(src, half.at[r, t], send0.at[r, t], recv0.at[r, t], sibling)

    def a_copies(r, t):
        return axis_copies(r, t, ORDERS[t][0], pair_sum, from_a, send_a, recv_a, 96)

    def b_copies(r, t):
        return axis_copies(r, t, ORDERS[t][1], owned, from_b, send_b, recv_b, 24)

    def c_copies(r, t):
        return axis_copies(r, t, ORDERS[t][2], spread, from_c, send_c, recv_c, 0)

    def stage_pair(r, parts):
        for t in range(3):
            g[parity(r), t] = dot(perm[t], parts(t).astype(BF16)).astype(BF16)
            pair_copy(r, t).start()

    def stage_qkv(r):
        slot = parity(r)

        def parts(t):
            if t == 0:
                return dot(x_t[:, :SLOTS], dq_round[slot])
            return dot(x_t[...], dkv[slot, :, (t - 1) * BLOCK : t * BLOCK])

        stage_pair(r, parts)

    def stage_a(r):
        for t in range(3):
            copy = pair_copy(r, t)
            copy.wait_recv()
            mine = g[parity(r), t, pl.ds(own_half, 384), :].astype(F32)
            pair_sum[r, t] = (mine + half[r, t].astype(F32)).astype(BF16)
            for copy in a_copies(r, t):
                copy.start()

    def stage_b(r):
        for t in range(3):
            mine = pl.multiple_of(at[ORDERS[t][0]] * 96, 96)
            total = g[parity(r), t, pl.ds(pl.multiple_of(own_half + mine, 96), 96), :].astype(F32)
            total = total + half[r, t, pl.ds(mine, 96), :].astype(F32)
            for copy in a_copies(r, t):
                copy.wait_recv()
            for d in range(3):
                total = total + from_a[r, t, d].astype(F32)
            owned[r, t] = total
            for copy in b_copies(r, t):
                copy.start()

    def stage_c(r):
        for t in range(3):
            total = owned[r, t, pl.ds(pl.multiple_of(at[ORDERS[t][1]] * 24, 24), 24), :]
            for copy in b_copies(r, t):
                copy.wait_recv()
            for d in range(3):
                total = total + from_b[r, t, d]
            for c in range(SIDE):
                spread[r, t, c, :6, :] = total[c * 6 : c * 6 + 6]
                spread[r, t, c, 6:, :] = jnp.zeros((2, BLOCK), F32)
            for copy in c_copies(r, t):
                copy.start()

    def stage_out(r):
        for t in range(3):
            total = spread[r, t, at[ORDERS[t][2]]]
            for copy in c_copies(r, t):
                copy.wait_recv()
            for d in range(3):
                total = total + from_c[r, t, d]
            total = total[:6] * factor
            if r < 3:
                first = t * WIDTH + r * BLOCK
                oq_ref[:, first : first + BLOCK] = total
            else:
                oo_ref[:, t * BLOCK : t * BLOCK + BLOCK] = total

    def sent(r):
        for t in range(3):
            for copy in a_copies(r, t) + b_copies(r, t) + c_copies(r, t):
                copy.wait_send()

    @pl.loop(0, HEADS // 2)
    def _(pair):
        lanes = pl.ds(pl.multiple_of(pair * 128, 128), 128)
        before = lax.max(pair - 1, 0)
        done = lax.max(pair // 2 - 1, 0)
        lane = lax.broadcasted_iota(jnp.int32, (KEYS, 128), 1)
        lane_q = lax.broadcasted_iota(jnp.int32, (SLOTS, 128), 1)
        nothing = jnp.zeros((SLOTS, 128), BF16)

        def head_rows(a):
            return pl.ds(pl.multiple_of(pair * 128 + a * 64, 64), 64)

        def open_head(a):
            own = slice(a * 64, a * 64 + 64)
            keys[a][...] = jnp.where(lane // 64 == a, k_tok[:, lanes], bias[...])
            q_rows[a][own, :] = q_t[head_rows(a), :]
            do_rows[a][own, :] = do_t[head_rows(a), :]

        def score_part(step, part):
            a, block = step // 3, step % 3
            rows = slice(part * PART, part * PART + PART)
            cols = slice(block * BLOCK, block * BLOCK + BLOCK)
            s = dot(keys[a][rows, :], q_rows[a][:, cols])
            scores[step % 2][rows, :] = s
            return jnp.max(s, axis=0, keepdims=True)

        def top(parts):
            return jnp.maximum(jnp.maximum(parts[0], parts[1]), parts[2])

        open_head(0)
        peak = top([score_part(0, part) for part in range(3)])
        open_head(1)
        for step in range(6):
            a, block = step // 3, step % 3
            cols = slice(block * BLOCK, block * BLOCK + BLOCK)
            score = scores[step % 2]
            peaks, sums = [], []
            for part in range(3):
                rows = slice(part * PART, part * PART + PART)
                if step < 5:
                    peaks.append(score_part(step + 1, part))
                raw = jnp.exp(score[rows, :] - peak)
                score[rows, :] = raw
                sums.append(jnp.sum(raw, axis=0, keepdims=True))
            inverse = 1.0 / (sums[0] + sums[1] + sums[2])
            for part in range(3):
                rows = slice(part * PART, part * PART + PART)
                grad_p[rows, :] = dot(v_tok[rows, lanes], do_rows[a][:, cols])
                prob[a][rows, cols] = (score[rows, :] * inverse).astype(BF16)
            out = dot(v_t[head_rows(a), :], prob[a][:, cols]).astype(BF16)
            o_t[head_rows(a), cols] = out
            if a == 0:
                close_keys(before, 1, block)
            else:
                close_keys(pair, 0, block)
            delta = jnp.sum(do_t[head_rows(a), cols].astype(F32) * out.astype(F32), axis=0, keepdims=True)
            for part in range(3):
                rows = slice(part * PART, part * PART + PART)
                grad[a][rows, cols] = (score[rows, :] * ((grad_p[rows, :] - delta) * inverse)).astype(BF16)
            dq_t[a * 64 : a * 64 + 64, cols] = (dot(k_t[head_rows(a), :], grad[a][:, cols]) * 0.125).astype(BF16)
            if step < 5:
                peak = top(peaks)
            if step == 2:
                @pl.when((pair == 2) | (pair == 4))
                def _():
                    stage_qkv(done)

                @pl.when((pair == 3) | (pair == 5))
                def _():
                    stage_b(done)

                @pl.when(pair == 4)
                def _():
                    stage_out(0)

            if block == 2:
                half_lanes = lane_q // 64 == a
                q_cat[a][...] = jnp.where(half_lanes, q_tok[:, lanes], nothing)
                do_cat[a][...] = jnp.where(half_lanes, do_tok[:, lanes], nothing)
        dq_round[lax.rem(pair // 2, 2), :, pl.ds(pl.multiple_of(lax.rem(pair, 2) * 128, 128), 128)] = dq_t[...].T

        @pl.when((pair == 2) | (pair == 4))
        def _():
            stage_a(done)

        @pl.when((pair == 3) | (pair == 5))
        def _():
            stage_c(done)

    for third in range(3):
        close_keys(HEADS // 2 - 1, 1, third)
    for t in range(3):
        pair_copy(0, t).wait_send()
    stage_qkv(2)
    for t in range(3):
        pair_copy(1, t).wait_send()
    stage_pair(3, lambda t: dot(o_t[...], mg[:, t * BLOCK : t * BLOCK + BLOCK]))
    stage_a(2)
    do_tok[...] = o_t[...].T
    stage_a(3)

    @pl.loop(0, 3)
    def _(c):
        cols = pl.ds(pl.multiple_of(c * BLOCK, BLOCK), BLOCK)
        mixed = x[:, cols].astype(F32) + dot(do_tok[...], wout[:, cols])
        q_tok[:, cols] = (mixed * val[:SLOTS, :1]).astype(BF16)

    store = pltpu.make_async_copy(q_tok, att_ref, load.at[0])
    store.start()
    stage_out(1)
    for stage in (stage_b, stage_c, stage_out):
        stage(2)
        stage(3)
    for r in range(4):
        sent(r)
    for r in (2, 3):
        for t in range(3):
            pair_copy(r, t).wait_send()
    store.wait()


def whole(feats, gain, w_embed, target, cot, w_qkv, w_out, factor):
    tall, wide, square = (KEYS, WIDTH), (WIDTH, KEYS), (SLOTS, WIDTH)
    vmem, anywhere = pl.BlockSpec(memory_space=pltpu.VMEM), pl.BlockSpec(memory_space=pl.ANY)
    dma = pltpu.SemaphoreType.DMA
    half16 = lambda *shapes: [pltpu.VMEM(shape, BF16) for shape in shapes]
    full32 = lambda *shapes: [pltpu.VMEM(shape, F32) for shape in shapes]
    scratch = half16(square, (6, 8, 16, WIDTH)) + full32((KEYS, 128)) + half16((KEYS, 128))
    scratch += half16(square, tall, tall, square, square, wide, wide, square, wide, square, square, square)
    scratch += half16((128, SLOTS), (2, SLOTS, BLOCK), (2, KEYS, 2 * BLOCK))
    scratch += full32((KEYS, BLOCK), (KEYS, BLOCK), (KEYS, BLOCK)) + half16(tall, tall, tall, tall)
    scratch += half16(*[(KEYS, 128)] * 2, *[(128, SLOTS)] * 4, *[(SLOTS, 128)] * 4, (3, WIDTH, WIDTH))
    scratch += full32((16, 8, 128), (16, 8, 128), (16, 128), (8, 16, 128)) + half16((6, 16, WIDTH))
    scratch += half16((2, 3, WIDTH, BLOCK), (4, 3, 384, BLOCK), (4, 3, 384, BLOCK), (4, 3, 3, 96, BLOCK))
    scratch += full32((4, 3, 96, BLOCK), (4, 3, 3, 24, BLOCK), (4, 3, SIDE, 8, BLOCK), (4, 3, 3, 8, BLOCK))
    scratch += [dma((8,)), dma((2, 15)), dma((2, 15)), dma((15,)), dma((15,)), dma((7,)), dma((7,))]
    scratch += [dma((4,))] * 4 + [dma((4, 3))] * 2 + [dma((4, 3, 3))] * 6
    return pl.pallas_call(
        functools.partial(whole_kernel, factor),
        out_shape=(
            jax.ShapeDtypeStruct(square, BF16),
            jax.ShapeDtypeStruct((6, 3 * WIDTH), F32),
            jax.ShapeDtypeStruct((6, WIDTH), F32),
        ),
        in_specs=[anywhere, vmem, anywhere, vmem, anywhere, anywhere, anywhere, vmem],
        out_specs=(anywhere, vmem, vmem),
        scratch_shapes=scratch,
        compiler_params=pltpu.CompilerParams(
            collective_id=1, has_side_effects=True, vmem_limit_bytes=63 * 1024 * 1024
        ),
        cost_estimate=pl.CostEstimate(flops=30_000_000_000, bytes_accessed=16_000_000, transcendentals=14_000_000),
        name="whole",
    )(feats, gain, w_embed, target, cot, w_qkv, w_out, jnp.asarray(row_orders()))


def shards(tile_feats, norm_gain, w_embed, slide_of_tile, w_qkv, w_out, cotangent):
    factor = (lax.axis_size("slide") * lax.axis_size("seq") * SLOTS) ** (-0.5)
    output, grad_qkv, grad_out = whole(
        tile_feats, norm_gain.reshape(1, WIDE), w_embed, slide_of_tile.reshape(1, TILES),
        cotangent[0], w_qkv, w_out, factor,
    )
    return (output[None], grad_qkv, grad_out)


def solution(mesh):
    return jax.shard_map(
        shards,
        mesh=mesh,
        in_specs=(
            P(("slide", "seq"), None),
            P(),
            P(),
            P(("slide", "seq"), None),
            P(),
            P(),
            P("slide", "seq", None),
        ),
        out_specs=(P("slide", "seq", None), P(("slide", "seq"), None), P(("slide", "seq"), None)),
        check_vma=False,
    )
```

```python
import functools

import jax
import jax.numpy as jnp
import numpy as np
from jax import lax
from jax.experimental import pallas as pl
from jax.experimental.pallas import tpu as pltpu
from jax.sharding import PartitionSpec as P

HEADS = 12
CAP = 48
RATE = 8
WIDTH = 768
WIDE = 1536
TILES = 384
SLOTS = 768
KEYS = 1536
BLOCK = 256
PART = 512
SIDE = 4
MASKED = -1e30
BF16 = jnp.bfloat16
F32 = jnp.float32
MESH = pl.DeviceIdType.MESH
ORDERS = (("x", "y", "z"), ("y", "z", "x"), ("z", "x", "y"))
NT = (((1,), (1,)), ((), ()))


def row_orders():
    feature = np.arange(WIDTH)
    device, inner = feature // 6, feature % 6
    at = {"core": device % 2, "z": device // 2 % 4, "x": device // 8 % 4, "y": device // 32}
    places = [
        at["core"] * 384 + at[a] * 96 + at[b] * 24 + at[c] * 6 + inner for a, b, c in ORDERS
    ]
    return np.broadcast_to(np.stack(places)[:, None, :], (3, 8, WIDTH)).astype(np.int32)


def dot(a, b):
    return jnp.dot(a, b, preferred_element_type=F32)


def whole_kernel(
    factor,
    feats_ref, gain_ref, we_ref, target_ref, cot_ref, wqkv_ref, wout_ref, place_ref,
    att_ref, oq_ref, oo_ref,
    x, xd, val, bias, q_tok, k_tok, v_tok, do_tok, q_t, k_t, v_t, do_t, x_t, mg, o_t, wout,
    dq_t, dq_round, dkv, score_0, score_1, grad_p, prob_0, prob_1, grad_0, grad_1,
    key_0, key_1, q_0, q_1, do_0, do_1, qc_0, qc_1, dc_0, dc_1, perm,
    tally, near_all, near, far, own_far,
    g, half, pair_sum, from_a, owned, from_b, spread, from_c,
    load, send_x, recv_x, send_n, recv_n, send_f, recv_f, send_z, recv_z, send_s, recv_s,
    send0, recv0, send_a, recv_a, send_b, recv_b, send_c, recv_c,
):
    scores, prob, grad = (score_0, score_1), (prob_0, prob_1), (grad_0, grad_1)
    keys, q_rows, do_rows = (key_0, key_1), (q_0, q_1), (do_0, do_1)
    q_cat, do_cat = (qc_0, qc_1), (dc_0, dc_1)
    slide, seq = lax.axis_index("slide"), lax.axis_index("seq")
    at = {"y": slide // SIDE, "x": slide % SIDE, "z": seq // 2}
    z, core = at["z"], seq % 2
    sibling = (slide, z * 2 + 1 - core)
    slides = [(lax.rem(slide + k, 16), seq) for k in range(1, 16)]
    blocks = [(slide, lax.rem(seq + k, 8)) for k in range(1, 8)]

    barrier = pltpu.get_barrier_semaphore()
    for device in slides + blocks:
        pl.semaphore_signal(barrier, inc=1, device_id=device, device_id_type=MESH)

    def remote(src, dst, send, recv, device):
        return pltpu.make_async_remote_copy(
            src_ref=src, dst_ref=dst, send_sem=send, recv_sem=recv, device_id=device, device_id_type=MESH
        )

    def begin(*args):
        copy = remote(*args)
        copy.start()
        return copy

    feats, normed, placed, w_e, w_q, w_k, w_v = (
        grad_0.at[:SLOTS], grad_1.at[:SLOTS], grad_1.at[SLOTS:], prob_1,
        prob_0.at[:SLOTS], prob_0.at[SLOTS:], grad_0.at[SLOTS:],
    )
    sources = [
        (feats_ref.at[:, :WIDTH], feats.at[:TILES]), (feats_ref.at[:, WIDTH:], feats.at[TILES:]),
        (we_ref, w_e), (cot_ref, mg), (wout_ref, wout),
        (wqkv_ref.at[:, :WIDTH], w_q), (wqkv_ref.at[:, WIDTH : 2 * WIDTH], w_k), (wqkv_ref.at[:, 2 * WIDTH :], w_v),
    ]
    loads = [pltpu.make_async_copy(src, dst, load.at[n]) for n, (src, dst) in enumerate(sources)]
    for copy in loads:
        copy.start()

    target = target_ref[...]
    named = lax.broadcasted_iota(jnp.int32, (16, TILES), 0) == target
    one_hot = jnp.where(named, 1.0, 0.0)
    earlier = (
        lax.broadcasted_iota(jnp.int32, (TILES, TILES), 0) < lax.broadcasted_iota(jnp.int32, (TILES, TILES), 1)
    ).astype(BF16)
    before_it = dot(one_hot.astype(BF16), earlier)
    rank = jnp.sum(one_hot * before_it, axis=0, keepdims=True)
    slot = target * CAP + rank.astype(jnp.int32)
    placing = x_t.at[:, :TILES]
    placing[...] = (lax.broadcasted_iota(jnp.int32, (SLOTS, TILES), 0) == slot).astype(BF16)
    total = jnp.sum(one_hot, axis=1, keepdims=True)
    for d in range(16):
        tally[d] = jnp.broadcast_to(total[d : d + 1], (8, 128))
    loads[0].wait()
    loads[1].wait()

    @pl.loop(0, 4)
    def _(c):
        low = pl.ds(pl.multiple_of(c * 96, 96), 96)
        high = pl.ds(pl.multiple_of(c * 96 + TILES, 96), 96)
        values = [feats[low, :].astype(F32), feats[high, :].astype(F32)]
        center = sum(jnp.sum(v, axis=-1, keepdims=True) for v in values) * (1.0 / WIDE)
        moved = [v - center for v in values]
        spread_sq = sum(jnp.sum(v * v, axis=-1, keepdims=True) for v in moved) * (1.0 / WIDE)
        scale = lax.rsqrt(spread_sq + 1e-06)
        normed[low, :] = (moved[0] * scale * gain_ref[:WIDTH].reshape(1, WIDTH)).astype(BF16)
        normed[high, :] = (moved[1] * scale * gain_ref[WIDTH:].reshape(1, WIDTH)).astype(BF16)

    pl.semaphore_wait(barrier, 22)
    near_copies = [
        begin(tally.at[dev[0]], near_all.at[slide], send_n.at[k], recv_n.at[k], dev) for k, dev in enumerate(slides)
    ]
    near_all[slide] = tally[slide]
    loads[2].wait()
    x_copies = []
    for part in range(2):
        cols = slice(part * 384, part * 384 + 384)
        embedded = dot(normed[:TILES, :], w_e[:WIDTH, cols]) + dot(normed[TILES:, :], w_e[WIDTH:, cols])
        o_t[:TILES, cols] = embedded.astype(BF16)
        placed[:, cols] = dot(placing[...], o_t[:TILES, cols]).astype(BF16)
        for k in (7, 8, 6, 9, 5, 10, 4, 11, 3, 12, 2, 13, 1, 14, 0):
            dev = slides[k]
            src = placed.at[pl.ds(pl.multiple_of(dev[0] * CAP, CAP), CAP), cols]
            dst = x.at[pl.ds(pl.multiple_of(slide * CAP, CAP), CAP), cols]
            x_copies.append(begin(src, dst, send_x.at[part, k], recv_x.at[part, k], dev))
    own = pl.ds(pl.multiple_of(slide * CAP, CAP), CAP)
    x[own, :] = placed[own, :]

    for copy in near_copies:
        copy.wait_recv()
    for i in range(16):
        near[i : i + 1, :] = near_all[i][:1]
    far_copies = [begin(near, far.at[seq], send_f.at[k], recv_f.at[k], dev) for k, dev in enumerate(blocks)]
    far[seq] = near[...]
    place_in = lax.broadcasted_iota(jnp.int32, (CAP, 128), 0).astype(F32)
    for i in range(16):
        val[i * CAP : i * CAP + CAP, :] = jnp.where(place_in < near[i : i + 1, :], 1.0, 0.0)
    for t in range(3):
        perm[t] = (lax.broadcasted_iota(jnp.int32, (WIDTH, WIDTH), 0) == place_ref[t][:1, :]).astype(BF16)
    row = lax.broadcasted_iota(jnp.int32, (64, SLOTS), 0)
    filler = jnp.where(row == 0, 1.0, 0.0).astype(BF16)
    zeros = jnp.zeros((64, SLOTS), BF16)
    q_0[64:, :], q_1[:64, :] = filler, filler
    do_0[64:, :], do_1[:64, :] = zeros, zeros
    for copy in loads[3:]:
        copy.wait()
    mg_val = val[:SLOTS, :].astype(BF16)
    for c in range(6):
        cols = slice(c * 128, c * 128 + 128)
        mg[:, cols] = mg[:, cols] * mg_val

    @pl.loop(0, 3)
    def _(c):
        cols = pl.ds(pl.multiple_of(c * BLOCK, BLOCK), BLOCK)
        d_heads = lax.dot_general(mg[...], wout[cols, :], NT, preferred_element_type=F32).astype(BF16)
        do_tok[:, cols] = d_heads
        do_t[cols, :] = d_heads.T

    row = lax.broadcasted_iota(jnp.int32, (96, SLOTS), 0)
    pick = lax.broadcasted_iota(jnp.int32, (96, SLOTS), 1) == (row % 16) * CAP + (row // 16) * RATE
    pick = pick.astype(BF16)
    for copy in x_copies:
        copy.wait_recv()
    rows = dot(pick, x[...]).astype(BF16)
    for m in range(6):
        own_far[m] = rows[m * 16 : m * 16 + 16]

    up = (slide, lax.rem(z + 1, SIDE) * 2 + core)
    down = (slide, lax.rem(z + 3, SIDE) * 2 + core)
    across = lax.rem(z + 2, SIDE) * 2 + core
    to_up = begin(own_far, xd.at[:, seq], send_z.at[0], recv_z.at[0], up)
    to_down = begin(own_far, xd.at[:, seq], send_z.at[1], recv_z.at[1], down)
    to_side = [begin(own_far, xd.at[:, seq], send_s.at[0], recv_s.at[0], sibling)]
    xd[:, seq] = own_far[...]

    def project(first, rows_of):
        @pl.loop(0, 3)
        def _(c):
            cols = pl.ds(pl.multiple_of(c * BLOCK, BLOCK), BLOCK)
            x_t[cols, first : first + SLOTS] = rows_of(cols).T
            for w, tok, turned in ((w_k, k_tok, k_t), (w_v, v_tok, v_t)):
                part = dot(rows_of(slice(None)), w[:, cols]).astype(BF16)
                tok[first : first + SLOTS, cols] = part
                turned[cols, first : first + SLOTS] = part.T

    @pl.loop(0, 3)
    def _(c):
        cols = pl.ds(pl.multiple_of(c * BLOCK, BLOCK), BLOCK)
        query = dot(x[...], w_q[:, cols]).astype(BF16) * BF16(0.125)
        q_tok[:, cols] = query
        q_t[cols, :] = query.T

    to_up.wait_recv()
    relay_up = begin(xd.at[pl.ds(0, 3), down[1]], xd.at[pl.ds(0, 3), down[1]], send_z.at[2], recv_z.at[2], up)
    to_side.append(begin(xd.at[:, down[1]], xd.at[:, down[1]], send_s.at[1], recv_s.at[1], sibling))
    to_down.wait_recv()
    relay_down = begin(xd.at[pl.ds(3, 3), up[1]], xd.at[pl.ds(3, 3), up[1]], send_z.at[3], recv_z.at[3], down)
    to_side.append(begin(xd.at[:, up[1]], xd.at[:, up[1]], send_s.at[2], recv_s.at[2], sibling))

    project(0, lambda cols: x[:, cols])

    relay_up.wait_recv()
    relay_down.wait_recv()
    to_side.append(begin(xd.at[:, across], xd.at[:, across], send_s.at[3], recv_s.at[3], sibling))
    for copy in far_copies:
        copy.wait_recv()
    for m in range(6):
        for j in range(8):
            first = SLOTS + m * 128 + j * 16
            val[first : first + 16, :] = jnp.where(far[j] > m * RATE, 1.0, 0.0)
    bias[...] = jnp.where(val[...] > 0.5, 0.0, MASKED).astype(BF16)
    for copy in to_side:
        copy.wait_recv()

    project(SLOTS, lambda cols: xd[:, :, :, cols].reshape(SLOTS, WIDTH if isinstance(cols, slice) else BLOCK))

    for copy in to_side + far_copies + near_copies + x_copies + [to_up, to_down, relay_up, relay_down]:
        copy.wait_send()

    def close_keys(pair, a, which):
        mine = lax.broadcasted_iota(jnp.int32, (KEYS, 128), 1) // 64 == a
        slot = lax.rem(pair // 2, 2)
        left, right, offset = ((prob[a], do_cat[a], BLOCK), (grad[a], q_cat[a], 0))[which]
        lanes = pl.ds(pl.multiple_of(lax.rem(pair, 2) * 128 + offset, 128), 128)
        part = dot(left[...], right[...]).astype(BF16)
        dkv[slot, :, lanes] = jnp.where(mine, part, dkv[slot, :, lanes])

    own_half = pl.multiple_of(core * 384, 384)
    its_half = pl.multiple_of((1 - core) * 384, 384)

    def parity(r):
        return r % 2 if isinstance(r, int) else lax.rem(r, 2)

    def axis_copies(r, t, axis, source, landing, send, recv, height):
        copies = []
        for d in (2, 1, 3):
            moved = dict(at)
            moved[axis] = lax.rem(at[axis] + d, SIDE)
            device = (moved["y"] * SIDE + moved["x"], moved["z"] * 2 + core)
            if height:
                src = source.at[r, t, pl.ds(pl.multiple_of(moved[axis] * height, height), height), :]
            else:
                src = source.at[r, t, moved[axis]]
            copies.append(remote(src, landing.at[r, t, d - 1], send.at[r, t, d - 1], recv.at[r, t, d - 1], device))
        return copies

    def pair_copy(r, t):
        src = g.at[parity(r), t, pl.ds(its_half, 384), :]
        return remote(src, half.at[r, t], send0.at[r, t], recv0.at[r, t], sibling)

    def a_copies(r, t):
        return axis_copies(r, t, ORDERS[t][0], pair_sum, from_a, send_a, recv_a, 96)

    def b_copies(r, t):
        return axis_copies(r, t, ORDERS[t][1], owned, from_b, send_b, recv_b, 24)

    def c_copies(r, t):
        return axis_copies(r, t, ORDERS[t][2], spread, from_c, send_c, recv_c, 0)

    def stage_pair(r, parts):
        for t in range(3):
            g[parity(r), t] = dot(perm[t], parts(t).astype(BF16)).astype(BF16)
            pair_copy(r, t).start()

    def stage_qkv(r):
        slot = parity(r)

        def parts(t):
            if t == 0:
                return dot(x_t[:, :SLOTS], dq_round[slot])
            return dot(x_t[...], dkv[slot, :, (t - 1) * BLOCK : t * BLOCK])

        stage_pair(r, parts)

    def stage_a(r):
        for t in range(3):
            copy = pair_copy(r, t)
            copy.wait_recv()
            mine = g[parity(r), t, pl.ds(own_half, 384), :].astype(F32)
            pair_sum[r, t] = (mine + half[r, t].astype(F32)).astype(BF16)
            for copy in a_copies(r, t):
                copy.start()

    def stage_b(r):
        for t in range(3):
            mine = pl.multiple_of(at[ORDERS[t][0]] * 96, 96)
            total = g[parity(r), t, pl.ds(pl.multiple_of(own_half + mine, 96), 96), :].astype(F32)
            total = total + half[r, t, pl.ds(mine, 96), :].astype(F32)
            for copy in a_copies(r, t):
                copy.wait_recv()
            for d in range(3):
                total = total + from_a[r, t, d].astype(F32)
            owned[r, t] = total
            for copy in b_copies(r, t):
                copy.start()

    def stage_c(r):
        for t in range(3):
            total = owned[r, t, pl.ds(pl.multiple_of(at[ORDERS[t][1]] * 24, 24), 24), :]
            for copy in b_copies(r, t):
                copy.wait_recv()
            for d in range(3):
                total = total + from_b[r, t, d]
            for c in range(SIDE):
                spread[r, t, c, :6, :] = total[c * 6 : c * 6 + 6]
                spread[r, t, c, 6:, :] = jnp.zeros((2, BLOCK), F32)
            for copy in c_copies(r, t):
                copy.start()

    def stage_out(r):
        for t in range(3):
            total = spread[r, t, at[ORDERS[t][2]]]
            for copy in c_copies(r, t):
                copy.wait_recv()
            for d in range(3):
                total = total + from_c[r, t, d]
            total = total[:6] * factor
            if r < 3:
                first = t * WIDTH + r * BLOCK
                oq_ref[:, first : first + BLOCK] = total
            else:
                oo_ref[:, t * BLOCK : t * BLOCK + BLOCK] = total

    def sent(r):
        for t in range(3):
            for copy in a_copies(r, t) + b_copies(r, t) + c_copies(r, t):
                copy.wait_send()

    @pl.loop(0, HEADS // 2)
    def _(pair):
        lanes = pl.ds(pl.multiple_of(pair * 128, 128), 128)
        before = lax.max(pair - 1, 0)
        done = lax.max(pair // 2 - 1, 0)
        lane = lax.broadcasted_iota(jnp.int32, (KEYS, 128), 1)
        lane_q = lax.broadcasted_iota(jnp.int32, (SLOTS, 128), 1)
        nothing = jnp.zeros((SLOTS, 128), BF16)

        def head_rows(a):
            return pl.ds(pl.multiple_of(pair * 128 + a * 64, 64), 64)

        def open_head(a):
            own = slice(a * 64, a * 64 + 64)
            keys[a][...] = jnp.where(lane // 64 == a, k_tok[:, lanes], bias[...])
            q_rows[a][own, :] = q_t[head_rows(a), :]
            do_rows[a][own, :] = do_t[head_rows(a), :]

        def score_step(step):
            a, block = step // 3, step % 3
            s = dot(keys[a][...], q_rows[a][:, block * BLOCK : block * BLOCK + BLOCK])
            scores[step % 2][...] = s
            return jnp.max(s, axis=0, keepdims=True)

        open_head(0)
        peak = score_step(0)
        open_head(1)
        for step in range(6):
            a, block = step // 3, step % 3
            cols = slice(block * BLOCK, block * BLOCK + BLOCK)
            score = scores[step % 2]
            sums = []
            if step < 5:
                next_peak = score_step(step + 1)
            for part in range(3):
                rows = slice(part * PART, part * PART + PART)
                raw = jnp.exp(score[rows, :] - peak)
                score[rows, :] = raw
                sums.append(jnp.sum(raw, axis=0, keepdims=True))
            inverse = 1.0 / (sums[0] + sums[1] + sums[2])
            grad_p[...] = dot(v_tok[:, lanes], do_rows[a][:, cols])
            for part in range(3):
                rows = slice(part * PART, part * PART + PART)
                prob[a][rows, cols] = (score[rows, :] * inverse).astype(BF16)
            out = dot(v_t[head_rows(a), :], prob[a][:, cols]).astype(BF16)
            o_t[head_rows(a), cols] = out
            if block < 2:
                close_keys(before if a == 0 else pair, 1 - a, block)
            delta = jnp.sum(do_t[head_rows(a), cols].astype(F32) * out.astype(F32), axis=0, keepdims=True)
            for part in range(3):
                rows = slice(part * PART, part * PART + PART)
                grad[a][rows, cols] = (score[rows, :] * ((grad_p[rows, :] - delta) * inverse)).astype(BF16)
            dq_t[a * 64 : a * 64 + 64, cols] = (dot(k_t[head_rows(a), :], grad[a][:, cols]) * 0.125).astype(BF16)
            if step < 5:
                peak = next_peak
            if step == 2:
                @pl.when((pair == 2) | (pair == 4))
                def _():
                    stage_qkv(done)

                @pl.when((pair == 3) | (pair == 5))
                def _():
                    stage_b(done)

                @pl.when(pair == 4)
                def _():
                    stage_out(0)

            if block == 2:
                half_lanes = lane_q // 64 == a
                q_cat[a][...] = jnp.where(half_lanes, q_tok[:, lanes], nothing)
                do_cat[a][...] = jnp.where(half_lanes, do_tok[:, lanes], nothing)
        dq_round[lax.rem(pair // 2, 2), :, pl.ds(pl.multiple_of(lax.rem(pair, 2) * 128, 128), 128)] = dq_t[...].T

        @pl.when((pair == 2) | (pair == 4))
        def _():
            stage_a(done)

        @pl.when((pair == 3) | (pair == 5))
        def _():
            stage_c(done)

    for which in range(2):
        close_keys(HEADS // 2 - 1, 1, which)
    for t in range(3):
        pair_copy(0, t).wait_send()
    stage_qkv(2)
    for t in range(3):
        pair_copy(1, t).wait_send()
    stage_pair(3, lambda t: dot(o_t[...], mg[:, t * BLOCK : t * BLOCK + BLOCK]))
    stage_a(2)
    do_tok[...] = o_t[...].T
    stage_a(3)

    @pl.loop(0, 3)
    def _(c):
        cols = pl.ds(pl.multiple_of(c * BLOCK, BLOCK), BLOCK)
        mixed = x[:, cols].astype(F32) + dot(do_tok[...], wout[:, cols])
        q_tok[:, cols] = (mixed * val[:SLOTS, :1]).astype(BF16)

    store = pltpu.make_async_copy(q_tok, att_ref, load.at[0])
    store.start()
    stage_out(1)
    for stage in (stage_b, stage_c, stage_out):
        stage(2)
        stage(3)
    for r in range(4):
        sent(r)
    for r in (2, 3):
        for t in range(3):
            pair_copy(r, t).wait_send()
    store.wait()


def whole(feats, gain, w_embed, target, cot, w_qkv, w_out, factor):
    tall, wide, square = (KEYS, WIDTH), (WIDTH, KEYS), (SLOTS, WIDTH)
    vmem, anywhere = pl.BlockSpec(memory_space=pltpu.VMEM), pl.BlockSpec(memory_space=pl.ANY)
    dma = pltpu.SemaphoreType.DMA
    half16 = lambda *shapes: [pltpu.VMEM(shape, BF16) for shape in shapes]
    full32 = lambda *shapes: [pltpu.VMEM(shape, F32) for shape in shapes]
    scratch = half16(square, (6, 8, 16, WIDTH)) + full32((KEYS, 128)) + half16((KEYS, 128))
    scratch += half16(square, tall, tall, square, square, wide, wide, square, wide, square, square, square)
    scratch += half16((128, SLOTS), (2, SLOTS, BLOCK), (2, KEYS, 2 * BLOCK))
    scratch += full32((KEYS, BLOCK), (KEYS, BLOCK), (KEYS, BLOCK)) + half16(tall, tall, tall, tall)
    scratch += half16(*[(KEYS, 128)] * 2, *[(128, SLOTS)] * 4, *[(SLOTS, 128)] * 4, (3, WIDTH, WIDTH))
    scratch += full32((16, 8, 128), (16, 8, 128), (16, 128), (8, 16, 128)) + half16((6, 16, WIDTH))
    scratch += half16((2, 3, WIDTH, BLOCK), (4, 3, 384, BLOCK), (4, 3, 384, BLOCK), (4, 3, 3, 96, BLOCK))
    scratch += full32((4, 3, 96, BLOCK), (4, 3, 3, 24, BLOCK), (4, 3, SIDE, 8, BLOCK), (4, 3, 3, 8, BLOCK))
    scratch += [dma((8,)), dma((2, 15)), dma((2, 15)), dma((15,)), dma((15,)), dma((7,)), dma((7,))]
    scratch += [dma((4,))] * 4 + [dma((4, 3))] * 2 + [dma((4, 3, 3))] * 6
    return pl.pallas_call(
        functools.partial(whole_kernel, factor),
        out_shape=(
            jax.ShapeDtypeStruct(square, BF16),
            jax.ShapeDtypeStruct((6, 3 * WIDTH), F32),
            jax.ShapeDtypeStruct((6, WIDTH), F32),
        ),
        in_specs=[anywhere, vmem, anywhere, vmem, anywhere, anywhere, anywhere, vmem],
        out_specs=(anywhere, vmem, vmem),
        scratch_shapes=scratch,
        compiler_params=pltpu.CompilerParams(
            collective_id=1, has_side_effects=True, vmem_limit_bytes=63 * 1024 * 1024
        ),
        cost_estimate=pl.CostEstimate(flops=30_000_000_000, bytes_accessed=16_000_000, transcendentals=14_000_000),
        name="whole",
    )(feats, gain, w_embed, target, cot, w_qkv, w_out, jnp.asarray(row_orders()))


def shards(tile_feats, norm_gain, w_embed, slide_of_tile, w_qkv, w_out, cotangent):
    factor = (lax.axis_size("slide") * lax.axis_size("seq") * SLOTS) ** (-0.5)
    output, grad_qkv, grad_out = whole(
        tile_feats, norm_gain, w_embed, slide_of_tile.reshape(1, TILES),
        cotangent[0], w_qkv, w_out, factor,
    )
    return (output[None], grad_qkv, grad_out)


def solution(mesh):
    return jax.shard_map(
        shards,
        mesh=mesh,
        in_specs=(
            P(("slide", "seq"), None),
            P(),
            P(),
            P(("slide", "seq"), None),
            P(),
            P(),
            P("slide", "seq", None),
        ),
        out_specs=(P("slide", "seq", None), P(("slide", "seq"), None), P(("slide", "seq"), None)),
        check_vma=False,
    )
```

```python
import functools

import jax
import jax.numpy as jnp
import numpy as np
from jax import lax
from jax.experimental import pallas as pl
from jax.experimental.pallas import tpu as pltpu
from jax.sharding import PartitionSpec as P

HEADS = 12
CAP = 48
RATE = 8
WIDTH = 768
WIDE = 1536
TILES = 384
SLOTS = 768
KEYS = 1536
BLOCK = 256
PART = 512
CHAIN = 64
PARTS = KEYS // PART
SIDE = 4
MASKED = -1e30
BF16 = jnp.bfloat16
F32 = jnp.float32
MESH = pl.DeviceIdType.MESH
ORDERS = (("x", "y", "z"), ("y", "z", "x"), ("z", "x", "y"))
NT = (((1,), (1,)), ((), ()))


def row_orders():
    feature = np.arange(WIDTH)
    device, inner = feature // 6, feature % 6
    at = {"core": device % 2, "z": device // 2 % 4, "x": device // 8 % 4, "y": device // 32}
    places = [
        at["core"] * 384 + at[a] * 96 + at[b] * 24 + at[c] * 6 + inner for a, b, c in ORDERS
    ]
    return np.broadcast_to(np.stack(places)[:, None, :], (3, 8, WIDTH)).astype(np.int32)


def dot(a, b):
    return jnp.dot(a, b, preferred_element_type=F32)


def whole_kernel(
    factor,
    feats_ref, gain_ref, we_ref, target_ref, cot_ref, wqkv_ref, wout_ref, place_ref,
    att_ref, oq_ref, oo_ref,
    x, xd, val, bias, q_tok, k_tok, v_tok, do_tok, q_t, k_t, v_t, do_t, x_t, mg, o_t, wout,
    dq_t, dq_round, dkv, score_0, score_1, grad_p, prob_0, prob_1, grad_0, grad_1,
    key_0, key_1, q_0, q_1, do_0, do_1, qc_0, qc_1, dc_0, dc_1, perm,
    tally, near_all, near, far, own_far,
    g, half, pair_sum, from_a, owned, from_b, spread, from_c,
    load, send_x, recv_x, send_n, recv_n, send_f, recv_f, send_z, recv_z, send_s, recv_s,
    send0, recv0, send_a, recv_a, send_b, recv_b, send_c, recv_c,
):
    scores, prob, grad = (score_0, score_1), (prob_0, prob_1), (grad_0, grad_1)
    keys, q_rows, do_rows = (key_0, key_1), (q_0, q_1), (do_0, do_1)
    q_cat, do_cat = (qc_0, qc_1), (dc_0, dc_1)
    slide, seq = lax.axis_index("slide"), lax.axis_index("seq")
    at = {"y": slide // SIDE, "x": slide % SIDE, "z": seq // 2}
    z, core = at["z"], seq % 2
    sibling = (slide, z * 2 + 1 - core)
    slides = [(lax.rem(slide + k, 16), seq) for k in range(1, 16)]
    blocks = [(slide, lax.rem(seq + k, 8)) for k in range(1, 8)]

    barrier = pltpu.get_barrier_semaphore()
    for device in slides + blocks:
        pl.semaphore_signal(barrier, inc=1, device_id=device, device_id_type=MESH)

    def remote(src, dst, send, recv, device):
        return pltpu.make_async_remote_copy(
            src_ref=src, dst_ref=dst, send_sem=send, recv_sem=recv, device_id=device, device_id_type=MESH
        )

    def begin(*args):
        copy = remote(*args)
        copy.start()
        return copy

    feats, normed, placed, w_e, w_q, w_k, w_v = (
        grad_0.at[:SLOTS], grad_1.at[:SLOTS], grad_1.at[SLOTS:], prob_1,
        prob_0.at[:SLOTS], prob_0.at[SLOTS:], grad_0.at[SLOTS:],
    )
    sources = [
        (feats_ref.at[:, :WIDTH], feats.at[:TILES]), (feats_ref.at[:, WIDTH:], feats.at[TILES:]),
        (we_ref, w_e), (cot_ref, mg), (wout_ref, wout),
        (wqkv_ref.at[:, :WIDTH], w_q), (wqkv_ref.at[:, WIDTH : 2 * WIDTH], w_k), (wqkv_ref.at[:, 2 * WIDTH :], w_v),
    ]
    loads = [pltpu.make_async_copy(src, dst, load.at[n]) for n, (src, dst) in enumerate(sources)]
    for copy in loads:
        copy.start()

    target = target_ref[...]
    named = lax.broadcasted_iota(jnp.int32, (16, TILES), 0) == target
    one_hot = jnp.where(named, 1.0, 0.0)
    earlier = (
        lax.broadcasted_iota(jnp.int32, (TILES, TILES), 0) < lax.broadcasted_iota(jnp.int32, (TILES, TILES), 1)
    ).astype(BF16)
    before_it = dot(one_hot.astype(BF16), earlier)
    rank = jnp.sum(one_hot * before_it, axis=0, keepdims=True)
    slot = target * CAP + rank.astype(jnp.int32)
    placing = x_t.at[:, :TILES]
    placing[...] = (lax.broadcasted_iota(jnp.int32, (SLOTS, TILES), 0) == slot).astype(BF16)
    total = jnp.sum(one_hot, axis=1, keepdims=True)
    for d in range(16):
        tally[d] = jnp.broadcast_to(total[d : d + 1], (8, 128))
    loads[0].wait()
    loads[1].wait()

    @pl.loop(0, 4)
    def _(c):
        low = pl.ds(pl.multiple_of(c * 96, 96), 96)
        high = pl.ds(pl.multiple_of(c * 96 + TILES, 96), 96)
        values = [feats[low, :].astype(F32), feats[high, :].astype(F32)]
        center = sum(jnp.sum(v, axis=-1, keepdims=True) for v in values) * (1.0 / WIDE)
        moved = [v - center for v in values]
        spread_sq = sum(jnp.sum(v * v, axis=-1, keepdims=True) for v in moved) * (1.0 / WIDE)
        scale = lax.rsqrt(spread_sq + 1e-06)
        normed[low, :] = (moved[0] * scale * gain_ref[:WIDTH].reshape(1, WIDTH)).astype(BF16)
        normed[high, :] = (moved[1] * scale * gain_ref[WIDTH:].reshape(1, WIDTH)).astype(BF16)

    pl.semaphore_wait(barrier, 22)
    near_copies = [
        begin(tally.at[dev[0]], near_all.at[slide], send_n.at[k], recv_n.at[k], dev) for k, dev in enumerate(slides)
    ]
    near_all[slide] = tally[slide]
    loads[2].wait()
    x_copies = []
    for part in range(2):
        cols = slice(part * 384, part * 384 + 384)
        embedded = dot(normed[:TILES, :], w_e[:WIDTH, cols]) + dot(normed[TILES:, :], w_e[WIDTH:, cols])
        o_t[:TILES, cols] = embedded.astype(BF16)
        placed[:, cols] = dot(placing[...], o_t[:TILES, cols]).astype(BF16)
        for k in (7, 8, 6, 9, 5, 10, 4, 11, 3, 12, 2, 13, 1, 14, 0):
            dev = slides[k]
            src = placed.at[pl.ds(pl.multiple_of(dev[0] * CAP, CAP), CAP), cols]
            dst = x.at[pl.ds(pl.multiple_of(slide * CAP, CAP), CAP), cols]
            x_copies.append(begin(src, dst, send_x.at[part, k], recv_x.at[part, k], dev))
    own = pl.ds(pl.multiple_of(slide * CAP, CAP), CAP)
    x[own, :] = placed[own, :]

    for copy in near_copies:
        copy.wait_recv()
    for i in range(16):
        near[i : i + 1, :] = near_all[i][:1]
    far_copies = [begin(near, far.at[seq], send_f.at[k], recv_f.at[k], dev) for k, dev in enumerate(blocks)]
    far[seq] = near[...]
    place_in = lax.broadcasted_iota(jnp.int32, (CAP, 128), 0).astype(F32)
    for i in range(16):
        val[i * CAP : i * CAP + CAP, :] = jnp.where(place_in < near[i : i + 1, :], 1.0, 0.0)
    for t in range(3):
        perm[t] = (lax.broadcasted_iota(jnp.int32, (WIDTH, WIDTH), 0) == place_ref[t][:1, :]).astype(BF16)
    row = lax.broadcasted_iota(jnp.int32, (64, SLOTS), 0)
    filler = jnp.where(row == 0, 1.0, 0.0).astype(BF16)
    zeros = jnp.zeros((64, SLOTS), BF16)
    q_0[64:, :], q_1[:64, :] = filler, filler
    do_0[64:, :], do_1[:64, :] = zeros, zeros
    for copy in loads[3:]:
        copy.wait()
    mg_val = val[:SLOTS, :].astype(BF16)
    for c in range(6):
        cols = slice(c * 128, c * 128 + 128)
        mg[:, cols] = mg[:, cols] * mg_val

    @pl.loop(0, 3)
    def _(c):
        cols = pl.ds(pl.multiple_of(c * BLOCK, BLOCK), BLOCK)
        d_heads = lax.dot_general(mg[...], wout[cols, :], NT, preferred_element_type=F32).astype(BF16)
        do_tok[:, cols] = d_heads
        do_t[cols, :] = d_heads.T

    row = lax.broadcasted_iota(jnp.int32, (96, SLOTS), 0)
    pick = lax.broadcasted_iota(jnp.int32, (96, SLOTS), 1) == (row % 16) * CAP + (row // 16) * RATE
    pick = pick.astype(BF16)
    for copy in x_copies:
        copy.wait_recv()
    rows = dot(pick, x[...]).astype(BF16)
    for m in range(6):
        own_far[m] = rows[m * 16 : m * 16 + 16]

    up = (slide, lax.rem(z + 1, SIDE) * 2 + core)
    down = (slide, lax.rem(z + 3, SIDE) * 2 + core)
    across = lax.rem(z + 2, SIDE) * 2 + core
    to_up = begin(own_far, xd.at[:, seq], send_z.at[0], recv_z.at[0], up)
    to_down = begin(own_far, xd.at[:, seq], send_z.at[1], recv_z.at[1], down)
    to_side = [begin(own_far, xd.at[:, seq], send_s.at[0], recv_s.at[0], sibling)]
    xd[:, seq] = own_far[...]

    def project(first, rows_of):
        @pl.loop(0, 3)
        def _(c):
            cols = pl.ds(pl.multiple_of(c * BLOCK, BLOCK), BLOCK)
            x_t[cols, first : first + SLOTS] = rows_of(cols).T
            for w, tok, turned in ((w_k, k_tok, k_t), (w_v, v_tok, v_t)):
                part = dot(rows_of(slice(None)), w[:, cols]).astype(BF16)
                tok[first : first + SLOTS, cols] = part
                turned[cols, first : first + SLOTS] = part.T

    @pl.loop(0, 3)
    def _(c):
        cols = pl.ds(pl.multiple_of(c * BLOCK, BLOCK), BLOCK)
        query = dot(x[...], w_q[:, cols]).astype(BF16) * BF16(0.125)
        q_tok[:, cols] = query
        q_t[cols, :] = query.T

    to_up.wait_recv()
    relay_up = begin(xd.at[pl.ds(0, 3), down[1]], xd.at[pl.ds(0, 3), down[1]], send_z.at[2], recv_z.at[2], up)
    to_side.append(begin(xd.at[:, down[1]], xd.at[:, down[1]], send_s.at[1], recv_s.at[1], sibling))
    to_down.wait_recv()
    relay_down = begin(xd.at[pl.ds(3, 3), up[1]], xd.at[pl.ds(3, 3), up[1]], send_z.at[3], recv_z.at[3], down)
    to_side.append(begin(xd.at[:, up[1]], xd.at[:, up[1]], send_s.at[2], recv_s.at[2], sibling))

    project(0, lambda cols: x[:, cols])

    relay_up.wait_recv()
    relay_down.wait_recv()
    to_side.append(begin(xd.at[:, across], xd.at[:, across], send_s.at[3], recv_s.at[3], sibling))
    for copy in far_copies:
        copy.wait_recv()
    for m in range(6):
        for j in range(8):
            first = SLOTS + m * 128 + j * 16
            val[first : first + 16, :] = jnp.where(far[j] > m * RATE, 1.0, 0.0)
    bias[...] = jnp.where(val[...] > 0.5, 0.0, MASKED).astype(BF16)
    for copy in to_side:
        copy.wait_recv()

    project(SLOTS, lambda cols: xd[:, :, :, cols].reshape(SLOTS, WIDTH if isinstance(cols, slice) else BLOCK))

    for copy in to_side + far_copies + near_copies + x_copies + [to_up, to_down, relay_up, relay_down]:
        copy.wait_send()

    def close_keys(pair, a, third):
        rows = slice(third * PART, third * PART + PART)
        mine = lax.broadcasted_iota(jnp.int32, (PART, 128), 1) // 64 == a
        slot = lax.rem(pair // 2, 2)
        for offset, left, right in ((0, grad[a], q_cat[a]), (BLOCK, prob[a], do_cat[a])):
            lanes = pl.ds(pl.multiple_of(lax.rem(pair, 2) * 128 + offset, 128), 128)
            part = dot(left[rows, :], right[...]).astype(BF16)
            dkv[slot, rows, lanes] = jnp.where(mine, part, dkv[slot, rows, lanes])

    own_half = pl.multiple_of(core * 384, 384)
    its_half = pl.multiple_of((1 - core) * 384, 384)

    def parity(r):
        return r % 2 if isinstance(r, int) else lax.rem(r, 2)

    def axis_copies(r, t, axis, source, landing, send, recv, height):
        copies = []
        for d in (2, 1, 3):
            moved = dict(at)
            moved[axis] = lax.rem(at[axis] + d, SIDE)
            device = (moved["y"] * SIDE + moved["x"], moved["z"] * 2 + core)
            if height:
                src = source.at[r, t, pl.ds(pl.multiple_of(moved[axis] * height, height), height), :]
            else:
                src = source.at[r, t, moved[axis]]
            copies.append(remote(src, landing.at[r, t, d - 1], send.at[r, t, d - 1], recv.at[r, t, d - 1], device))
        return copies

    def pair_copy(r, t):
        src = g.at[parity(r), t, pl.ds(its_half, 384), :]
        return remote(src, half.at[r, t], send0.at[r, t], recv0.at[r, t], sibling)

    def a_copies(r, t):
        return axis_copies(r, t, ORDERS[t][0], pair_sum, from_a, send_a, recv_a, 96)

    def b_copies(r, t):
        return axis_copies(r, t, ORDERS[t][1], owned, from_b, send_b, recv_b, 24)

    def c_copies(r, t):
        return axis_copies(r, t, ORDERS[t][2], spread, from_c, send_c, recv_c, 0)

    def stage_pair(r, parts):
        for t in range(3):
            g[parity(r), t] = dot(perm[t], parts(t).astype(BF16)).astype(BF16)
            pair_copy(r, t).start()

    def stage_qkv(r):
        slot = parity(r)

        def parts(t):
            if t == 0:
                return dot(x_t[:, :SLOTS], dq_round[slot])
            return dot(x_t[...], dkv[slot, :, (t - 1) * BLOCK : t * BLOCK])

        stage_pair(r, parts)

    def stage_a(r):
        for t in range(3):
            copy = pair_copy(r, t)
            copy.wait_recv()
            mine = g[parity(r), t, pl.ds(own_half, 384), :].astype(F32)
            pair_sum[r, t] = (mine + half[r, t].astype(F32)).astype(BF16)
            for copy in a_copies(r, t):
                copy.start()

    def stage_b(r):
        for t in range(3):
            mine = pl.multiple_of(at[ORDERS[t][0]] * 96, 96)
            total = g[parity(r), t, pl.ds(pl.multiple_of(own_half + mine, 96), 96), :].astype(F32)
            total = total + half[r, t, pl.ds(mine, 96), :].astype(F32)
            for copy in a_copies(r, t):
                copy.wait_recv()
            for d in range(3):
                total = total + from_a[r, t, d].astype(F32)
            owned[r, t] = total
            for copy in b_copies(r, t):
                copy.start()

    def stage_c(r):
        for t in range(3):
            total = owned[r, t, pl.ds(pl.multiple_of(at[ORDERS[t][1]] * 24, 24), 24), :]
            for copy in b_copies(r, t):
                copy.wait_recv()
            for d in range(3):
                total = total + from_b[r, t, d]
            for c in range(SIDE):
                spread[r, t, c, :6, :] = total[c * 6 : c * 6 + 6]
                spread[r, t, c, 6:, :] = jnp.zeros((2, BLOCK), F32)
            for copy in c_copies(r, t):
                copy.start()

    def stage_out(r):
        for t in range(3):
            total = spread[r, t, at[ORDERS[t][2]]]
            for copy in c_copies(r, t):
                copy.wait_recv()
            for d in range(3):
                total = total + from_c[r, t, d]
            total = total[:6] * factor
            if r < 3:
                first = t * WIDTH + r * BLOCK
                oq_ref[:, first : first + BLOCK] = total
            else:
                oo_ref[:, t * BLOCK : t * BLOCK + BLOCK] = total

    def sent(r):
        for t in range(3):
            for copy in a_copies(r, t) + b_copies(r, t) + c_copies(r, t):
                copy.wait_send()

    @pl.loop(0, HEADS // 2)
    def _(pair):
        lanes = pl.ds(pl.multiple_of(pair * 128, 128), 128)
        before = lax.max(pair - 1, 0)
        done = lax.max(pair // 2 - 1, 0)
        lane = lax.broadcasted_iota(jnp.int32, (KEYS, 128), 1)
        lane_q = lax.broadcasted_iota(jnp.int32, (SLOTS, 128), 1)
        nothing = jnp.zeros((SLOTS, 128), BF16)

        def head_rows(a):
            return pl.ds(pl.multiple_of(pair * 128 + a * 64, 64), 64)

        def open_head(a):
            own = slice(a * 64, a * 64 + 64)
            keys[a][...] = jnp.where(lane // 64 == a, k_tok[:, lanes], bias[...])
            q_rows[a][own, :] = q_t[head_rows(a), :]
            do_rows[a][own, :] = do_t[head_rows(a), :]

        def score_part(step, part):
            a, block = step // 3, step % 3
            rows = slice(part * PART, part * PART + PART)
            s = dot(keys[a][rows, :], q_rows[a][:, block * BLOCK : block * BLOCK + BLOCK])
            scores[step % 2][rows, :] = s
            return jnp.max(s, axis=0, keepdims=True)

        def short(part):
            return [slice(first, first + CHAIN) for first in range(part * PART, part * PART + PART, CHAIN)]

        open_head(0)
        peaks = [score_part(0, part) for part in range(PARTS)]
        open_head(1)
        for step in range(6):
            a, block = step // 3, step % 3
            cols = slice(block * BLOCK, block * BLOCK + BLOCK)
            score = scores[step % 2]
            peak = functools.reduce(jnp.maximum, peaks)
            peaks, total = [], jnp.zeros((8, BLOCK), F32)
            for part in range(PARTS):
                if step < 5:
                    peaks.append(score_part(step + 1, part))
                for rows in short(part):
                    raw = jnp.exp(score[rows, :] - peak)
                    score[rows, :] = raw
                    total = total + jnp.sum(raw.reshape(CHAIN // 8, 8, BLOCK), axis=0)
            inverse = 1.0 / jnp.sum(total, axis=0, keepdims=True)
            for part in range(PARTS):
                whole_part = slice(part * PART, part * PART + PART)
                grad_p[whole_part, :] = dot(v_tok[whole_part, lanes], do_rows[a][:, cols])
                for rows in short(part):
                    prob[a][rows, cols] = (score[rows, :] * inverse).astype(BF16)
            out = dot(v_t[head_rows(a), :], prob[a][:, cols]).astype(BF16)
            o_t[head_rows(a), cols] = out
            if a == 0:
                close_keys(before, 1, block)
            else:
                close_keys(pair, 0, block)
            delta = jnp.sum(do_t[head_rows(a), cols].astype(F32) * out.astype(F32), axis=0, keepdims=True)
            for part in range(PARTS):
                for rows in short(part):
                    grad[a][rows, cols] = (score[rows, :] * ((grad_p[rows, :] - delta) * inverse)).astype(BF16)
            dq_t[a * 64 : a * 64 + 64, cols] = (dot(k_t[head_rows(a), :], grad[a][:, cols]) * 0.125).astype(BF16)
            if step == 2:
                @pl.when((pair == 2) | (pair == 4))
                def _():
                    stage_qkv(done)

                @pl.when((pair == 3) | (pair == 5))
                def _():
                    stage_b(done)

                @pl.when(pair == 4)
                def _():
                    stage_out(0)

            if block == 2:
                half_lanes = lane_q // 64 == a
                q_cat[a][...] = jnp.where(half_lanes, q_tok[:, lanes], nothing)
                do_cat[a][...] = jnp.where(half_lanes, do_tok[:, lanes], nothing)
        dq_round[lax.rem(pair // 2, 2), :, pl.ds(pl.multiple_of(lax.rem(pair, 2) * 128, 128), 128)] = dq_t[...].T

        @pl.when((pair == 2) | (pair == 4))
        def _():
            stage_a(done)

        @pl.when((pair == 3) | (pair == 5))
        def _():
            stage_c(done)

    for third in range(3):
        close_keys(HEADS // 2 - 1, 1, third)
    for t in range(3):
        pair_copy(0, t).wait_send()
    stage_qkv(2)
    for t in range(3):
        pair_copy(1, t).wait_send()
    stage_pair(3, lambda t: dot(o_t[...], mg[:, t * BLOCK : t * BLOCK + BLOCK]))
    stage_a(2)
    do_tok[...] = o_t[...].T
    stage_a(3)

    @pl.loop(0, 3)
    def _(c):
        cols = pl.ds(pl.multiple_of(c * BLOCK, BLOCK), BLOCK)
        mixed = x[:, cols].astype(F32) + dot(do_tok[...], wout[:, cols])
        q_tok[:, cols] = (mixed * val[:SLOTS, :1]).astype(BF16)

    store = pltpu.make_async_copy(q_tok, att_ref, load.at[0])
    store.start()
    stage_out(1)
    for stage in (stage_b, stage_c, stage_out):
        stage(2)
        stage(3)
    for r in range(4):
        sent(r)
    for r in (2, 3):
        for t in range(3):
            pair_copy(r, t).wait_send()
    store.wait()


def whole(feats, gain, w_embed, target, cot, w_qkv, w_out, factor):
    tall, wide, square = (KEYS, WIDTH), (WIDTH, KEYS), (SLOTS, WIDTH)
    vmem, anywhere = pl.BlockSpec(memory_space=pltpu.VMEM), pl.BlockSpec(memory_space=pl.ANY)
    dma = pltpu.SemaphoreType.DMA
    half16 = lambda *shapes: [pltpu.VMEM(shape, BF16) for shape in shapes]
    full32 = lambda *shapes: [pltpu.VMEM(shape, F32) for shape in shapes]
    scratch = half16(square, (6, 8, 16, WIDTH)) + full32((KEYS, 128)) + half16((KEYS, 128))
    scratch += half16(square, tall, tall, square, square, wide, wide, square, wide, square, square, square)
    scratch += half16((128, SLOTS), (2, SLOTS, BLOCK), (2, KEYS, 2 * BLOCK))
    scratch += full32((KEYS, BLOCK), (KEYS, BLOCK), (KEYS, BLOCK)) + half16(tall, tall, tall, tall)
    scratch += half16(*[(KEYS, 128)] * 2, *[(128, SLOTS)] * 4, *[(SLOTS, 128)] * 4, (3, WIDTH, WIDTH))
    scratch += full32((16, 8, 128), (16, 8, 128), (16, 128), (8, 16, 128)) + half16((6, 16, WIDTH))
    scratch += half16((2, 3, WIDTH, BLOCK), (4, 3, 384, BLOCK), (4, 3, 384, BLOCK), (4, 3, 3, 96, BLOCK))
    scratch += full32((4, 3, 96, BLOCK), (4, 3, 3, 24, BLOCK), (4, 3, SIDE, 8, BLOCK), (4, 3, 3, 8, BLOCK))
    scratch += [dma((8,)), dma((2, 15)), dma((2, 15)), dma((15,)), dma((15,)), dma((7,)), dma((7,))]
    scratch += [dma((4,))] * 4 + [dma((4, 3))] * 2 + [dma((4, 3, 3))] * 6
    return pl.pallas_call(
        functools.partial(whole_kernel, factor),
        out_shape=(
            jax.ShapeDtypeStruct(square, BF16),
            jax.ShapeDtypeStruct((6, 3 * WIDTH), F32),
            jax.ShapeDtypeStruct((6, WIDTH), F32),
        ),
        in_specs=[anywhere, vmem, anywhere, vmem, anywhere, anywhere, anywhere, vmem],
        out_specs=(anywhere, vmem, vmem),
        scratch_shapes=scratch,
        compiler_params=pltpu.CompilerParams(
            collective_id=1, has_side_effects=True, vmem_limit_bytes=63 * 1024 * 1024
        ),
        cost_estimate=pl.CostEstimate(flops=30_000_000_000, bytes_accessed=16_000_000, transcendentals=14_000_000),
        name="whole",
    )(feats, gain, w_embed, target, cot, w_qkv, w_out, jnp.asarray(row_orders()))


def hand_over_kernel(*refs):
    ins, outs, held, sem_in, sem_out = refs[:3], refs[3:6], refs[6:9], refs[9], refs[10]
    pieces = [(0, slice(first, first + 192)) for first in range(0, SLOTS, 192)] + [(1, slice(0, 6)), (2, slice(0, 6))]
    arriving, leaving = [], []
    for n, (which, rows) in enumerate(pieces):
        arriving.append(pltpu.make_async_copy(ins[which].at[rows], held[which].at[rows], sem_in.at[n]))
        leaving.append(pltpu.make_async_copy(held[which].at[rows], outs[which].at[rows], sem_out.at[n]))
    for copy in arriving:
        copy.start()
    for first, second in zip(arriving, leaving):
        first.wait()
        second.start()
    for copy in leaving:
        copy.wait()


def hand_over(*arrays):
    anywhere = pl.BlockSpec(memory_space=pl.ANY)
    return pl.pallas_call(
        hand_over_kernel,
        out_shape=tuple(jax.ShapeDtypeStruct(a.shape, a.dtype) for a in arrays),
        in_specs=[anywhere] * 3,
        out_specs=(anywhere,) * 3,
        scratch_shapes=[pltpu.VMEM(a.shape, a.dtype) for a in arrays] + [pltpu.SemaphoreType.DMA((6,))] * 2,
        compiler_params=pltpu.CompilerParams(vmem_limit_bytes=63 * 1024 * 1024),
        name="hand_over",
    )(*arrays)


def shards(tile_feats, norm_gain, w_embed, slide_of_tile, w_qkv, w_out, cotangent):
    factor = (lax.axis_size("slide") * lax.axis_size("seq") * SLOTS) ** (-0.5)
    output, grad_qkv, grad_out = hand_over(*whole(
        tile_feats, norm_gain, w_embed, slide_of_tile.reshape(1, TILES),
        cotangent[0], w_qkv, w_out, factor,
    ))
    return (output[None], grad_qkv, grad_out)


def solution(mesh):
    return jax.shard_map(
        shards,
        mesh=mesh,
        in_specs=(
            P(("slide", "seq"), None),
            P(),
            P(),
            P(("slide", "seq"), None),
            P(),
            P(),
            P("slide", "seq", None),
        ),
        out_specs=(P("slide", "seq", None), P(("slide", "seq"), None), P(("slide", "seq"), None)),
        check_vma=False,
    )
```

```python
import functools

import jax
import jax.numpy as jnp
import numpy as np
from jax import lax
from jax.experimental import pallas as pl
from jax.experimental.pallas import tpu as pltpu
from jax.sharding import PartitionSpec as P

HEADS = 12
CAP = 48
RATE = 8
WIDTH = 768
WIDE = 1536
TILES = 384
SLOTS = 768
KEYS = 1536
BLOCK = 256
PART = 512
CHAIN = 64
PARTS = KEYS // PART
SIDE = 4
MASKED = -1e30
BF16 = jnp.bfloat16
F32 = jnp.float32
MESH = pl.DeviceIdType.MESH
ORDERS = (("x", "y", "z"), ("y", "z", "x"), ("z", "x", "y"))
NT = (((1,), (1,)), ((), ()))


def row_orders():
    feature = np.arange(WIDTH)
    device, inner = feature // 6, feature % 6
    at = {"core": device % 2, "z": device // 2 % 4, "x": device // 8 % 4, "y": device // 32}
    places = [
        at["core"] * 384 + at[a] * 96 + at[b] * 24 + at[c] * 6 + inner for a, b, c in ORDERS
    ]
    return np.broadcast_to(np.stack(places)[:, None, :], (3, 8, WIDTH)).astype(np.int32)


def dot(a, b):
    return jnp.dot(a, b, preferred_element_type=F32)


def whole_kernel(
    factor,
    feats_ref, gain_ref, we_ref, target_ref, cot_ref, wqkv_ref, wout_ref, place_ref,
    att_ref, oq_ref, oo_ref,
    x, xd, val, bias, q_tok, k_tok, v_tok, do_tok, q_t, k_t, v_t, do_t, x_t, mg, o_t, wout,
    dq_t, dq_round, dkv, score_0, score_1, grad_p, prob_0, prob_1, grad_0, grad_1,
    key_0, key_1, q_0, q_1, do_0, do_1, qc_0, qc_1, dc_0, dc_1, perm,
    tally, near_all, near, far, own_far,
    g, half, pair_sum, from_a, owned, from_b, spread, from_c,
    load, send_x, recv_x, send_n, recv_n, send_f, recv_f, send_z, recv_z, send_s, recv_s,
    send0, recv0, send_a, recv_a, send_b, recv_b, send_c, recv_c,
):
    scores, prob, grad = (score_0, score_1), (prob_0, prob_1), (grad_0, grad_1)
    keys, q_rows, do_rows = (key_0, key_1), (q_0, q_1), (do_0, do_1)
    q_cat, do_cat = (qc_0, qc_1), (dc_0, dc_1)
    slide, seq = lax.axis_index("slide"), lax.axis_index("seq")
    at = {"y": slide // SIDE, "x": slide % SIDE, "z": seq // 2}
    z, core = at["z"], seq % 2
    sibling = (slide, z * 2 + 1 - core)
    slides = [(lax.rem(slide + k, 16), seq) for k in range(1, 16)]
    blocks = [(slide, lax.rem(seq + k, 8)) for k in range(1, 8)]

    barrier = pltpu.get_barrier_semaphore()
    for device in slides + blocks:
        pl.semaphore_signal(barrier, inc=1, device_id=device, device_id_type=MESH)

    def remote(src, dst, send, recv, device):
        return pltpu.make_async_remote_copy(
            src_ref=src, dst_ref=dst, send_sem=send, recv_sem=recv, device_id=device, device_id_type=MESH
        )

    def begin(*args):
        copy = remote(*args)
        copy.start()
        return copy

    feats, normed, placed, w_e, w_q, w_k, w_v = (
        grad_0.at[:SLOTS], grad_1.at[:SLOTS], grad_1.at[SLOTS:], prob_1,
        prob_0.at[:SLOTS], prob_0.at[SLOTS:], grad_0.at[SLOTS:],
    )
    sources = [
        (feats_ref.at[:, :WIDTH], feats.at[:TILES]), (feats_ref.at[:, WIDTH:], feats.at[TILES:]),
        (we_ref, w_e), (cot_ref, mg), (wout_ref, wout),
        (wqkv_ref.at[:, :WIDTH], w_q), (wqkv_ref.at[:, WIDTH : 2 * WIDTH], w_k), (wqkv_ref.at[:, 2 * WIDTH :], w_v),
    ]
    loads = [pltpu.make_async_copy(src, dst, load.at[n]) for n, (src, dst) in enumerate(sources)]
    for copy in loads:
        copy.start()

    target = target_ref[...]
    named = lax.broadcasted_iota(jnp.int32, (16, TILES), 0) == target
    one_hot = jnp.where(named, 1.0, 0.0)
    earlier = (
        lax.broadcasted_iota(jnp.int32, (TILES, TILES), 0) < lax.broadcasted_iota(jnp.int32, (TILES, TILES), 1)
    ).astype(BF16)
    before_it = dot(one_hot.astype(BF16), earlier)
    rank = jnp.sum(one_hot * before_it, axis=0, keepdims=True)
    slot = target * CAP + rank.astype(jnp.int32)
    placing = x_t.at[:, :TILES]
    placing[...] = (lax.broadcasted_iota(jnp.int32, (SLOTS, TILES), 0) == slot).astype(BF16)
    total = jnp.sum(one_hot, axis=1, keepdims=True)
    for d in range(16):
        tally[d] = jnp.broadcast_to(total[d : d + 1], (8, 128))
    loads[0].wait()
    loads[1].wait()

    @pl.loop(0, 4)
    def _(c):
        low = pl.ds(pl.multiple_of(c * 96, 96), 96)
        high = pl.ds(pl.multiple_of(c * 96 + TILES, 96), 96)
        values = [feats[low, :].astype(F32), feats[high, :].astype(F32)]
        center = sum(jnp.sum(v, axis=-1, keepdims=True) for v in values) * (1.0 / WIDE)
        moved = [v - center for v in values]
        spread_sq = sum(jnp.sum(v * v, axis=-1, keepdims=True) for v in moved) * (1.0 / WIDE)
        scale = lax.rsqrt(spread_sq + 1e-06)
        normed[low, :] = (moved[0] * scale * gain_ref[:WIDTH].reshape(1, WIDTH)).astype(BF16)
        normed[high, :] = (moved[1] * scale * gain_ref[WIDTH:].reshape(1, WIDTH)).astype(BF16)

    pl.semaphore_wait(barrier, 22)
    near_copies = [
        begin(tally.at[dev[0]], near_all.at[slide], send_n.at[k], recv_n.at[k], dev) for k, dev in enumerate(slides)
    ]
    near_all[slide] = tally[slide]
    loads[2].wait()
    x_copies = []
    for part in range(2):
        cols = slice(part * 384, part * 384 + 384)
        embedded = dot(normed[:TILES, :], w_e[:WIDTH, cols]) + dot(normed[TILES:, :], w_e[WIDTH:, cols])
        o_t[:TILES, cols] = embedded.astype(BF16)
        placed[:, cols] = dot(placing[...], o_t[:TILES, cols]).astype(BF16)
        for k in (7, 8, 6, 9, 5, 10, 4, 11, 3, 12, 2, 13, 1, 14, 0):
            dev = slides[k]
            src = placed.at[pl.ds(pl.multiple_of(dev[0] * CAP, CAP), CAP), cols]
            dst = x.at[pl.ds(pl.multiple_of(slide * CAP, CAP), CAP), cols]
            x_copies.append(begin(src, dst, send_x.at[part, k], recv_x.at[part, k], dev))
    own = pl.ds(pl.multiple_of(slide * CAP, CAP), CAP)
    x[own, :] = placed[own, :]

    for copy in near_copies:
        copy.wait_recv()
    for i in range(16):
        near[i : i + 1, :] = near_all[i][:1]
    far_copies = [begin(near, far.at[seq], send_f.at[k], recv_f.at[k], dev) for k, dev in enumerate(blocks)]
    far[seq] = near[...]
    place_in = lax.broadcasted_iota(jnp.int32, (CAP, 128), 0).astype(F32)
    for i in range(16):
        val[i * CAP : i * CAP + CAP, :] = jnp.where(place_in < near[i : i + 1, :], 1.0, 0.0)
    for t in range(3):
        perm[t] = (lax.broadcasted_iota(jnp.int32, (WIDTH, WIDTH), 0) == place_ref[t][:1, :]).astype(BF16)
    row = lax.broadcasted_iota(jnp.int32, (64, SLOTS), 0)
    filler = jnp.where(row == 0, 1.0, 0.0).astype(BF16)
    zeros = jnp.zeros((64, SLOTS), BF16)
    q_0[64:, :], q_1[:64, :] = filler, filler
    do_0[64:, :], do_1[:64, :] = zeros, zeros
    for copy in loads[3:]:
        copy.wait()
    mg_val = val[:SLOTS, :].astype(BF16)
    for c in range(6):
        cols = slice(c * 128, c * 128 + 128)
        mg[:, cols] = mg[:, cols] * mg_val

    @pl.loop(0, 3)
    def _(c):
        cols = pl.ds(pl.multiple_of(c * BLOCK, BLOCK), BLOCK)
        d_heads = lax.dot_general(mg[...], wout[cols, :], NT, preferred_element_type=F32).astype(BF16)
        do_tok[:, cols] = d_heads
        do_t[cols, :] = d_heads.T

    row = lax.broadcasted_iota(jnp.int32, (96, SLOTS), 0)
    pick = lax.broadcasted_iota(jnp.int32, (96, SLOTS), 1) == (row % 16) * CAP + (row // 16) * RATE
    pick = pick.astype(BF16)
    for copy in x_copies:
        copy.wait_recv()
    rows = dot(pick, x[...]).astype(BF16)
    for m in range(6):
        own_far[m] = rows[m * 16 : m * 16 + 16]

    up = (slide, lax.rem(z + 1, SIDE) * 2 + core)
    down = (slide, lax.rem(z + 3, SIDE) * 2 + core)
    across = lax.rem(z + 2, SIDE) * 2 + core
    to_up = begin(own_far, xd.at[:, seq], send_z.at[0], recv_z.at[0], up)
    to_down = begin(own_far, xd.at[:, seq], send_z.at[1], recv_z.at[1], down)
    to_side = [begin(own_far, xd.at[:, seq], send_s.at[0], recv_s.at[0], sibling)]
    xd[:, seq] = own_far[...]

    def project(first, rows_of):
        @pl.loop(0, 3)
        def _(c):
            cols = pl.ds(pl.multiple_of(c * BLOCK, BLOCK), BLOCK)
            x_t[cols, first : first + SLOTS] = rows_of(cols).T
            for w, tok, turned in ((w_k, k_tok, k_t), (w_v, v_tok, v_t)):
                part = dot(rows_of(slice(None)), w[:, cols]).astype(BF16)
                tok[first : first + SLOTS, cols] = part
                turned[cols, first : first + SLOTS] = part.T

    @pl.loop(0, 3)
    def _(c):
        cols = pl.ds(pl.multiple_of(c * BLOCK, BLOCK), BLOCK)
        query = dot(x[...], w_q[:, cols]).astype(BF16) * BF16(0.125)
        q_tok[:, cols] = query
        q_t[cols, :] = query.T

    to_up.wait_recv()
    relay_up = begin(xd.at[pl.ds(0, 3), down[1]], xd.at[pl.ds(0, 3), down[1]], send_z.at[2], recv_z.at[2], up)
    to_side.append(begin(xd.at[:, down[1]], xd.at[:, down[1]], send_s.at[1], recv_s.at[1], sibling))
    to_down.wait_recv()
    relay_down = begin(xd.at[pl.ds(3, 3), up[1]], xd.at[pl.ds(3, 3), up[1]], send_z.at[3], recv_z.at[3], down)
    to_side.append(begin(xd.at[:, up[1]], xd.at[:, up[1]], send_s.at[2], recv_s.at[2], sibling))

    project(0, lambda cols: x[:, cols])

    relay_up.wait_recv()
    relay_down.wait_recv()
    to_side.append(begin(xd.at[:, across], xd.at[:, across], send_s.at[3], recv_s.at[3], sibling))
    for copy in far_copies:
        copy.wait_recv()
    for m in range(6):
        for j in range(8):
            first = SLOTS + m * 128 + j * 16
            val[first : first + 16, :] = jnp.where(far[j] > m * RATE, 1.0, 0.0)
    bias[...] = jnp.where(val[...] > 0.5, 0.0, MASKED).astype(BF16)
    for copy in to_side:
        copy.wait_recv()

    project(SLOTS, lambda cols: xd[:, :, :, cols].reshape(SLOTS, WIDTH if isinstance(cols, slice) else BLOCK))

    for copy in to_side + far_copies + near_copies + x_copies + [to_up, to_down, relay_up, relay_down]:
        copy.wait_send()

    def close_keys(pair, a, which, third):
        rows = slice(third * PART, third * PART + PART)
        mine = lax.broadcasted_iota(jnp.int32, (PART, 128), 1) // 64 == a
        slot = lax.rem(pair // 2, 2)
        left, right, offset = ((prob[a], do_cat[a], BLOCK), (grad[a], q_cat[a], 0))[which]
        lanes = pl.ds(pl.multiple_of(lax.rem(pair, 2) * 128 + offset, 128), 128)
        part = dot(left[rows, :], right[...]).astype(BF16)
        dkv[slot, rows, lanes] = jnp.where(mine, part, dkv[slot, rows, lanes])

    own_half = pl.multiple_of(core * 384, 384)
    its_half = pl.multiple_of((1 - core) * 384, 384)

    def parity(r):
        return r % 2 if isinstance(r, int) else lax.rem(r, 2)

    def axis_copies(r, t, axis, source, landing, send, recv, height):
        copies = []
        for d in (2, 1, 3):
            moved = dict(at)
            moved[axis] = lax.rem(at[axis] + d, SIDE)
            device = (moved["y"] * SIDE + moved["x"], moved["z"] * 2 + core)
            if height:
                src = source.at[r, t, pl.ds(pl.multiple_of(moved[axis] * height, height), height), :]
            else:
                src = source.at[r, t, moved[axis]]
            copies.append(remote(src, landing.at[r, t, d - 1], send.at[r, t, d - 1], recv.at[r, t, d - 1], device))
        return copies

    def pair_copy(r, t):
        src = g.at[parity(r), t, pl.ds(its_half, 384), :]
        return remote(src, half.at[r, t], send0.at[r, t], recv0.at[r, t], sibling)

    def a_copies(r, t):
        return axis_copies(r, t, ORDERS[t][0], pair_sum, from_a, send_a, recv_a, 96)

    def b_copies(r, t):
        return axis_copies(r, t, ORDERS[t][1], owned, from_b, send_b, recv_b, 24)

    def c_copies(r, t):
        return axis_copies(r, t, ORDERS[t][2], spread, from_c, send_c, recv_c, 0)

    def stage_pair(r, parts):
        for t in range(3):
            g[parity(r), t] = dot(perm[t], parts(t).astype(BF16)).astype(BF16)
            pair_copy(r, t).start()

    def stage_qkv(r):
        slot = parity(r)

        def parts(t):
            if t == 0:
                return dot(x_t[:, :SLOTS], dq_round[slot])
            return dot(x_t[...], dkv[slot, :, (t - 1) * BLOCK : t * BLOCK])

        stage_pair(r, parts)

    def stage_a(r):
        for t in range(3):
            copy = pair_copy(r, t)
            copy.wait_recv()
            mine = g[parity(r), t, pl.ds(own_half, 384), :].astype(F32)
            pair_sum[r, t] = (mine + half[r, t].astype(F32)).astype(BF16)
            for copy in a_copies(r, t):
                copy.start()

    def stage_b(r):
        for t in range(3):
            mine = pl.multiple_of(at[ORDERS[t][0]] * 96, 96)
            total = g[parity(r), t, pl.ds(pl.multiple_of(own_half + mine, 96), 96), :].astype(F32)
            total = total + half[r, t, pl.ds(mine, 96), :].astype(F32)
            for copy in a_copies(r, t):
                copy.wait_recv()
            for d in range(3):
                total = total + from_a[r, t, d].astype(F32)
            owned[r, t] = total
            for copy in b_copies(r, t):
                copy.start()

    def stage_c(r):
        for t in range(3):
            total = owned[r, t, pl.ds(pl.multiple_of(at[ORDERS[t][1]] * 24, 24), 24), :]
            for copy in b_copies(r, t):
                copy.wait_recv()
            for d in range(3):
                total = total + from_b[r, t, d]
            for c in range(SIDE):
                spread[r, t, c, :6, :] = total[c * 6 : c * 6 + 6]
                spread[r, t, c, 6:, :] = jnp.zeros((2, BLOCK), F32)
            for copy in c_copies(r, t):
                copy.start()

    def stage_out(r):
        for t in range(3):
            total = spread[r, t, at[ORDERS[t][2]]]
            for copy in c_copies(r, t):
                copy.wait_recv()
            for d in range(3):
                total = total + from_c[r, t, d]
            total = total[:6] * factor
            if r < 3:
                first = t * WIDTH + r * BLOCK
                oq_ref[:, first : first + BLOCK] = total
            else:
                oo_ref[:, t * BLOCK : t * BLOCK + BLOCK] = total

    def sent(r):
        for t in range(3):
            for copy in a_copies(r, t) + b_copies(r, t) + c_copies(r, t):
                copy.wait_send()

    @pl.loop(0, HEADS // 2)
    def _(pair):
        lanes = pl.ds(pl.multiple_of(pair * 128, 128), 128)
        before = lax.max(pair - 1, 0)
        done = lax.max(pair // 2 - 1, 0)
        lane = lax.broadcasted_iota(jnp.int32, (KEYS, 128), 1)
        lane_q = lax.broadcasted_iota(jnp.int32, (SLOTS, 128), 1)
        nothing = jnp.zeros((SLOTS, 128), BF16)

        def head_rows(a):
            return pl.ds(pl.multiple_of(pair * 128 + a * 64, 64), 64)

        def open_head(a):
            own = slice(a * 64, a * 64 + 64)
            keys[a][...] = jnp.where(lane // 64 == a, k_tok[:, lanes], bias[...])
            q_rows[a][own, :] = q_t[head_rows(a), :]
            do_rows[a][own, :] = do_t[head_rows(a), :]

        def score_part(step, part):
            a, block = step // 3, step % 3
            rows = slice(part * PART, part * PART + PART)
            s = dot(keys[a][rows, :], q_rows[a][:, block * BLOCK : block * BLOCK + BLOCK])
            scores[step % 2][rows, :] = s
            return jnp.max(s, axis=0, keepdims=True)

        def short(part):
            return [slice(first, first + CHAIN) for first in range(part * PART, part * PART + PART, CHAIN)]

        open_head(0)
        peaks = [score_part(0, part) for part in range(PARTS)]
        open_head(1)
        for step in range(6):
            a, block = step // 3, step % 3
            cols = slice(block * BLOCK, block * BLOCK + BLOCK)
            score = scores[step % 2]
            closing = (before if a == 0 else pair, 1 - a)
            peak = functools.reduce(jnp.maximum, peaks)
            peaks, total = [], jnp.zeros((8, BLOCK), F32)
            for part in range(PARTS):
                if step < 5:
                    peaks.append(score_part(step + 1, part))
                for rows in short(part):
                    raw = jnp.exp(score[rows, :] - peak)
                    score[rows, :] = raw
                    total = total + jnp.sum(raw.reshape(CHAIN // 8, 8, BLOCK), axis=0)
                if part == 1:
                    close_keys(*closing, 0, block)
            inverse = 1.0 / jnp.sum(total, axis=0, keepdims=True)
            out = 0.0
            for part in range(PARTS):
                keys_of = slice(part * PART, part * PART + PART)
                for rows in short(part):
                    prob[a][rows, cols] = (score[rows, :] * inverse).astype(BF16)
                grad_p[keys_of, :] = dot(v_tok[keys_of, lanes], do_rows[a][:, cols])
                out = out + dot(v_t[head_rows(a), keys_of], prob[a][keys_of, cols])
            out = out.astype(BF16)
            o_t[head_rows(a), cols] = out
            delta = jnp.sum(do_t[head_rows(a), cols].astype(F32) * out.astype(F32), axis=0, keepdims=True)
            d_query = 0.0
            for part in range(PARTS):
                keys_of = slice(part * PART, part * PART + PART)
                for rows in short(part):
                    grad[a][rows, cols] = (score[rows, :] * ((grad_p[rows, :] - delta) * inverse)).astype(BF16)
                if part == 1:
                    close_keys(*closing, 1, block)
                d_query = d_query + dot(k_t[head_rows(a), keys_of], grad[a][keys_of, cols])
            dq_t[a * 64 : a * 64 + 64, cols] = (d_query * 0.125).astype(BF16)
            if step == 2:
                @pl.when((pair == 2) | (pair == 4))
                def _():
                    stage_qkv(done)

                @pl.when((pair == 3) | (pair == 5))
                def _():
                    stage_b(done)

                @pl.when(pair == 4)
                def _():
                    stage_out(0)

            if block == 2:
                half_lanes = lane_q // 64 == a
                q_cat[a][...] = jnp.where(half_lanes, q_tok[:, lanes], nothing)
                do_cat[a][...] = jnp.where(half_lanes, do_tok[:, lanes], nothing)
        dq_round[lax.rem(pair // 2, 2), :, pl.ds(pl.multiple_of(lax.rem(pair, 2) * 128, 128), 128)] = dq_t[...].T

        @pl.when((pair == 2) | (pair == 4))
        def _():
            stage_a(done)

        @pl.when((pair == 3) | (pair == 5))
        def _():
            stage_c(done)

    for third in range(3):
        for which in range(2):
            close_keys(HEADS // 2 - 1, 1, which, third)
    for t in range(3):
        pair_copy(0, t).wait_send()
    stage_qkv(2)
    for t in range(3):
        pair_copy(1, t).wait_send()
    stage_pair(3, lambda t: dot(o_t[...], mg[:, t * BLOCK : t * BLOCK + BLOCK]))
    stage_a(2)
    do_tok[...] = o_t[...].T
    stage_a(3)

    @pl.loop(0, 3)
    def _(c):
        cols = pl.ds(pl.multiple_of(c * BLOCK, BLOCK), BLOCK)
        mixed = x[:, cols].astype(F32) + dot(do_tok[...], wout[:, cols])
        q_tok[:, cols] = (mixed * val[:SLOTS, :1]).astype(BF16)

    store = pltpu.make_async_copy(q_tok, att_ref, load.at[0])
    store.start()
    stage_out(1)
    for stage in (stage_b, stage_c, stage_out):
        stage(2)
        stage(3)
    for r in range(4):
        sent(r)
    for r in (2, 3):
        for t in range(3):
            pair_copy(r, t).wait_send()
    store.wait()


def whole(feats, gain, w_embed, target, cot, w_qkv, w_out, factor):
    tall, wide, square = (KEYS, WIDTH), (WIDTH, KEYS), (SLOTS, WIDTH)
    vmem, anywhere = pl.BlockSpec(memory_space=pltpu.VMEM), pl.BlockSpec(memory_space=pl.ANY)
    dma = pltpu.SemaphoreType.DMA
    half16 = lambda *shapes: [pltpu.VMEM(shape, BF16) for shape in shapes]
    full32 = lambda *shapes: [pltpu.VMEM(shape, F32) for shape in shapes]
    scratch = half16(square, (6, 8, 16, WIDTH)) + full32((KEYS, 128)) + half16((KEYS, 128))
    scratch += half16(square, tall, tall, square, square, wide, wide, square, wide, square, square, square)
    scratch += half16((128, SLOTS), (2, SLOTS, BLOCK), (2, KEYS, 2 * BLOCK))
    scratch += full32((KEYS, BLOCK), (KEYS, BLOCK), (KEYS, BLOCK)) + half16(tall, tall, tall, tall)
    scratch += half16(*[(KEYS, 128)] * 2, *[(128, SLOTS)] * 4, *[(SLOTS, 128)] * 4, (3, WIDTH, WIDTH))
    scratch += full32((16, 8, 128), (16, 8, 128), (16, 128), (8, 16, 128)) + half16((6, 16, WIDTH))
    scratch += half16((2, 3, WIDTH, BLOCK), (4, 3, 384, BLOCK), (4, 3, 384, BLOCK), (4, 3, 3, 96, BLOCK))
    scratch += full32((4, 3, 96, BLOCK), (4, 3, 3, 24, BLOCK), (4, 3, SIDE, 8, BLOCK), (4, 3, 3, 8, BLOCK))
    scratch += [dma((8,)), dma((2, 15)), dma((2, 15)), dma((15,)), dma((15,)), dma((7,)), dma((7,))]
    scratch += [dma((4,))] * 4 + [dma((4, 3))] * 2 + [dma((4, 3, 3))] * 6
    return pl.pallas_call(
        functools.partial(whole_kernel, factor),
        out_shape=(
            jax.ShapeDtypeStruct(square, BF16),
            jax.ShapeDtypeStruct((6, 3 * WIDTH), F32),
            jax.ShapeDtypeStruct((6, WIDTH), F32),
        ),
        in_specs=[anywhere, vmem, anywhere, vmem, anywhere, anywhere, anywhere, vmem],
        out_specs=(anywhere, vmem, vmem),
        scratch_shapes=scratch,
        compiler_params=pltpu.CompilerParams(
            collective_id=1, has_side_effects=True, vmem_limit_bytes=63 * 1024 * 1024
        ),
        cost_estimate=pl.CostEstimate(flops=30_000_000_000, bytes_accessed=16_000_000, transcendentals=14_000_000),
        name="whole",
    )(feats, gain, w_embed, target, cot, w_qkv, w_out, jnp.asarray(row_orders()))


def hand_over_kernel(*refs):
    ins, outs, held, sem_in, sem_out = refs[:3], refs[3:6], refs[6:9], refs[9], refs[10]
    pieces = [(0, slice(first, first + 192)) for first in range(0, SLOTS, 192)] + [(1, slice(0, 6)), (2, slice(0, 6))]
    arriving, leaving = [], []
    for n, (which, rows) in enumerate(pieces):
        arriving.append(pltpu.make_async_copy(ins[which].at[rows], held[which].at[rows], sem_in.at[n]))
        leaving.append(pltpu.make_async_copy(held[which].at[rows], outs[which].at[rows], sem_out.at[n]))
    for copy in arriving:
        copy.start()
    for first, second in zip(arriving, leaving):
        first.wait()
        second.start()
    for copy in leaving:
        copy.wait()


def hand_over(*arrays):
    anywhere = pl.BlockSpec(memory_space=pl.ANY)
    return pl.pallas_call(
        hand_over_kernel,
        out_shape=tuple(jax.ShapeDtypeStruct(a.shape, a.dtype) for a in arrays),
        in_specs=[anywhere] * 3,
        out_specs=(anywhere,) * 3,
        scratch_shapes=[pltpu.VMEM(a.shape, a.dtype) for a in arrays] + [pltpu.SemaphoreType.DMA((6,))] * 2,
        compiler_params=pltpu.CompilerParams(vmem_limit_bytes=63 * 1024 * 1024),
        name="hand_over",
    )(*arrays)


def shards(tile_feats, norm_gain, w_embed, slide_of_tile, w_qkv, w_out, cotangent):
    factor = (lax.axis_size("slide") * lax.axis_size("seq") * SLOTS) ** (-0.5)
    output, grad_qkv, grad_out = hand_over(*whole(
        tile_feats, norm_gain, w_embed, slide_of_tile.reshape(1, TILES),
        cotangent[0], w_qkv, w_out, factor,
    ))
    return (output[None], grad_qkv, grad_out)


def solution(mesh):
    return jax.shard_map(
        shards,
        mesh=mesh,
        in_specs=(
            P(("slide", "seq"), None),
            P(),
            P(),
            P(("slide", "seq"), None),
            P(),
            P(),
            P("slide", "seq", None),
        ),
        out_specs=(P("slide", "seq", None), P(("slide", "seq"), None), P(("slide", "seq"), None)),
        check_vma=False,
    )
```

```python
import functools

import jax
import jax.numpy as jnp
import numpy as np
from jax import lax
from jax.experimental import pallas as pl
from jax.experimental.pallas import tpu as pltpu
from jax.sharding import PartitionSpec as P

HEADS = 12
CAP = 48
RATE = 8
WIDTH = 768
WIDE = 1536
TILES = 384
SLOTS = 768
KEYS = 1536
BLOCK = 256
PART = 512
CHAIN = 64
PARTS = KEYS // PART
SIDE = 4
MASKED = -1e30
BF16 = jnp.bfloat16
F32 = jnp.float32
MESH = pl.DeviceIdType.MESH
ORDERS = (("x", "y", "z"), ("y", "z", "x"), ("z", "x", "y"))
NT = (((1,), (1,)), ((), ()))
TN = (((0,), (0,)), ((), ()))


def row_orders():
    feature = np.arange(WIDTH)
    device, inner = feature // 6, feature % 6
    at = {"core": device % 2, "z": device // 2 % 4, "x": device // 8 % 4, "y": device // 32}
    places = [
        at["core"] * 384 + at[a] * 96 + at[b] * 24 + at[c] * 6 + inner for a, b, c in ORDERS
    ]
    return np.broadcast_to(np.stack(places)[:, None, :], (3, 8, WIDTH)).astype(np.int32)


def dot(a, b):
    return jnp.dot(a, b, preferred_element_type=F32)


def whole_kernel(
    factor,
    feats_ref, gain_ref, we_ref, target_ref, cot_ref, wqkv_ref, wout_ref, place_ref,
    att_ref, oq_ref, oo_ref,
    x, xd, val, bias, q_tok, k_tok, v_tok, do_tok, q_t, do_t, x_t, mg, o_t, wout,
    dq_round, dkv, score_0, score_1, grad_p, prob_0, prob_1, grad_0, grad_1,
    key_0, key_1, q_0, q_1, do_0, do_1, qc_0, qc_1, dc_0, dc_1, perm,
    tally, near_all, near, far, own_far,
    g, half, pair_sum, from_a, owned, from_b, spread, from_c,
    load, send_x, recv_x, send_n, recv_n, send_f, recv_f, send_z, recv_z, send_s, recv_s,
    send0, recv0, send_a, recv_a, send_b, recv_b, send_c, recv_c,
):
    scores, prob, grad = (score_0, score_1), (prob_0, prob_1), (grad_0, grad_1)
    keys, q_rows, do_rows = (key_0, key_1), (q_0, q_1), (do_0, do_1)
    q_cat, do_cat = (qc_0, qc_1), (dc_0, dc_1)
    slide, seq = lax.axis_index("slide"), lax.axis_index("seq")
    at = {"y": slide // SIDE, "x": slide % SIDE, "z": seq // 2}
    z, core = at["z"], seq % 2
    sibling = (slide, z * 2 + 1 - core)
    slides = [(lax.rem(slide + k, 16), seq) for k in range(1, 16)]
    blocks = [(slide, lax.rem(seq + k, 8)) for k in range(1, 8)]

    barrier = pltpu.get_barrier_semaphore()
    for device in slides + blocks:
        pl.semaphore_signal(barrier, inc=1, device_id=device, device_id_type=MESH)

    def remote(src, dst, send, recv, device):
        return pltpu.make_async_remote_copy(
            src_ref=src, dst_ref=dst, send_sem=send, recv_sem=recv, device_id=device, device_id_type=MESH
        )

    def begin(*args):
        copy = remote(*args)
        copy.start()
        return copy

    feats, normed, placed, w_e, w_q, w_k, w_v = (
        grad_0.at[:SLOTS], grad_1.at[:SLOTS], grad_1.at[SLOTS:], prob_1,
        prob_0.at[:SLOTS], prob_0.at[SLOTS:], grad_0.at[SLOTS:],
    )
    sources = [
        (feats_ref.at[:, :WIDTH], feats.at[:TILES]), (feats_ref.at[:, WIDTH:], feats.at[TILES:]),
        (we_ref, w_e), (cot_ref, mg), (wout_ref, wout),
        (wqkv_ref.at[:, :WIDTH], w_q), (wqkv_ref.at[:, WIDTH : 2 * WIDTH], w_k), (wqkv_ref.at[:, 2 * WIDTH :], w_v),
    ]
    loads = [pltpu.make_async_copy(src, dst, load.at[n]) for n, (src, dst) in enumerate(sources)]
    for copy in loads:
        copy.start()

    target = target_ref[...]
    named = lax.broadcasted_iota(jnp.int32, (16, TILES), 0) == target
    one_hot = jnp.where(named, 1.0, 0.0)
    earlier = (
        lax.broadcasted_iota(jnp.int32, (TILES, TILES), 0) < lax.broadcasted_iota(jnp.int32, (TILES, TILES), 1)
    ).astype(BF16)
    before_it = dot(one_hot.astype(BF16), earlier)
    rank = jnp.sum(one_hot * before_it, axis=0, keepdims=True)
    slot = target * CAP + rank.astype(jnp.int32)
    placing = x_t.at[:, :TILES]
    placing[...] = (lax.broadcasted_iota(jnp.int32, (SLOTS, TILES), 0) == slot).astype(BF16)
    total = jnp.sum(one_hot, axis=1, keepdims=True)
    for d in range(16):
        tally[d] = jnp.broadcast_to(total[d : d + 1], (8, 128))
    loads[0].wait()
    loads[1].wait()

    @pl.loop(0, 4)
    def _(c):
        low = pl.ds(pl.multiple_of(c * 96, 96), 96)
        high = pl.ds(pl.multiple_of(c * 96 + TILES, 96), 96)
        values = [feats[low, :].astype(F32), feats[high, :].astype(F32)]
        center = sum(jnp.sum(v, axis=-1, keepdims=True) for v in values) * (1.0 / WIDE)
        moved = [v - center for v in values]
        spread_sq = sum(jnp.sum(v * v, axis=-1, keepdims=True) for v in moved) * (1.0 / WIDE)
        scale = lax.rsqrt(spread_sq + 1e-06)
        normed[low, :] = (moved[0] * scale * gain_ref[:WIDTH].reshape(1, WIDTH)).astype(BF16)
        normed[high, :] = (moved[1] * scale * gain_ref[WIDTH:].reshape(1, WIDTH)).astype(BF16)

    pl.semaphore_wait(barrier, 22)
    near_copies = [
        begin(tally.at[dev[0]], near_all.at[slide], send_n.at[k], recv_n.at[k], dev) for k, dev in enumerate(slides)
    ]
    near_all[slide] = tally[slide]
    loads[2].wait()
    x_copies = []
    for part in range(2):
        cols = slice(part * 384, part * 384 + 384)
        embedded = dot(normed[:TILES, :], w_e[:WIDTH, cols]) + dot(normed[TILES:, :], w_e[WIDTH:, cols])
        o_t[:TILES, cols] = embedded.astype(BF16)
        placed[:, cols] = dot(placing[...], o_t[:TILES, cols]).astype(BF16)
        for k in (7, 8, 6, 9, 5, 10, 4, 11, 3, 12, 2, 13, 1, 14, 0):
            dev = slides[k]
            src = placed.at[pl.ds(pl.multiple_of(dev[0] * CAP, CAP), CAP), cols]
            dst = x.at[pl.ds(pl.multiple_of(slide * CAP, CAP), CAP), cols]
            x_copies.append(begin(src, dst, send_x.at[part, k], recv_x.at[part, k], dev))
    own = pl.ds(pl.multiple_of(slide * CAP, CAP), CAP)
    x[own, :] = placed[own, :]

    for copy in near_copies:
        copy.wait_recv()
    for i in range(16):
        near[i : i + 1, :] = near_all[i][:1]
    far_copies = [begin(near, far.at[seq], send_f.at[k], recv_f.at[k], dev) for k, dev in enumerate(blocks)]
    far[seq] = near[...]
    place_in = lax.broadcasted_iota(jnp.int32, (CAP, 128), 0).astype(F32)
    for i in range(16):
        val[i * CAP : i * CAP + CAP, :] = jnp.where(place_in < near[i : i + 1, :], 1.0, 0.0)
    for t in range(3):
        perm[t] = (lax.broadcasted_iota(jnp.int32, (WIDTH, WIDTH), 0) == place_ref[t][:1, :]).astype(BF16)
    row = lax.broadcasted_iota(jnp.int32, (64, SLOTS), 0)
    filler = jnp.where(row == 0, 1.0, 0.0).astype(BF16)
    zeros = jnp.zeros((64, SLOTS), BF16)
    q_0[64:, :], q_1[:64, :] = filler, filler
    do_0[64:, :], do_1[:64, :] = zeros, zeros
    for copy in loads[3:]:
        copy.wait()
    mg_val = val[:SLOTS, :].astype(BF16)
    for c in range(6):
        cols = slice(c * 128, c * 128 + 128)
        mg[:, cols] = mg[:, cols] * mg_val

    @pl.loop(0, 3)
    def _(c):
        cols = pl.ds(pl.multiple_of(c * BLOCK, BLOCK), BLOCK)
        d_heads = lax.dot_general(mg[...], wout[cols, :], NT, preferred_element_type=F32).astype(BF16)
        do_tok[:, cols] = d_heads
        do_t[cols, :] = d_heads.T

    row = lax.broadcasted_iota(jnp.int32, (96, SLOTS), 0)
    pick = lax.broadcasted_iota(jnp.int32, (96, SLOTS), 1) == (row % 16) * CAP + (row // 16) * RATE
    pick = pick.astype(BF16)
    for copy in x_copies:
        copy.wait_recv()
    rows = dot(pick, x[...]).astype(BF16)
    for m in range(6):
        own_far[m] = rows[m * 16 : m * 16 + 16]

    up = (slide, lax.rem(z + 1, SIDE) * 2 + core)
    down = (slide, lax.rem(z + 3, SIDE) * 2 + core)
    across = lax.rem(z + 2, SIDE) * 2 + core
    to_up = begin(own_far, xd.at[:, seq], send_z.at[0], recv_z.at[0], up)
    to_down = begin(own_far, xd.at[:, seq], send_z.at[1], recv_z.at[1], down)
    to_side = [begin(own_far, xd.at[:, seq], send_s.at[0], recv_s.at[0], sibling)]
    xd[:, seq] = own_far[...]

    def project(first, rows_of):
        @pl.loop(0, 3)
        def _(c):
            cols = pl.ds(pl.multiple_of(c * BLOCK, BLOCK), BLOCK)
            x_t[cols, first : first + SLOTS] = rows_of(cols).T
            for w, tok in ((w_k, k_tok), (w_v, v_tok)):
                part = dot(rows_of(slice(None)), w[:, cols]).astype(BF16)
                tok[first : first + SLOTS, cols] = part

    @pl.loop(0, 3)
    def _(c):
        cols = pl.ds(pl.multiple_of(c * BLOCK, BLOCK), BLOCK)
        query = dot(x[...], w_q[:, cols]).astype(BF16) * BF16(0.125)
        q_tok[:, cols] = query
        q_t[cols, :] = query.T

    to_up.wait_recv()
    relay_up = begin(xd.at[pl.ds(0, 3), down[1]], xd.at[pl.ds(0, 3), down[1]], send_z.at[2], recv_z.at[2], up)
    to_side.append(begin(xd.at[:, down[1]], xd.at[:, down[1]], send_s.at[1], recv_s.at[1], sibling))
    to_down.wait_recv()
    relay_down = begin(xd.at[pl.ds(3, 3), up[1]], xd.at[pl.ds(3, 3), up[1]], send_z.at[3], recv_z.at[3], down)
    to_side.append(begin(xd.at[:, up[1]], xd.at[:, up[1]], send_s.at[2], recv_s.at[2], sibling))

    project(0, lambda cols: x[:, cols])

    relay_up.wait_recv()
    relay_down.wait_recv()
    to_side.append(begin(xd.at[:, across], xd.at[:, across], send_s.at[3], recv_s.at[3], sibling))
    for copy in far_copies:
        copy.wait_recv()
    for m in range(6):
        for j in range(8):
            first = SLOTS + m * 128 + j * 16
            val[first : first + 16, :] = jnp.where(far[j] > m * RATE, 1.0, 0.0)
    bias[...] = jnp.where(val[...] > 0.5, 0.0, MASKED).astype(BF16)
    for copy in to_side:
        copy.wait_recv()

    project(SLOTS, lambda cols: xd[:, :, :, cols].reshape(SLOTS, WIDTH if isinstance(cols, slice) else BLOCK))

    for copy in to_side + far_copies + near_copies + x_copies + [to_up, to_down, relay_up, relay_down]:
        copy.wait_send()

    def close_keys(pair, a, third):
        rows = slice(third * PART, third * PART + PART)
        mine = lax.broadcasted_iota(jnp.int32, (PART, 128), 1) // 64 == a
        slot = lax.rem(pair // 2, 2)
        for offset, left, right in ((0, grad[a], q_cat[a]), (BLOCK, prob[a], do_cat[a])):
            lanes = pl.ds(pl.multiple_of(lax.rem(pair, 2) * 128 + offset, 128), 128)
            part = dot(left[rows, :], right[...]).astype(BF16)
            dkv[slot, rows, lanes] = jnp.where(mine, part, dkv[slot, rows, lanes])

    own_half = pl.multiple_of(core * 384, 384)
    its_half = pl.multiple_of((1 - core) * 384, 384)

    def parity(r):
        return r % 2 if isinstance(r, int) else lax.rem(r, 2)

    def axis_copies(r, t, axis, source, landing, send, recv, height):
        copies = []
        for d in (2, 1, 3):
            moved = dict(at)
            moved[axis] = lax.rem(at[axis] + d, SIDE)
            device = (moved["y"] * SIDE + moved["x"], moved["z"] * 2 + core)
            if height:
                src = source.at[r, t, pl.ds(pl.multiple_of(moved[axis] * height, height), height), :]
            else:
                src = source.at[r, t, moved[axis]]
            copies.append(remote(src, landing.at[r, t, d - 1], send.at[r, t, d - 1], recv.at[r, t, d - 1], device))
        return copies

    def pair_copy(r, t):
        src = g.at[parity(r), t, pl.ds(its_half, 384), :]
        return remote(src, half.at[r, t], send0.at[r, t], recv0.at[r, t], sibling)

    def a_copies(r, t):
        return axis_copies(r, t, ORDERS[t][0], pair_sum, from_a, send_a, recv_a, 96)

    def b_copies(r, t):
        return axis_copies(r, t, ORDERS[t][1], owned, from_b, send_b, recv_b, 24)

    def c_copies(r, t):
        return axis_copies(r, t, ORDERS[t][2], spread, from_c, send_c, recv_c, 0)

    def stage_pair(r, parts):
        for t in range(3):
            g[parity(r), t] = dot(perm[t], parts(t).astype(BF16)).astype(BF16)
            pair_copy(r, t).start()

    def stage_qkv(r):
        slot = parity(r)

        def parts(t):
            if t == 0:
                return dot(x_t[:, :SLOTS], dq_round[slot])
            return dot(x_t[...], dkv[slot, :, (t - 1) * BLOCK : t * BLOCK])

        stage_pair(r, parts)

    def stage_a(r):
        for t in range(3):
            copy = pair_copy(r, t)
            copy.wait_recv()
            mine = g[parity(r), t, pl.ds(own_half, 384), :].astype(F32)
            pair_sum[r, t] = (mine + half[r, t].astype(F32)).astype(BF16)
            for copy in a_copies(r, t):
                copy.start()

    def stage_b(r):
        for t in range(3):
            mine = pl.multiple_of(at[ORDERS[t][0]] * 96, 96)
            total = g[parity(r), t, pl.ds(pl.multiple_of(own_half + mine, 96), 96), :].astype(F32)
            total = total + half[r, t, pl.ds(mine, 96), :].astype(F32)
            for copy in a_copies(r, t):
                copy.wait_recv()
            for d in range(3):
                total = total + from_a[r, t, d].astype(F32)
            owned[r, t] = total
            for copy in b_copies(r, t):
                copy.start()

    def stage_c(r):
        for t in range(3):
            total = owned[r, t, pl.ds(pl.multiple_of(at[ORDERS[t][1]] * 24, 24), 24), :]
            for copy in b_copies(r, t):
                copy.wait_recv()
            for d in range(3):
                total = total + from_b[r, t, d]
            for c in range(SIDE):
                spread[r, t, c, :6, :] = total[c * 6 : c * 6 + 6]
                spread[r, t, c, 6:, :] = jnp.zeros((2, BLOCK), F32)
            for copy in c_copies(r, t):
                copy.start()

    def stage_out(r):
        for t in range(3):
            total = spread[r, t, at[ORDERS[t][2]]]
            for copy in c_copies(r, t):
                copy.wait_recv()
            for d in range(3):
                total = total + from_c[r, t, d]
            total = total[:6] * factor
            if r < 3:
                first = t * WIDTH + r * BLOCK
                oq_ref[:, first : first + BLOCK] = total
            else:
                oo_ref[:, t * BLOCK : t * BLOCK + BLOCK] = total

    def sent(r):
        for t in range(3):
            for copy in a_copies(r, t) + b_copies(r, t) + c_copies(r, t):
                copy.wait_send()

    @pl.loop(0, HEADS // 2)
    def _(pair):
        lanes = pl.ds(pl.multiple_of(pair * 128, 128), 128)
        before = lax.max(pair - 1, 0)
        done = lax.max(pair // 2 - 1, 0)
        lane = lax.broadcasted_iota(jnp.int32, (KEYS, 128), 1)
        lane_q = lax.broadcasted_iota(jnp.int32, (SLOTS, 128), 1)
        nothing = jnp.zeros((SLOTS, 128), BF16)
        q_slot, q_lanes = lax.rem(pair // 2, 2), pl.ds(pl.multiple_of(lax.rem(pair, 2) * 128, 128), 128)

        def head_rows(a):
            return pl.ds(pl.multiple_of(pair * 128 + a * 64, 64), 64)

        def open_head(a):
            own = slice(a * 64, a * 64 + 64)
            keys[a][...] = jnp.where(lane // 64 == a, k_tok[:, lanes], bias[...])
            q_rows[a][own, :] = q_t[head_rows(a), :]
            do_rows[a][own, :] = do_t[head_rows(a), :]

        def score_part(step, part):
            a, block = step // 3, step % 3
            rows = slice(part * PART, part * PART + PART)
            s = dot(keys[a][rows, :], q_rows[a][:, block * BLOCK : block * BLOCK + BLOCK])
            scores[step % 2][rows, :] = s
            return jnp.max(s, axis=0, keepdims=True)

        def short(part):
            return [slice(first, first + CHAIN) for first in range(part * PART, part * PART + PART, CHAIN)]

        open_head(0)
        peaks = [score_part(0, part) for part in range(PARTS)]
        open_head(1)
        for step in range(6):
            a, block = step // 3, step % 3
            cols = slice(block * BLOCK, block * BLOCK + BLOCK)
            score = scores[step % 2]
            peak = functools.reduce(jnp.maximum, peaks)
            peaks, total = [], jnp.zeros((8, BLOCK), F32)
            for part in range(PARTS):
                if step < 5:
                    peaks.append(score_part(step + 1, part))
                for rows in short(part):
                    raw = jnp.exp(score[rows, :] - peak)
                    score[rows, :] = raw
                    total = total + jnp.sum(raw.reshape(CHAIN // 8, 8, BLOCK), axis=0)
            inverse = 1.0 / jnp.sum(total, axis=0, keepdims=True)
            for part in range(PARTS):
                whole_part = slice(part * PART, part * PART + PART)
                grad_p[whole_part, :] = dot(v_tok[whole_part, lanes], do_rows[a][:, cols])
                for rows in short(part):
                    prob[a][rows, cols] = (score[rows, :] * inverse).astype(BF16)
            out = lax.dot_general(prob[a][:, cols], v_tok[:, lanes], TN, preferred_element_type=F32).astype(BF16)
            out = out.T[a * 64 : a * 64 + 64]
            o_t[head_rows(a), cols] = out
            if a == 0:
                close_keys(before, 1, block)
            else:
                close_keys(pair, 0, block)
            delta = jnp.sum(do_t[head_rows(a), cols].astype(F32) * out.astype(F32), axis=0, keepdims=True)
            for part in range(PARTS):
                for rows in short(part):
                    grad[a][rows, cols] = (score[rows, :] * ((grad_p[rows, :] - delta) * inverse)).astype(BF16)
            d_query = lax.dot_general(grad[a][:, cols], k_tok[:, lanes], TN, preferred_element_type=F32) * 0.125
            d_query = jnp.where(lane_q[:BLOCK] // 64 == a, d_query.astype(BF16), dq_round[q_slot, cols, q_lanes])
            dq_round[q_slot, cols, q_lanes] = d_query
            if step == 2:
                @pl.when((pair == 2) | (pair == 4))
                def _():
                    stage_qkv(done)

                @pl.when((pair == 3) | (pair == 5))
                def _():
                    stage_b(done)

                @pl.when(pair == 4)
                def _():
                    stage_out(0)

            if block == 2:
                half_lanes = lane_q // 64 == a
                q_cat[a][...] = jnp.where(half_lanes, q_tok[:, lanes], nothing)
                do_cat[a][...] = jnp.where(half_lanes, do_tok[:, lanes], nothing)
        @pl.when((pair == 2) | (pair == 4))
        def _():
            stage_a(done)

        @pl.when((pair == 3) | (pair == 5))
        def _():
            stage_c(done)

    for third in range(3):
        close_keys(HEADS // 2 - 1, 1, third)
    for t in range(3):
        pair_copy(0, t).wait_send()
    stage_qkv(2)
    for t in range(3):
        pair_copy(1, t).wait_send()
    stage_pair(3, lambda t: dot(o_t[...], mg[:, t * BLOCK : t * BLOCK + BLOCK]))
    stage_a(2)
    do_tok[...] = o_t[...].T
    stage_a(3)

    @pl.loop(0, 3)
    def _(c):
        cols = pl.ds(pl.multiple_of(c * BLOCK, BLOCK), BLOCK)
        mixed = x[:, cols].astype(F32) + dot(do_tok[...], wout[:, cols])
        q_tok[:, cols] = (mixed * val[:SLOTS, :1]).astype(BF16)

    store = pltpu.make_async_copy(q_tok, att_ref, load.at[0])
    store.start()
    stage_out(1)
    for stage in (stage_b, stage_c, stage_out):
        stage(2)
        stage(3)
    for r in range(4):
        sent(r)
    for r in (2, 3):
        for t in range(3):
            pair_copy(r, t).wait_send()
    store.wait()


def whole(feats, gain, w_embed, target, cot, w_qkv, w_out, factor):
    tall, wide, square = (KEYS, WIDTH), (WIDTH, KEYS), (SLOTS, WIDTH)
    vmem, anywhere = pl.BlockSpec(memory_space=pltpu.VMEM), pl.BlockSpec(memory_space=pl.ANY)
    dma = pltpu.SemaphoreType.DMA
    half16 = lambda *shapes: [pltpu.VMEM(shape, BF16) for shape in shapes]
    full32 = lambda *shapes: [pltpu.VMEM(shape, F32) for shape in shapes]
    scratch = half16(square, (6, 8, 16, WIDTH)) + full32((KEYS, 128)) + half16((KEYS, 128))
    scratch += half16(square, tall, tall, square, square, square, wide, square, square, square)
    scratch += half16((2, SLOTS, BLOCK), (2, KEYS, 2 * BLOCK))
    scratch += full32((KEYS, BLOCK), (KEYS, BLOCK), (KEYS, BLOCK)) + half16(tall, tall, tall, tall)
    scratch += half16(*[(KEYS, 128)] * 2, *[(128, SLOTS)] * 4, *[(SLOTS, 128)] * 4, (3, WIDTH, WIDTH))
    scratch += full32((16, 8, 128), (16, 8, 128), (16, 128), (8, 16, 128)) + half16((6, 16, WIDTH))
    scratch += half16((2, 3, WIDTH, BLOCK), (4, 3, 384, BLOCK), (4, 3, 384, BLOCK), (4, 3, 3, 96, BLOCK))
    scratch += full32((4, 3, 96, BLOCK), (4, 3, 3, 24, BLOCK), (4, 3, SIDE, 8, BLOCK), (4, 3, 3, 8, BLOCK))
    scratch += [dma((8,)), dma((2, 15)), dma((2, 15)), dma((15,)), dma((15,)), dma((7,)), dma((7,))]
    scratch += [dma((4,))] * 4 + [dma((4, 3))] * 2 + [dma((4, 3, 3))] * 6
    return pl.pallas_call(
        functools.partial(whole_kernel, factor),
        out_shape=(
            jax.ShapeDtypeStruct(square, BF16),
            jax.ShapeDtypeStruct((6, 3 * WIDTH), F32),
            jax.ShapeDtypeStruct((6, WIDTH), F32),
        ),
        in_specs=[anywhere, vmem, anywhere, vmem, anywhere, anywhere, anywhere, vmem],
        out_specs=(anywhere, vmem, vmem),
        scratch_shapes=scratch,
        compiler_params=pltpu.CompilerParams(
            collective_id=1, has_side_effects=True, vmem_limit_bytes=63 * 1024 * 1024
        ),
        cost_estimate=pl.CostEstimate(flops=30_000_000_000, bytes_accessed=16_000_000, transcendentals=14_000_000),
        name="whole",
    )(feats, gain, w_embed, target, cot, w_qkv, w_out, jnp.asarray(row_orders()))


def hand_over_kernel(*refs):
    ins, outs, held, sem_in, sem_out = refs[:3], refs[3:6], refs[6:9], refs[9], refs[10]
    pieces = [(0, slice(first, first + 192)) for first in range(0, SLOTS, 192)] + [(1, slice(0, 6)), (2, slice(0, 6))]
    arriving, leaving = [], []
    for n, (which, rows) in enumerate(pieces):
        arriving.append(pltpu.make_async_copy(ins[which].at[rows], held[which].at[rows], sem_in.at[n]))
        leaving.append(pltpu.make_async_copy(held[which].at[rows], outs[which].at[rows], sem_out.at[n]))
    for copy in arriving:
        copy.start()
    for first, second in zip(arriving, leaving):
        first.wait()
        second.start()
    for copy in leaving:
        copy.wait()


def hand_over(*arrays):
    anywhere = pl.BlockSpec(memory_space=pl.ANY)
    return pl.pallas_call(
        hand_over_kernel,
        out_shape=tuple(jax.ShapeDtypeStruct(a.shape, a.dtype) for a in arrays),
        in_specs=[anywhere] * 3,
        out_specs=(anywhere,) * 3,
        scratch_shapes=[pltpu.VMEM(a.shape, a.dtype) for a in arrays] + [pltpu.SemaphoreType.DMA((6,))] * 2,
        compiler_params=pltpu.CompilerParams(vmem_limit_bytes=63 * 1024 * 1024),
        name="hand_over",
    )(*arrays)


def shards(tile_feats, norm_gain, w_embed, slide_of_tile, w_qkv, w_out, cotangent):
    factor = (lax.axis_size("slide") * lax.axis_size("seq") * SLOTS) ** (-0.5)
    output, grad_qkv, grad_out = hand_over(*whole(
        tile_feats, norm_gain, w_embed, slide_of_tile.reshape(1, TILES),
        cotangent[0], w_qkv, w_out, factor,
    ))
    return (output[None], grad_qkv, grad_out)


def solution(mesh):
    return jax.shard_map(
        shards,
        mesh=mesh,
        in_specs=(
            P(("slide", "seq"), None),
            P(),
            P(),
            P(("slide", "seq"), None),
            P(),
            P(),
            P("slide", "seq", None),
        ),
        out_specs=(P("slide", "seq", None), P(("slide", "seq"), None), P(("slide", "seq"), None)),
        check_vma=False,
    )
```

```python
import functools

import jax
import jax.numpy as jnp
import numpy as np
from jax import lax
from jax.experimental import pallas as pl
from jax.experimental.pallas import tpu as pltpu
from jax.sharding import PartitionSpec as P

HEADS = 12
CAP = 48
RATE = 8
WIDTH = 768
WIDE = 1536
TILES = 384
SLOTS = 768
KEYS = 1536
BLOCK = 256
PART = 512
CHAIN = 128
PIECES = KEYS // CHAIN
SIDE = 4
MASKED = -1e30
BF16 = jnp.bfloat16
F32 = jnp.float32
MESH = pl.DeviceIdType.MESH
ORDERS = (("x", "y", "z"), ("y", "z", "x"), ("z", "x", "y"))
NT = (((1,), (1,)), ((), ()))


def row_orders():
    feature = np.arange(WIDTH)
    device, inner = feature // 6, feature % 6
    at = {"core": device % 2, "z": device // 2 % 4, "x": device // 8 % 4, "y": device // 32}
    places = [
        at["core"] * 384 + at[a] * 96 + at[b] * 24 + at[c] * 6 + inner for a, b, c in ORDERS
    ]
    return np.broadcast_to(np.stack(places)[:, None, :], (3, 8, WIDTH)).astype(np.int32)


def dot(a, b):
    return jnp.dot(a, b, preferred_element_type=F32)


def whole_kernel(
    factor,
    feats_ref, gain_ref, we_ref, target_ref, cot_ref, wqkv_ref, wout_ref, place_ref,
    att_ref, oq_ref, oo_ref,
    x, xd, val, bias, q_tok, k_tok, v_tok, do_tok, q_t, k_t, v_t, do_t, x_t, mg, o_t, wout,
    dq_t, dq_round, dkv, score_0, score_1, prob_0, prob_1, grad_0, grad_1,
    key_0, key_1, q_0, q_1, do_0, do_1, qc_0, qc_1, dc_0, dc_1, perm,
    tally, near_all, near, far, own_far,
    g, half, pair_sum, from_a, owned, from_b, spread, from_c,
    load, send_x, recv_x, send_n, recv_n, send_f, recv_f, send_z, recv_z, send_s, recv_s,
    send0, recv0, send_a, recv_a, send_b, recv_b, send_c, recv_c,
):
    scores, prob, grad = (score_0, score_1), (prob_0, prob_1), (grad_0, grad_1)
    keys, q_rows, do_rows = (key_0, key_1), (q_0, q_1), (do_0, do_1)
    q_cat, do_cat = (qc_0, qc_1), (dc_0, dc_1)
    slide, seq = lax.axis_index("slide"), lax.axis_index("seq")
    at = {"y": slide // SIDE, "x": slide % SIDE, "z": seq // 2}
    z, core = at["z"], seq % 2
    sibling = (slide, z * 2 + 1 - core)
    slides = [(lax.rem(slide + k, 16), seq) for k in range(1, 16)]
    blocks = [(slide, lax.rem(seq + k, 8)) for k in range(1, 8)]

    barrier = pltpu.get_barrier_semaphore()
    for device in slides + blocks:
        pl.semaphore_signal(barrier, inc=1, device_id=device, device_id_type=MESH)

    def remote(src, dst, send, recv, device):
        return pltpu.make_async_remote_copy(
            src_ref=src, dst_ref=dst, send_sem=send, recv_sem=recv, device_id=device, device_id_type=MESH
        )

    def begin(*args):
        copy = remote(*args)
        copy.start()
        return copy

    feats, normed, placed, w_e, w_q, w_k, w_v = (
        grad_0.at[:SLOTS], grad_1.at[:SLOTS], grad_1.at[SLOTS:], prob_1,
        prob_0.at[:SLOTS], prob_0.at[SLOTS:], grad_0.at[SLOTS:],
    )
    sources = [
        (feats_ref.at[:, :WIDTH], feats.at[:TILES]), (feats_ref.at[:, WIDTH:], feats.at[TILES:]),
        (we_ref, w_e), (cot_ref, mg), (wout_ref, wout),
        (wqkv_ref.at[:, :WIDTH], w_q), (wqkv_ref.at[:, WIDTH : 2 * WIDTH], w_k), (wqkv_ref.at[:, 2 * WIDTH :], w_v),
    ]
    loads = [pltpu.make_async_copy(src, dst, load.at[n]) for n, (src, dst) in enumerate(sources)]
    for copy in loads:
        copy.start()

    target = target_ref[...]
    named = lax.broadcasted_iota(jnp.int32, (16, TILES), 0) == target
    one_hot = jnp.where(named, 1.0, 0.0)
    earlier = (
        lax.broadcasted_iota(jnp.int32, (TILES, TILES), 0) < lax.broadcasted_iota(jnp.int32, (TILES, TILES), 1)
    ).astype(BF16)
    before_it = dot(one_hot.astype(BF16), earlier)
    rank = jnp.sum(one_hot * before_it, axis=0, keepdims=True)
    slot = target * CAP + rank.astype(jnp.int32)
    placing = x_t.at[:, :TILES]
    placing[...] = (lax.broadcasted_iota(jnp.int32, (SLOTS, TILES), 0) == slot).astype(BF16)
    total = jnp.sum(one_hot, axis=1, keepdims=True)
    for d in range(16):
        tally[d] = jnp.broadcast_to(total[d : d + 1], (8, 128))
    loads[0].wait()
    loads[1].wait()

    @pl.loop(0, 4)
    def _(c):
        low = pl.ds(pl.multiple_of(c * 96, 96), 96)
        high = pl.ds(pl.multiple_of(c * 96 + TILES, 96), 96)
        values = [feats[low, :].astype(F32), feats[high, :].astype(F32)]
        center = sum(jnp.sum(v, axis=-1, keepdims=True) for v in values) * (1.0 / WIDE)
        moved = [v - center for v in values]
        spread_sq = sum(jnp.sum(v * v, axis=-1, keepdims=True) for v in moved) * (1.0 / WIDE)
        scale = lax.rsqrt(spread_sq + 1e-06)
        normed[low, :] = (moved[0] * scale * gain_ref[:WIDTH].reshape(1, WIDTH)).astype(BF16)
        normed[high, :] = (moved[1] * scale * gain_ref[WIDTH:].reshape(1, WIDTH)).astype(BF16)

    pl.semaphore_wait(barrier, 22)
    near_copies = [
        begin(tally.at[dev[0]], near_all.at[slide], send_n.at[k], recv_n.at[k], dev) for k, dev in enumerate(slides)
    ]
    near_all[slide] = tally[slide]
    loads[2].wait()
    x_copies = []
    for part in range(2):
        cols = slice(part * 384, part * 384 + 384)
        embedded = dot(normed[:TILES, :], w_e[:WIDTH, cols]) + dot(normed[TILES:, :], w_e[WIDTH:, cols])
        o_t[:TILES, cols] = embedded.astype(BF16)
        placed[:, cols] = dot(placing[...], o_t[:TILES, cols]).astype(BF16)
        for k in (7, 8, 6, 9, 5, 10, 4, 11, 3, 12, 2, 13, 1, 14, 0):
            dev = slides[k]
            src = placed.at[pl.ds(pl.multiple_of(dev[0] * CAP, CAP), CAP), cols]
            dst = x.at[pl.ds(pl.multiple_of(slide * CAP, CAP), CAP), cols]
            x_copies.append(begin(src, dst, send_x.at[part, k], recv_x.at[part, k], dev))
    own = pl.ds(pl.multiple_of(slide * CAP, CAP), CAP)
    x[own, :] = placed[own, :]

    for copy in near_copies:
        copy.wait_recv()
    for i in range(16):
        near[i : i + 1, :] = near_all[i][:1]
    far_copies = [begin(near, far.at[seq], send_f.at[k], recv_f.at[k], dev) for k, dev in enumerate(blocks)]
    far[seq] = near[...]
    place_in = lax.broadcasted_iota(jnp.int32, (CAP, 128), 0).astype(F32)
    for i in range(16):
        val[i * CAP : i * CAP + CAP, :] = jnp.where(place_in < near[i : i + 1, :], 1.0, 0.0)
    for t in range(3):
        perm[t] = (lax.broadcasted_iota(jnp.int32, (WIDTH, WIDTH), 0) == place_ref[t][:1, :]).astype(BF16)
    row = lax.broadcasted_iota(jnp.int32, (64, SLOTS), 0)
    filler = jnp.where(row == 0, 1.0, 0.0).astype(BF16)
    zeros = jnp.zeros((64, SLOTS), BF16)
    q_0[64:, :], q_1[:64, :] = filler, filler
    do_0[64:, :], do_1[:64, :] = zeros, zeros
    for copy in loads[3:]:
        copy.wait()
    mg_val = val[:SLOTS, :].astype(BF16)
    for c in range(6):
        cols = slice(c * 128, c * 128 + 128)
        mg[:, cols] = mg[:, cols] * mg_val

    @pl.loop(0, 3)
    def _(c):
        cols = pl.ds(pl.multiple_of(c * BLOCK, BLOCK), BLOCK)
        d_heads = lax.dot_general(mg[...], wout[cols, :], NT, preferred_element_type=F32).astype(BF16)
        do_tok[:, cols] = d_heads
        do_t[cols, :] = d_heads.T

    row = lax.broadcasted_iota(jnp.int32, (96, SLOTS), 0)
    pick = lax.broadcasted_iota(jnp.int32, (96, SLOTS), 1) == (row % 16) * CAP + (row // 16) * RATE
    pick = pick.astype(BF16)
    for copy in x_copies:
        copy.wait_recv()
    rows = dot(pick, x[...]).astype(BF16)
    for m in range(6):
        own_far[m] = rows[m * 16 : m * 16 + 16]

    up = (slide, lax.rem(z + 1, SIDE) * 2 + core)
    down = (slide, lax.rem(z + 3, SIDE) * 2 + core)
    across = lax.rem(z + 2, SIDE) * 2 + core
    to_up = begin(own_far, xd.at[:, seq], send_z.at[0], recv_z.at[0], up)
    to_down = begin(own_far, xd.at[:, seq], send_z.at[1], recv_z.at[1], down)
    to_side = [begin(own_far, xd.at[:, seq], send_s.at[0], recv_s.at[0], sibling)]
    xd[:, seq] = own_far[...]

    def project(first, rows_of):
        @pl.loop(0, 3)
        def _(c):
            cols = pl.ds(pl.multiple_of(c * BLOCK, BLOCK), BLOCK)
            x_t[cols, first : first + SLOTS] = rows_of(cols).T
            for w, tok, turned in ((w_k, k_tok, k_t), (w_v, v_tok, v_t)):
                part = dot(rows_of(slice(None)), w[:, cols]).astype(BF16)
                tok[first : first + SLOTS, cols] = part
                turned[cols, first : first + SLOTS] = part.T

    @pl.loop(0, 3)
    def _(c):
        cols = pl.ds(pl.multiple_of(c * BLOCK, BLOCK), BLOCK)
        query = dot(x[...], w_q[:, cols]).astype(BF16) * BF16(0.125)
        q_tok[:, cols] = query
        q_t[cols, :] = query.T

    to_up.wait_recv()
    relay_up = begin(xd.at[pl.ds(0, 3), down[1]], xd.at[pl.ds(0, 3), down[1]], send_z.at[2], recv_z.at[2], up)
    to_side.append(begin(xd.at[:, down[1]], xd.at[:, down[1]], send_s.at[1], recv_s.at[1], sibling))
    to_down.wait_recv()
    relay_down = begin(xd.at[pl.ds(3, 3), up[1]], xd.at[pl.ds(3, 3), up[1]], send_z.at[3], recv_z.at[3], down)
    to_side.append(begin(xd.at[:, up[1]], xd.at[:, up[1]], send_s.at[2], recv_s.at[2], sibling))

    project(0, lambda cols: x[:, cols])

    relay_up.wait_recv()
    relay_down.wait_recv()
    to_side.append(begin(xd.at[:, across], xd.at[:, across], send_s.at[3], recv_s.at[3], sibling))
    for copy in far_copies:
        copy.wait_recv()
    for m in range(6):
        for j in range(8):
            first = SLOTS + m * 128 + j * 16
            val[first : first + 16, :] = jnp.where(far[j] > m * RATE, 1.0, 0.0)
    bias[...] = jnp.where(val[...] > 0.5, 0.0, MASKED).astype(BF16)
    for copy in to_side:
        copy.wait_recv()

    project(SLOTS, lambda cols: xd[:, :, :, cols].reshape(SLOTS, WIDTH if isinstance(cols, slice) else BLOCK))

    for copy in to_side + far_copies + near_copies + x_copies + [to_up, to_down, relay_up, relay_down]:
        copy.wait_send()

    def close_keys(pair, a, third):
        rows = slice(third * PART, third * PART + PART)
        mine = lax.broadcasted_iota(jnp.int32, (PART, 128), 1) // 64 == a
        slot = lax.rem(pair // 2, 2)
        for offset, left, right in ((0, grad[a], q_cat[a]), (BLOCK, prob[a], do_cat[a])):
            lanes = pl.ds(pl.multiple_of(lax.rem(pair, 2) * 128 + offset, 128), 128)
            part = dot(left[rows, :], right[...]).astype(BF16)
            dkv[slot, rows, lanes] = jnp.where(mine, part, dkv[slot, rows, lanes])

    own_half = pl.multiple_of(core * 384, 384)
    its_half = pl.multiple_of((1 - core) * 384, 384)

    def parity(r):
        return r % 2 if isinstance(r, int) else lax.rem(r, 2)

    def axis_copies(r, t, axis, source, landing, send, recv, height):
        copies = []
        for d in (2, 1, 3):
            moved = dict(at)
            moved[axis] = lax.rem(at[axis] + d, SIDE)
            device = (moved["y"] * SIDE + moved["x"], moved["z"] * 2 + core)
            if height:
                src = source.at[r, t, pl.ds(pl.multiple_of(moved[axis] * height, height), height), :]
            else:
                src = source.at[r, t, moved[axis]]
            copies.append(remote(src, landing.at[r, t, d - 1], send.at[r, t, d - 1], recv.at[r, t, d - 1], device))
        return copies

    def pair_copy(r, t):
        src = g.at[parity(r), t, pl.ds(its_half, 384), :]
        return remote(src, half.at[r, t], send0.at[r, t], recv0.at[r, t], sibling)

    def a_copies(r, t):
        return axis_copies(r, t, ORDERS[t][0], pair_sum, from_a, send_a, recv_a, 96)

    def b_copies(r, t):
        return axis_copies(r, t, ORDERS[t][1], owned, from_b, send_b, recv_b, 24)

    def c_copies(r, t):
        return axis_copies(r, t, ORDERS[t][2], spread, from_c, send_c, recv_c, 0)

    def stage_pair(r, parts):
        for t in range(3):
            g[parity(r), t] = dot(perm[t], parts(t).astype(BF16)).astype(BF16)
            pair_copy(r, t).start()

    def stage_qkv(r):
        slot = parity(r)

        def parts(t):
            if t == 0:
                return dot(x_t[:, :SLOTS], dq_round[slot])
            return dot(x_t[...], dkv[slot, :, (t - 1) * BLOCK : t * BLOCK])

        stage_pair(r, parts)

    def stage_a(r):
        for t in range(3):
            copy = pair_copy(r, t)
            copy.wait_recv()
            mine = g[parity(r), t, pl.ds(own_half, 384), :].astype(F32)
            pair_sum[r, t] = (mine + half[r, t].astype(F32)).astype(BF16)
            for copy in a_copies(r, t):
                copy.start()

    def stage_b(r):
        for t in range(3):
            mine = pl.multiple_of(at[ORDERS[t][0]] * 96, 96)
            total = g[parity(r), t, pl.ds(pl.multiple_of(own_half + mine, 96), 96), :].astype(F32)
            total = total + half[r, t, pl.ds(mine, 96), :].astype(F32)
            for copy in a_copies(r, t):
                copy.wait_recv()
            for d in range(3):
                total = total + from_a[r, t, d].astype(F32)
            owned[r, t] = total
            for copy in b_copies(r, t):
                copy.start()

    def stage_c(r):
        for t in range(3):
            total = owned[r, t, pl.ds(pl.multiple_of(at[ORDERS[t][1]] * 24, 24), 24), :]
            for copy in b_copies(r, t):
                copy.wait_recv()
            for d in range(3):
                total = total + from_b[r, t, d]
            for c in range(SIDE):
                spread[r, t, c, :6, :] = total[c * 6 : c * 6 + 6]
                spread[r, t, c, 6:, :] = jnp.zeros((2, BLOCK), F32)
            for copy in c_copies(r, t):
                copy.start()

    def stage_out(r):
        for t in range(3):
            total = spread[r, t, at[ORDERS[t][2]]]
            for copy in c_copies(r, t):
                copy.wait_recv()
            for d in range(3):
                total = total + from_c[r, t, d]
            total = total[:6] * factor
            if r < 3:
                first = t * WIDTH + r * BLOCK
                oq_ref[:, first : first + BLOCK] = total
            else:
                oo_ref[:, t * BLOCK : t * BLOCK + BLOCK] = total

    def sent(r):
        for t in range(3):
            for copy in a_copies(r, t) + b_copies(r, t) + c_copies(r, t):
                copy.wait_send()

    @pl.loop(0, HEADS // 2)
    def _(pair):
        lanes = pl.ds(pl.multiple_of(pair * 128, 128), 128)
        before = lax.max(pair - 1, 0)
        done = lax.max(pair // 2 - 1, 0)
        lane = lax.broadcasted_iota(jnp.int32, (KEYS, 128), 1)
        lane_q = lax.broadcasted_iota(jnp.int32, (SLOTS, 128), 1)
        nothing = jnp.zeros((SLOTS, 128), BF16)

        def head_rows(a):
            return pl.ds(pl.multiple_of(pair * 128 + a * 64, 64), 64)

        def open_head(a):
            own = slice(a * 64, a * 64 + 64)
            keys[a][...] = jnp.where(lane // 64 == a, k_tok[:, lanes], bias[...])
            q_rows[a][own, :] = q_t[head_rows(a), :]
            do_rows[a][own, :] = do_t[head_rows(a), :]

        def score_piece(step, piece):
            a, block = step // 3, step % 3
            rows = slice(piece * CHAIN, piece * CHAIN + CHAIN)
            s = dot(keys[a][rows, :], q_rows[a][:, block * BLOCK : block * BLOCK + BLOCK])
            peak = jnp.max(s, axis=0, keepdims=True)
            raw = jnp.exp(s - peak)
            scores[step % 2][rows, :] = raw
            return peak, jnp.sum(raw, axis=0, keepdims=True)

        def factors(parts):
            peak = functools.reduce(jnp.maximum, [p for p, _ in parts])
            weights = [jnp.exp(p - peak) for p, _ in parts]
            inverse = 1.0 / sum(w * total for w, (_, total) in zip(weights, parts))
            return [w * inverse for w in weights]

        open_head(0)
        parts = [score_piece(0, piece) for piece in range(PIECES)]
        open_head(1)
        for step in range(6):
            a, block = step // 3, step % 3
            cols = slice(block * BLOCK, block * BLOCK + BLOCK)
            score = scores[step % 2]
            factor_of = factors(parts)
            parts = []
            for piece in range(PIECES):
                rows = slice(piece * CHAIN, piece * CHAIN + CHAIN)
                prob[a][rows, cols] = (score[rows, :] * factor_of[piece]).astype(BF16)
                if step < 5:
                    parts.append(score_piece(step + 1, piece))
            out = dot(v_t[head_rows(a), :], prob[a][:, cols]).astype(BF16)
            o_t[head_rows(a), cols] = out
            if a == 0:
                close_keys(before, 1, block)
            else:
                close_keys(pair, 0, block)
            delta = jnp.sum(do_t[head_rows(a), cols].astype(F32) * out.astype(F32), axis=0, keepdims=True)
            for piece in range(PIECES):
                rows = slice(piece * CHAIN, piece * CHAIN + CHAIN)
                grad_p = dot(v_tok[rows, lanes], do_rows[a][:, cols])
                grad[a][rows, cols] = (score[rows, :] * ((grad_p - delta) * factor_of[piece])).astype(BF16)
            dq_t[a * 64 : a * 64 + 64, cols] = (dot(k_t[head_rows(a), :], grad[a][:, cols]) * 0.125).astype(BF16)
            if step == 2:
                @pl.when((pair == 2) | (pair == 4))
                def _():
                    stage_qkv(done)

                @pl.when((pair == 3) | (pair == 5))
                def _():
                    stage_b(done)

                @pl.when(pair == 4)
                def _():
                    stage_out(0)

            if block == 2:
                half_lanes = lane_q // 64 == a
                q_cat[a][...] = jnp.where(half_lanes, q_tok[:, lanes], nothing)
                do_cat[a][...] = jnp.where(half_lanes, do_tok[:, lanes], nothing)
        dq_round[lax.rem(pair // 2, 2), :, pl.ds(pl.multiple_of(lax.rem(pair, 2) * 128, 128), 128)] = dq_t[...].T

        @pl.when((pair == 2) | (pair == 4))
        def _():
            stage_a(done)

        @pl.when((pair == 3) | (pair == 5))
        def _():
            stage_c(done)

    for third in range(3):
        close_keys(HEADS // 2 - 1, 1, third)
    for t in range(3):
        pair_copy(0, t).wait_send()
    stage_qkv(2)
    for t in range(3):
        pair_copy(1, t).wait_send()
    stage_pair(3, lambda t: dot(o_t[...], mg[:, t * BLOCK : t * BLOCK + BLOCK]))
    stage_a(2)
    do_tok[...] = o_t[...].T
    stage_a(3)

    @pl.loop(0, 3)
    def _(c):
        cols = pl.ds(pl.multiple_of(c * BLOCK, BLOCK), BLOCK)
        mixed = x[:, cols].astype(F32) + dot(do_tok[...], wout[:, cols])
        q_tok[:, cols] = (mixed * val[:SLOTS, :1]).astype(BF16)

    store = pltpu.make_async_copy(q_tok, att_ref, load.at[0])
    store.start()
    stage_out(1)
    for stage in (stage_b, stage_c, stage_out):
        stage(2)
        stage(3)
    for r in range(4):
        sent(r)
    for r in (2, 3):
        for t in range(3):
            pair_copy(r, t).wait_send()
    store.wait()


def whole(feats, gain, w_embed, target, cot, w_qkv, w_out, factor):
    tall, wide, square = (KEYS, WIDTH), (WIDTH, KEYS), (SLOTS, WIDTH)
    vmem, anywhere = pl.BlockSpec(memory_space=pltpu.VMEM), pl.BlockSpec(memory_space=pl.ANY)
    dma = pltpu.SemaphoreType.DMA
    half16 = lambda *shapes: [pltpu.VMEM(shape, BF16) for shape in shapes]
    full32 = lambda *shapes: [pltpu.VMEM(shape, F32) for shape in shapes]
    scratch = half16(square, (6, 8, 16, WIDTH)) + full32((KEYS, 128)) + half16((KEYS, 128))
    scratch += half16(square, tall, tall, square, square, wide, wide, square, wide, square, square, square)
    scratch += half16((128, SLOTS), (2, SLOTS, BLOCK), (2, KEYS, 2 * BLOCK))
    scratch += full32((KEYS, BLOCK), (KEYS, BLOCK)) + half16(tall, tall, tall, tall)
    scratch += half16(*[(KEYS, 128)] * 2, *[(128, SLOTS)] * 4, *[(SLOTS, 128)] * 4, (3, WIDTH, WIDTH))
    scratch += full32((16, 8, 128), (16, 8, 128), (16, 128), (8, 16, 128)) + half16((6, 16, WIDTH))
    scratch += half16((2, 3, WIDTH, BLOCK), (4, 3, 384, BLOCK), (4, 3, 384, BLOCK), (4, 3, 3, 96, BLOCK))
    scratch += full32((4, 3, 96, BLOCK), (4, 3, 3, 24, BLOCK), (4, 3, SIDE, 8, BLOCK), (4, 3, 3, 8, BLOCK))
    scratch += [dma((8,)), dma((2, 15)), dma((2, 15)), dma((15,)), dma((15,)), dma((7,)), dma((7,))]
    scratch += [dma((4,))] * 4 + [dma((4, 3))] * 2 + [dma((4, 3, 3))] * 6
    return pl.pallas_call(
        functools.partial(whole_kernel, factor),
        out_shape=(
            jax.ShapeDtypeStruct(square, BF16),
            jax.ShapeDtypeStruct((6, 3 * WIDTH), F32),
            jax.ShapeDtypeStruct((6, WIDTH), F32),
        ),
        in_specs=[anywhere, vmem, anywhere, vmem, anywhere, anywhere, anywhere, vmem],
        out_specs=(anywhere, vmem, vmem),
        scratch_shapes=scratch,
        compiler_params=pltpu.CompilerParams(
            collective_id=1, has_side_effects=True, vmem_limit_bytes=63 * 1024 * 1024
        ),
        cost_estimate=pl.CostEstimate(flops=30_000_000_000, bytes_accessed=16_000_000, transcendentals=14_000_000),
        name="whole",
    )(feats, gain, w_embed, target, cot, w_qkv, w_out, jnp.asarray(row_orders()))


def hand_over_kernel(*refs):
    ins, outs, held, sem_in, sem_out = refs[:3], refs[3:6], refs[6:9], refs[9], refs[10]
    pieces = [(0, slice(first, first + 192)) for first in range(0, SLOTS, 192)] + [(1, slice(0, 6)), (2, slice(0, 6))]
    arriving, leaving = [], []
    for n, (which, rows) in enumerate(pieces):
        arriving.append(pltpu.make_async_copy(ins[which].at[rows], held[which].at[rows], sem_in.at[n]))
        leaving.append(pltpu.make_async_copy(held[which].at[rows], outs[which].at[rows], sem_out.at[n]))
    for copy in arriving:
        copy.start()
    for first, second in zip(arriving, leaving):
        first.wait()
        second.start()
    for copy in leaving:
        copy.wait()


def hand_over(*arrays):
    anywhere = pl.BlockSpec(memory_space=pl.ANY)
    return pl.pallas_call(
        hand_over_kernel,
        out_shape=tuple(jax.ShapeDtypeStruct(a.shape, a.dtype) for a in arrays),
        in_specs=[anywhere] * 3,
        out_specs=(anywhere,) * 3,
        scratch_shapes=[pltpu.VMEM(a.shape, a.dtype) for a in arrays] + [pltpu.SemaphoreType.DMA((6,))] * 2,
        compiler_params=pltpu.CompilerParams(vmem_limit_bytes=63 * 1024 * 1024),
        name="hand_over",
    )(*arrays)


def shards(tile_feats, norm_gain, w_embed, slide_of_tile, w_qkv, w_out, cotangent):
    factor = (lax.axis_size("slide") * lax.axis_size("seq") * SLOTS) ** (-0.5)
    output, grad_qkv, grad_out = hand_over(*whole(
        tile_feats, norm_gain, w_embed, slide_of_tile.reshape(1, TILES),
        cotangent[0], w_qkv, w_out, factor,
    ))
    return (output[None], grad_qkv, grad_out)


def solution(mesh):
    return jax.shard_map(
        shards,
        mesh=mesh,
        in_specs=(
            P(("slide", "seq"), None),
            P(),
            P(),
            P(("slide", "seq"), None),
            P(),
            P(),
            P("slide", "seq", None),
        ),
        out_specs=(P("slide", "seq", None), P(("slide", "seq"), None), P(("slide", "seq"), None)),
        check_vma=False,
    )
```

```python
import functools

import jax
import jax.numpy as jnp
import numpy as np
from jax import lax
from jax.experimental import pallas as pl
from jax.experimental.pallas import tpu as pltpu
from jax.sharding import PartitionSpec as P

HEADS = 12
CAP = 48
RATE = 8
WIDTH = 768
WIDE = 1536
TILES = 384
SLOTS = 768
KEYS = 1536
BLOCK = 256
PART = 512
CHAIN = 256
PIECES = KEYS // CHAIN
SIDE = 4
MASKED = -1e30
BF16 = jnp.bfloat16
F32 = jnp.float32
MESH = pl.DeviceIdType.MESH
ORDERS = (("x", "y", "z"), ("y", "z", "x"), ("z", "x", "y"))
NT = (((1,), (1,)), ((), ()))


def row_orders():
    feature = np.arange(WIDTH)
    device, inner = feature // 6, feature % 6
    at = {"core": device % 2, "z": device // 2 % 4, "x": device // 8 % 4, "y": device // 32}
    places = [
        at["core"] * 384 + at[a] * 96 + at[b] * 24 + at[c] * 6 + inner for a, b, c in ORDERS
    ]
    return np.broadcast_to(np.stack(places)[:, None, :], (3, 8, WIDTH)).astype(np.int32)


def dot(a, b):
    return jnp.dot(a, b, preferred_element_type=F32)


def whole_kernel(
    factor,
    feats_ref, gain_ref, we_ref, target_ref, cot_ref, wqkv_ref, wout_ref, place_ref,
    att_ref, oq_ref, oo_ref,
    x, xd, val, bias, q_tok, k_tok, v_tok, do_tok, q_t, k_t, v_t, do_t, x_t, mg, o_t, wout,
    dq_t, dq_round, dkv, score_0, score_1, prob_0, prob_1, grad_0, grad_1,
    key_0, key_1, q_0, q_1, do_0, do_1, qc_0, qc_1, dc_0, dc_1, perm,
    tally, near_all, near, far, own_far,
    g, half, pair_sum, from_a, owned, from_b, spread, from_c,
    load, send_x, recv_x, send_n, recv_n, send_f, recv_f, send_z, recv_z, send_s, recv_s,
    send0, recv0, send_a, recv_a, send_b, recv_b, send_c, recv_c,
):
    scores, prob, grad = (score_0, score_1), (prob_0, prob_1), (grad_0, grad_1)
    keys, q_rows, do_rows = (key_0, key_1), (q_0, q_1), (do_0, do_1)
    q_cat, do_cat = (qc_0, qc_1), (dc_0, dc_1)
    slide, seq = lax.axis_index("slide"), lax.axis_index("seq")
    at = {"y": slide // SIDE, "x": slide % SIDE, "z": seq // 2}
    z, core = at["z"], seq % 2
    sibling = (slide, z * 2 + 1 - core)
    slides = [(lax.rem(slide + k, 16), seq) for k in range(1, 16)]
    blocks = [(slide, lax.rem(seq + k, 8)) for k in range(1, 8)]

    barrier = pltpu.get_barrier_semaphore()
    for device in slides + blocks:
        pl.semaphore_signal(barrier, inc=1, device_id=device, device_id_type=MESH)

    def remote(src, dst, send, recv, device):
        return pltpu.make_async_remote_copy(
            src_ref=src, dst_ref=dst, send_sem=send, recv_sem=recv, device_id=device, device_id_type=MESH
        )

    def begin(*args):
        copy = remote(*args)
        copy.start()
        return copy

    feats, normed, placed, w_e, w_q, w_k, w_v = (
        grad_0.at[:SLOTS], grad_1.at[:SLOTS], grad_1.at[SLOTS:], prob_1,
        prob_0.at[:SLOTS], prob_0.at[SLOTS:], grad_0.at[SLOTS:],
    )
    sources = [
        (feats_ref.at[:, :WIDTH], feats.at[:TILES]), (feats_ref.at[:, WIDTH:], feats.at[TILES:]),
        (we_ref, w_e), (cot_ref, mg), (wout_ref, wout),
        (wqkv_ref.at[:, :WIDTH], w_q), (wqkv_ref.at[:, WIDTH : 2 * WIDTH], w_k), (wqkv_ref.at[:, 2 * WIDTH :], w_v),
    ]
    loads = [pltpu.make_async_copy(src, dst, load.at[n]) for n, (src, dst) in enumerate(sources)]
    for copy in loads:
        copy.start()

    target = target_ref[...]
    named = lax.broadcasted_iota(jnp.int32, (16, TILES), 0) == target
    one_hot = jnp.where(named, 1.0, 0.0)
    earlier = (
        lax.broadcasted_iota(jnp.int32, (TILES, TILES), 0) < lax.broadcasted_iota(jnp.int32, (TILES, TILES), 1)
    ).astype(BF16)
    before_it = dot(one_hot.astype(BF16), earlier)
    rank = jnp.sum(one_hot * before_it, axis=0, keepdims=True)
    slot = target * CAP + rank.astype(jnp.int32)
    placing = x_t.at[:, :TILES]
    placing[...] = (lax.broadcasted_iota(jnp.int32, (SLOTS, TILES), 0) == slot).astype(BF16)
    total = jnp.sum(one_hot, axis=1, keepdims=True)
    for d in range(16):
        tally[d] = jnp.broadcast_to(total[d : d + 1], (8, 128))
    loads[0].wait()
    loads[1].wait()

    @pl.loop(0, 4)
    def _(c):
        low = pl.ds(pl.multiple_of(c * 96, 96), 96)
        high = pl.ds(pl.multiple_of(c * 96 + TILES, 96), 96)
        values = [feats[low, :].astype(F32), feats[high, :].astype(F32)]
        center = sum(jnp.sum(v, axis=-1, keepdims=True) for v in values) * (1.0 / WIDE)
        moved = [v - center for v in values]
        spread_sq = sum(jnp.sum(v * v, axis=-1, keepdims=True) for v in moved) * (1.0 / WIDE)
        scale = lax.rsqrt(spread_sq + 1e-06)
        normed[low, :] = (moved[0] * scale * gain_ref[:WIDTH].reshape(1, WIDTH)).astype(BF16)
        normed[high, :] = (moved[1] * scale * gain_ref[WIDTH:].reshape(1, WIDTH)).astype(BF16)

    pl.semaphore_wait(barrier, 22)
    near_copies = [
        begin(tally.at[dev[0]], near_all.at[slide], send_n.at[k], recv_n.at[k], dev) for k, dev in enumerate(slides)
    ]
    near_all[slide] = tally[slide]
    loads[2].wait()
    x_copies = []
    for part in range(2):
        cols = slice(part * 384, part * 384 + 384)
        embedded = dot(normed[:TILES, :], w_e[:WIDTH, cols]) + dot(normed[TILES:, :], w_e[WIDTH:, cols])
        o_t[:TILES, cols] = embedded.astype(BF16)
        placed[:, cols] = dot(placing[...], o_t[:TILES, cols]).astype(BF16)
        for k in (7, 8, 6, 9, 5, 10, 4, 11, 3, 12, 2, 13, 1, 14, 0):
            dev = slides[k]
            src = placed.at[pl.ds(pl.multiple_of(dev[0] * CAP, CAP), CAP), cols]
            dst = x.at[pl.ds(pl.multiple_of(slide * CAP, CAP), CAP), cols]
            x_copies.append(begin(src, dst, send_x.at[part, k], recv_x.at[part, k], dev))
    own = pl.ds(pl.multiple_of(slide * CAP, CAP), CAP)
    x[own, :] = placed[own, :]

    for copy in near_copies:
        copy.wait_recv()
    for i in range(16):
        near[i : i + 1, :] = near_all[i][:1]
    far_copies = [begin(near, far.at[seq], send_f.at[k], recv_f.at[k], dev) for k, dev in enumerate(blocks)]
    far[seq] = near[...]
    place_in = lax.broadcasted_iota(jnp.int32, (CAP, 128), 0).astype(F32)
    for i in range(16):
        val[i * CAP : i * CAP + CAP, :] = jnp.where(place_in < near[i : i + 1, :], 1.0, 0.0)
    for t in range(3):
        perm[t] = (lax.broadcasted_iota(jnp.int32, (WIDTH, WIDTH), 0) == place_ref[t][:1, :]).astype(BF16)
    row = lax.broadcasted_iota(jnp.int32, (64, SLOTS), 0)
    filler = jnp.where(row == 0, 1.0, 0.0).astype(BF16)
    zeros = jnp.zeros((64, SLOTS), BF16)
    q_0[64:, :], q_1[:64, :] = filler, filler
    do_0[64:, :], do_1[:64, :] = zeros, zeros
    for copy in loads[3:]:
        copy.wait()
    mg_val = val[:SLOTS, :].astype(BF16)
    for c in range(6):
        cols = slice(c * 128, c * 128 + 128)
        mg[:, cols] = mg[:, cols] * mg_val

    @pl.loop(0, 3)
    def _(c):
        cols = pl.ds(pl.multiple_of(c * BLOCK, BLOCK), BLOCK)
        d_heads = lax.dot_general(mg[...], wout[cols, :], NT, preferred_element_type=F32).astype(BF16)
        do_tok[:, cols] = d_heads
        do_t[cols, :] = d_heads.T

    row = lax.broadcasted_iota(jnp.int32, (96, SLOTS), 0)
    pick = lax.broadcasted_iota(jnp.int32, (96, SLOTS), 1) == (row % 16) * CAP + (row // 16) * RATE
    pick = pick.astype(BF16)
    for copy in x_copies:
        copy.wait_recv()
    rows = dot(pick, x[...]).astype(BF16)
    for m in range(6):
        own_far[m] = rows[m * 16 : m * 16 + 16]

    up = (slide, lax.rem(z + 1, SIDE) * 2 + core)
    down = (slide, lax.rem(z + 3, SIDE) * 2 + core)
    across = lax.rem(z + 2, SIDE) * 2 + core
    to_up = begin(own_far, xd.at[:, seq], send_z.at[0], recv_z.at[0], up)
    to_down = begin(own_far, xd.at[:, seq], send_z.at[1], recv_z.at[1], down)
    to_side = [begin(own_far, xd.at[:, seq], send_s.at[0], recv_s.at[0], sibling)]
    xd[:, seq] = own_far[...]

    def project(first, rows_of):
        @pl.loop(0, 3)
        def _(c):
            cols = pl.ds(pl.multiple_of(c * BLOCK, BLOCK), BLOCK)
            x_t[cols, first : first + SLOTS] = rows_of(cols).T
            for w, tok, turned in ((w_k, k_tok, k_t), (w_v, v_tok, v_t)):
                part = dot(rows_of(slice(None)), w[:, cols]).astype(BF16)
                tok[first : first + SLOTS, cols] = part
                turned[cols, first : first + SLOTS] = part.T

    @pl.loop(0, 3)
    def _(c):
        cols = pl.ds(pl.multiple_of(c * BLOCK, BLOCK), BLOCK)
        query = dot(x[...], w_q[:, cols]).astype(BF16) * BF16(0.125)
        q_tok[:, cols] = query
        q_t[cols, :] = query.T

    to_up.wait_recv()
    relay_up = begin(xd.at[pl.ds(0, 3), down[1]], xd.at[pl.ds(0, 3), down[1]], send_z.at[2], recv_z.at[2], up)
    to_side.append(begin(xd.at[:, down[1]], xd.at[:, down[1]], send_s.at[1], recv_s.at[1], sibling))
    to_down.wait_recv()
    relay_down = begin(xd.at[pl.ds(3, 3), up[1]], xd.at[pl.ds(3, 3), up[1]], send_z.at[3], recv_z.at[3], down)
    to_side.append(begin(xd.at[:, up[1]], xd.at[:, up[1]], send_s.at[2], recv_s.at[2], sibling))

    project(0, lambda cols: x[:, cols])

    relay_up.wait_recv()
    relay_down.wait_recv()
    to_side.append(begin(xd.at[:, across], xd.at[:, across], send_s.at[3], recv_s.at[3], sibling))
    for copy in far_copies:
        copy.wait_recv()
    for m in range(6):
        for j in range(8):
            first = SLOTS + m * 128 + j * 16
            val[first : first + 16, :] = jnp.where(far[j] > m * RATE, 1.0, 0.0)
    bias[...] = jnp.where(val[...] > 0.5, 0.0, MASKED).astype(BF16)
    for copy in to_side:
        copy.wait_recv()

    project(SLOTS, lambda cols: xd[:, :, :, cols].reshape(SLOTS, WIDTH if isinstance(cols, slice) else BLOCK))

    for copy in to_side + far_copies + near_copies + x_copies + [to_up, to_down, relay_up, relay_down]:
        copy.wait_send()

    def close_keys(pair, a, third):
        rows = slice(third * PART, third * PART + PART)
        mine = lax.broadcasted_iota(jnp.int32, (PART, 128), 1) // 64 == a
        slot = lax.rem(pair // 2, 2)
        for offset, left, right in ((0, grad[a], q_cat[a]), (BLOCK, prob[a], do_cat[a])):
            lanes = pl.ds(pl.multiple_of(lax.rem(pair, 2) * 128 + offset, 128), 128)
            part = dot(left[rows, :], right[...]).astype(BF16)
            dkv[slot, rows, lanes] = jnp.where(mine, part, dkv[slot, rows, lanes])

    own_half = pl.multiple_of(core * 384, 384)
    its_half = pl.multiple_of((1 - core) * 384, 384)

    def parity(r):
        return r % 2 if isinstance(r, int) else lax.rem(r, 2)

    def axis_copies(r, t, axis, source, landing, send, recv, height):
        copies = []
        for d in (2, 1, 3):
            moved = dict(at)
            moved[axis] = lax.rem(at[axis] + d, SIDE)
            device = (moved["y"] * SIDE + moved["x"], moved["z"] * 2 + core)
            if height:
                src = source.at[r, t, pl.ds(pl.multiple_of(moved[axis] * height, height), height), :]
            else:
                src = source.at[r, t, moved[axis]]
            copies.append(remote(src, landing.at[r, t, d - 1], send.at[r, t, d - 1], recv.at[r, t, d - 1], device))
        return copies

    def pair_copy(r, t):
        src = g.at[parity(r), t, pl.ds(its_half, 384), :]
        return remote(src, half.at[r, t], send0.at[r, t], recv0.at[r, t], sibling)

    def a_copies(r, t):
        return axis_copies(r, t, ORDERS[t][0], pair_sum, from_a, send_a, recv_a, 96)

    def b_copies(r, t):
        return axis_copies(r, t, ORDERS[t][1], owned, from_b, send_b, recv_b, 24)

    def c_copies(r, t):
        return axis_copies(r, t, ORDERS[t][2], spread, from_c, send_c, recv_c, 0)

    def stage_pair(r, parts):
        for t in range(3):
            g[parity(r), t] = dot(perm[t], parts(t).astype(BF16)).astype(BF16)
            pair_copy(r, t).start()

    def stage_qkv(r):
        slot = parity(r)

        def parts(t):
            if t == 0:
                return dot(x_t[:, :SLOTS], dq_round[slot])
            return dot(x_t[...], dkv[slot, :, (t - 1) * BLOCK : t * BLOCK])

        stage_pair(r, parts)

    def stage_a(r):
        for t in range(3):
            copy = pair_copy(r, t)
            copy.wait_recv()
            mine = g[parity(r), t, pl.ds(own_half, 384), :].astype(F32)
            pair_sum[r, t] = (mine + half[r, t].astype(F32)).astype(BF16)
            for copy in a_copies(r, t):
                copy.start()

    def stage_b(r):
        for t in range(3):
            mine = pl.multiple_of(at[ORDERS[t][0]] * 96, 96)
            total = g[parity(r), t, pl.ds(pl.multiple_of(own_half + mine, 96), 96), :].astype(F32)
            total = total + half[r, t, pl.ds(mine, 96), :].astype(F32)
            for copy in a_copies(r, t):
                copy.wait_recv()
            for d in range(3):
                total = total + from_a[r, t, d].astype(F32)
            owned[r, t] = total
            for copy in b_copies(r, t):
                copy.start()

    def stage_c(r):
        for t in range(3):
            total = owned[r, t, pl.ds(pl.multiple_of(at[ORDERS[t][1]] * 24, 24), 24), :]
            for copy in b_copies(r, t):
                copy.wait_recv()
            for d in range(3):
                total = total + from_b[r, t, d]
            for c in range(SIDE):
                spread[r, t, c, :6, :] = total[c * 6 : c * 6 + 6]
                spread[r, t, c, 6:, :] = jnp.zeros((2, BLOCK), F32)
            for copy in c_copies(r, t):
                copy.start()

    def stage_out(r):
        for t in range(3):
            total = spread[r, t, at[ORDERS[t][2]]]
            for copy in c_copies(r, t):
                copy.wait_recv()
            for d in range(3):
                total = total + from_c[r, t, d]
            total = total[:6] * factor
            if r < 3:
                first = t * WIDTH + r * BLOCK
                oq_ref[:, first : first + BLOCK] = total
            else:
                oo_ref[:, t * BLOCK : t * BLOCK + BLOCK] = total

    def sent(r):
        for t in range(3):
            for copy in a_copies(r, t) + b_copies(r, t) + c_copies(r, t):
                copy.wait_send()

    @pl.loop(0, HEADS // 2)
    def _(pair):
        lanes = pl.ds(pl.multiple_of(pair * 128, 128), 128)
        before = lax.max(pair - 1, 0)
        done = lax.max(pair // 2 - 1, 0)
        lane = lax.broadcasted_iota(jnp.int32, (KEYS, 128), 1)
        lane_q = lax.broadcasted_iota(jnp.int32, (SLOTS, 128), 1)
        nothing = jnp.zeros((SLOTS, 128), BF16)

        def head_rows(a):
            return pl.ds(pl.multiple_of(pair * 128 + a * 64, 64), 64)

        def open_head(a):
            own = slice(a * 64, a * 64 + 64)
            keys[a][...] = jnp.where(lane // 64 == a, k_tok[:, lanes], bias[...])
            q_rows[a][own, :] = q_t[head_rows(a), :]
            do_rows[a][own, :] = do_t[head_rows(a), :]

        def score_piece(step, piece):
            a, block = step // 3, step % 3
            rows = slice(piece * CHAIN, piece * CHAIN + CHAIN)
            s = dot(keys[a][rows, :], q_rows[a][:, block * BLOCK : block * BLOCK + BLOCK])
            peak = jnp.max(s, axis=0, keepdims=True)
            raw = jnp.exp(s - peak)
            scores[step % 2][rows, :] = raw
            return peak, jnp.sum(raw, axis=0, keepdims=True)

        def factors(parts):
            peak = functools.reduce(jnp.maximum, [p for p, _ in parts])
            weights = [jnp.exp(p - peak) for p, _ in parts]
            inverse = 1.0 / sum(w * total for w, (_, total) in zip(weights, parts))
            return [w * inverse for w in weights]

        open_head(0)
        parts = [score_piece(0, piece) for piece in range(PIECES)]
        open_head(1)
        for step in range(6):
            a, block = step // 3, step % 3
            cols = slice(block * BLOCK, block * BLOCK + BLOCK)
            score = scores[step % 2]
            factor_of = factors(parts)
            parts = []
            for piece in range(PIECES):
                rows = slice(piece * CHAIN, piece * CHAIN + CHAIN)
                prob[a][rows, cols] = (score[rows, :] * factor_of[piece]).astype(BF16)
                if step < 5:
                    parts.append(score_piece(step + 1, piece))
            out = dot(v_t[head_rows(a), :], prob[a][:, cols]).astype(BF16)
            o_t[head_rows(a), cols] = out
            if a == 0:
                close_keys(before, 1, block)
            else:
                close_keys(pair, 0, block)
            delta = jnp.sum(do_t[head_rows(a), cols].astype(F32) * out.astype(F32), axis=0, keepdims=True)
            for piece in range(PIECES):
                rows = slice(piece * CHAIN, piece * CHAIN + CHAIN)
                grad_p = dot(v_tok[rows, lanes], do_rows[a][:, cols])
                grad[a][rows, cols] = (score[rows, :] * ((grad_p - delta) * factor_of[piece])).astype(BF16)
            dq_t[a * 64 : a * 64 + 64, cols] = (dot(k_t[head_rows(a), :], grad[a][:, cols]) * 0.125).astype(BF16)
            if step == 2:
                @pl.when((pair == 2) | (pair == 4))
                def _():
                    stage_qkv(done)

                @pl.when((pair == 3) | (pair == 5))
                def _():
                    stage_b(done)

                @pl.when(pair == 4)
                def _():
                    stage_out(0)

            if block == 2:
                half_lanes = lane_q // 64 == a
                q_cat[a][...] = jnp.where(half_lanes, q_tok[:, lanes], nothing)
                do_cat[a][...] = jnp.where(half_lanes, do_tok[:, lanes], nothing)
        dq_round[lax.rem(pair // 2, 2), :, pl.ds(pl.multiple_of(lax.rem(pair, 2) * 128, 128), 128)] = dq_t[...].T

        @pl.when((pair == 2) | (pair == 4))
        def _():
            stage_a(done)

        @pl.when((pair == 3) | (pair == 5))
        def _():
            stage_c(done)

    for third in range(3):
        close_keys(HEADS // 2 - 1, 1, third)
    for t in range(3):
        pair_copy(0, t).wait_send()
    stage_qkv(2)
    for t in range(3):
        pair_copy(1, t).wait_send()
    stage_pair(3, lambda t: dot(o_t[...], mg[:, t * BLOCK : t * BLOCK + BLOCK]))
    stage_a(2)
    do_tok[...] = o_t[...].T
    stage_a(3)

    @pl.loop(0, 3)
    def _(c):
        cols = pl.ds(pl.multiple_of(c * BLOCK, BLOCK), BLOCK)
        mixed = x[:, cols].astype(F32) + dot(do_tok[...], wout[:, cols])
        q_tok[:, cols] = (mixed * val[:SLOTS, :1]).astype(BF16)

    store = pltpu.make_async_copy(q_tok, att_ref, load.at[0])
    store.start()
    stage_out(1)
    for stage in (stage_b, stage_c, stage_out):
        stage(2)
        stage(3)
    for r in range(4):
        sent(r)
    for r in (2, 3):
        for t in range(3):
            pair_copy(r, t).wait_send()
    store.wait()


def whole(feats, gain, w_embed, target, cot, w_qkv, w_out, factor):
    tall, wide, square = (KEYS, WIDTH), (WIDTH, KEYS), (SLOTS, WIDTH)
    vmem, anywhere = pl.BlockSpec(memory_space=pltpu.VMEM), pl.BlockSpec(memory_space=pl.ANY)
    dma = pltpu.SemaphoreType.DMA
    half16 = lambda *shapes: [pltpu.VMEM(shape, BF16) for shape in shapes]
    full32 = lambda *shapes: [pltpu.VMEM(shape, F32) for shape in shapes]
    scratch = half16(square, (6, 8, 16, WIDTH)) + full32((KEYS, 128)) + half16((KEYS, 128))
    scratch += half16(square, tall, tall, square, square, wide, wide, square, wide, square, square, square)
    scratch += half16((128, SLOTS), (2, SLOTS, BLOCK), (2, KEYS, 2 * BLOCK))
    scratch += full32((KEYS, BLOCK), (KEYS, BLOCK)) + half16(tall, tall, tall, tall)
    scratch += half16(*[(KEYS, 128)] * 2, *[(128, SLOTS)] * 4, *[(SLOTS, 128)] * 4, (3, WIDTH, WIDTH))
    scratch += full32((16, 8, 128), (16, 8, 128), (16, 128), (8, 16, 128)) + half16((6, 16, WIDTH))
    scratch += half16((2, 3, WIDTH, BLOCK), (4, 3, 384, BLOCK), (4, 3, 384, BLOCK), (4, 3, 3, 96, BLOCK))
    scratch += full32((4, 3, 96, BLOCK), (4, 3, 3, 24, BLOCK), (4, 3, SIDE, 8, BLOCK), (4, 3, 3, 8, BLOCK))
    scratch += [dma((8,)), dma((2, 15)), dma((2, 15)), dma((15,)), dma((15,)), dma((7,)), dma((7,))]
    scratch += [dma((4,))] * 4 + [dma((4, 3))] * 2 + [dma((4, 3, 3))] * 6
    return pl.pallas_call(
        functools.partial(whole_kernel, factor),
        out_shape=(
            jax.ShapeDtypeStruct(square, BF16),
            jax.ShapeDtypeStruct((6, 3 * WIDTH), F32),
            jax.ShapeDtypeStruct((6, WIDTH), F32),
        ),
        in_specs=[anywhere, vmem, anywhere, vmem, anywhere, anywhere, anywhere, vmem],
        out_specs=(anywhere, vmem, vmem),
        scratch_shapes=scratch,
        compiler_params=pltpu.CompilerParams(
            collective_id=1, has_side_effects=True, vmem_limit_bytes=63 * 1024 * 1024
        ),
        cost_estimate=pl.CostEstimate(flops=30_000_000_000, bytes_accessed=16_000_000, transcendentals=14_000_000),
        name="whole",
    )(feats, gain, w_embed, target, cot, w_qkv, w_out, jnp.asarray(row_orders()))


def hand_over_kernel(*refs):
    ins, outs, held, sem_in, sem_out = refs[:3], refs[3:6], refs[6:9], refs[9], refs[10]
    pieces = [(0, slice(first, first + 192)) for first in range(0, SLOTS, 192)] + [(1, slice(0, 6)), (2, slice(0, 6))]
    arriving, leaving = [], []
    for n, (which, rows) in enumerate(pieces):
        arriving.append(pltpu.make_async_copy(ins[which].at[rows], held[which].at[rows], sem_in.at[n]))
        leaving.append(pltpu.make_async_copy(held[which].at[rows], outs[which].at[rows], sem_out.at[n]))
    for copy in arriving:
        copy.start()
    for first, second in zip(arriving, leaving):
        first.wait()
        second.start()
    for copy in leaving:
        copy.wait()


def hand_over(*arrays):
    anywhere = pl.BlockSpec(memory_space=pl.ANY)
    return pl.pallas_call(
        hand_over_kernel,
        out_shape=tuple(jax.ShapeDtypeStruct(a.shape, a.dtype) for a in arrays),
        in_specs=[anywhere] * 3,
        out_specs=(anywhere,) * 3,
        scratch_shapes=[pltpu.VMEM(a.shape, a.dtype) for a in arrays] + [pltpu.SemaphoreType.DMA((6,))] * 2,
        compiler_params=pltpu.CompilerParams(vmem_limit_bytes=63 * 1024 * 1024),
        name="hand_over",
    )(*arrays)


def shards(tile_feats, norm_gain, w_embed, slide_of_tile, w_qkv, w_out, cotangent):
    factor = (lax.axis_size("slide") * lax.axis_size("seq") * SLOTS) ** (-0.5)
    output, grad_qkv, grad_out = hand_over(*whole(
        tile_feats, norm_gain, w_embed, slide_of_tile.reshape(1, TILES),
        cotangent[0], w_qkv, w_out, factor,
    ))
    return (output[None], grad_qkv, grad_out)


def solution(mesh):
    return jax.shard_map(
        shards,
        mesh=mesh,
        in_specs=(
            P(("slide", "seq"), None),
            P(),
            P(),
            P(("slide", "seq"), None),
            P(),
            P(),
            P("slide", "seq", None),
        ),
        out_specs=(P("slide", "seq", None), P(("slide", "seq"), None), P(("slide", "seq"), None)),
        check_vma=False,
    )
```

```python
import functools

import jax
import jax.numpy as jnp
import numpy as np
from jax import lax
from jax.experimental import pallas as pl
from jax.experimental.pallas import tpu as pltpu
from jax.sharding import PartitionSpec as P

HEADS = 12
CAP = 48
RATE = 8
WIDTH = 768
WIDE = 1536
TILES = 384
SLOTS = 768
KEYS = 1536
BLOCK = 256
PART = 512
CHAIN = 128
PIECES = KEYS // CHAIN
SIDE = 4
MASKED = -1e30
BF16 = jnp.bfloat16
F32 = jnp.float32
MESH = pl.DeviceIdType.MESH
ORDERS = (("x", "y", "z"), ("y", "z", "x"), ("z", "x", "y"))
NT = (((1,), (1,)), ((), ()))


def row_orders():
    feature = np.arange(WIDTH)
    device, inner = feature // 6, feature % 6
    at = {"core": device % 2, "z": device // 2 % 4, "x": device // 8 % 4, "y": device // 32}
    places = [
        at["core"] * 384 + at[a] * 96 + at[b] * 24 + at[c] * 6 + inner for a, b, c in ORDERS
    ]
    rank = np.arange(CAP)
    position = np.where(rank % RATE == 0, rank // RATE, 5 + rank - rank // RATE)
    group = np.arange(16)[:, None]
    arrival = np.where(position < 16, group * 16 + position, 256 + group * 32 + position - 16)
    natural = np.argsort(arrival.reshape(-1))
    return np.broadcast_to(np.stack(places + [natural])[:, None, :], (4, 8, WIDTH)).astype(np.int32)


def dot(a, b):
    return jnp.dot(a, b, preferred_element_type=F32)


def whole_kernel(
    factor,
    feats_ref, gain_ref, we_ref, target_ref, cot_ref, wqkv_ref, wout_ref, place_ref,
    att_ref, oq_ref, oo_ref,
    x, arrived, xd, val, bias, q_tok, k_tok, v_tok, do_tok, q_t, k_t, v_t, do_t, x_t, mg, o_t, wout,
    dq_t, dq_round, dkv, score_0, score_1, prob_0, prob_1, grad_0, grad_1,
    key_0, key_1, q_0, q_1, do_0, do_1, qc_0, qc_1, dc_0, dc_1, perm,
    tally, near_all, near, far, own_far,
    g, half, pair_sum, from_a, owned, from_b, spread, from_c,
    load, send_x, recv_x, send_n, recv_n, send_f, recv_f, send_z, recv_z, send_s, recv_s,
    send0, recv0, send_a, recv_a, send_b, recv_b, send_c, recv_c,
):
    scores, prob, grad = (score_0, score_1), (prob_0, prob_1), (grad_0, grad_1)
    keys, q_rows, do_rows = (key_0, key_1), (q_0, q_1), (do_0, do_1)
    q_cat, do_cat = (qc_0, qc_1), (dc_0, dc_1)
    slide, seq = lax.axis_index("slide"), lax.axis_index("seq")
    at = {"y": slide // SIDE, "x": slide % SIDE, "z": seq // 2}
    z, core = at["z"], seq % 2
    sibling = (slide, z * 2 + 1 - core)
    slides = [(lax.rem(slide + k, 16), seq) for k in range(1, 16)]
    blocks = [(slide, lax.rem(seq + k, 8)) for k in range(1, 8)]

    barrier = pltpu.get_barrier_semaphore()
    for device in slides + blocks:
        pl.semaphore_signal(barrier, inc=1, device_id=device, device_id_type=MESH)

    def remote(src, dst, send, recv, device):
        return pltpu.make_async_remote_copy(
            src_ref=src, dst_ref=dst, send_sem=send, recv_sem=recv, device_id=device, device_id_type=MESH
        )

    def begin(*args):
        copy = remote(*args)
        copy.start()
        return copy

    feats, normed, placed, w_e, w_q, w_k, w_v = (
        grad_0.at[:SLOTS], grad_1.at[:SLOTS], grad_1.at[SLOTS:], prob_1,
        prob_0.at[:SLOTS], prob_0.at[SLOTS:], grad_0.at[SLOTS:],
    )
    sources = [
        (feats_ref.at[:, :WIDTH], feats.at[:TILES]), (feats_ref.at[:, WIDTH:], feats.at[TILES:]),
        (we_ref, w_e), (cot_ref, mg), (wout_ref, wout),
        (wqkv_ref.at[:, :WIDTH], w_q), (wqkv_ref.at[:, WIDTH : 2 * WIDTH], w_k), (wqkv_ref.at[:, 2 * WIDTH :], w_v),
    ]
    loads = [pltpu.make_async_copy(src, dst, load.at[n]) for n, (src, dst) in enumerate(sources)]
    for copy in loads:
        copy.start()

    target = target_ref[...]
    named = lax.broadcasted_iota(jnp.int32, (16, TILES), 0) == target
    one_hot = jnp.where(named, 1.0, 0.0)
    earlier = (
        lax.broadcasted_iota(jnp.int32, (TILES, TILES), 0) < lax.broadcasted_iota(jnp.int32, (TILES, TILES), 1)
    ).astype(BF16)
    before_it = dot(one_hot.astype(BF16), earlier)
    rank = jnp.sum(one_hot * before_it, axis=0, keepdims=True)
    rank = rank.astype(jnp.int32)
    eighth = jnp.right_shift(rank, 3)
    position = jnp.where(rank == eighth * RATE, eighth, 5 + rank - eighth)
    slot = jnp.where(position < 16, target * 16 + position, 256 + target * 32 + position - 16)
    placing = x_t.at[:, :TILES]
    placing[...] = (lax.broadcasted_iota(jnp.int32, (SLOTS, TILES), 0) == slot).astype(BF16)
    total = jnp.sum(one_hot, axis=1, keepdims=True)
    for d in range(16):
        tally[d] = jnp.broadcast_to(total[d : d + 1], (8, 128))
    loads[0].wait()
    loads[1].wait()

    @pl.loop(0, 4)
    def _(c):
        low = pl.ds(pl.multiple_of(c * 96, 96), 96)
        high = pl.ds(pl.multiple_of(c * 96 + TILES, 96), 96)
        values = [feats[low, :].astype(F32), feats[high, :].astype(F32)]
        center = sum(jnp.sum(v, axis=-1, keepdims=True) for v in values) * (1.0 / WIDE)
        moved = [v - center for v in values]
        spread_sq = sum(jnp.sum(v * v, axis=-1, keepdims=True) for v in moved) * (1.0 / WIDE)
        scale = lax.rsqrt(spread_sq + 1e-06)
        normed[low, :] = (moved[0] * scale * gain_ref[:WIDTH].reshape(1, WIDTH)).astype(BF16)
        normed[high, :] = (moved[1] * scale * gain_ref[WIDTH:].reshape(1, WIDTH)).astype(BF16)

    pl.semaphore_wait(barrier, 22)
    near_copies = [
        begin(tally.at[dev[0]], near_all.at[slide], send_n.at[k], recv_n.at[k], dev) for k, dev in enumerate(slides)
    ]
    near_all[slide] = tally[slide]
    loads[2].wait()
    def tile_copies(first_of, height, cols, send, recv):
        copies = []
        for k in (7, 8, 6, 9, 5, 10, 4, 11, 3, 12, 2, 13, 1, 14, 0):
            dev = slides[k]
            src = placed.at[pl.ds(pl.multiple_of(first_of + dev[0] * height, height), height), cols]
            dst = arrived.at[pl.ds(pl.multiple_of(first_of + slide * height, height), height), cols]
            copies.append(begin(src, dst, send.at[k], recv.at[k], dev))
        return copies

    first_copies = []
    for part in range(2):
        cols = slice(part * 384, part * 384 + 384)
        embedded = dot(normed[:TILES, :], w_e[:WIDTH, cols]) + dot(normed[TILES:, :], w_e[WIDTH:, cols])
        o_t[:TILES, cols] = embedded.astype(BF16)
        placed[:, cols] = dot(placing[...], o_t[:TILES, cols]).astype(BF16)
        first_copies += tile_copies(0, 16, cols, send_x.at[part], recv_x.at[part])
    rest_copies = tile_copies(256, 32, slice(None), send_x.at[2], recv_x.at[2])
    for first_of, height in ((0, 16), (256, 32)):
        own = pl.ds(pl.multiple_of(first_of + slide * height, height), height)
        arrived[own, :] = placed[own, :]

    for copy in near_copies:
        copy.wait_recv()
    for i in range(16):
        near[i : i + 1, :] = near_all[i][:1]
    far_copies = [begin(near, far.at[seq], send_f.at[k], recv_f.at[k], dev) for k, dev in enumerate(blocks)]
    far[seq] = near[...]
    place_in = lax.broadcasted_iota(jnp.int32, (CAP, 128), 0).astype(F32)
    for i in range(16):
        val[i * CAP : i * CAP + CAP, :] = jnp.where(place_in < near[i : i + 1, :], 1.0, 0.0)
    for t in range(3):
        perm[t] = (lax.broadcasted_iota(jnp.int32, (WIDTH, WIDTH), 0) == place_ref[t][:1, :]).astype(BF16)
    row = lax.broadcasted_iota(jnp.int32, (64, SLOTS), 0)
    filler = jnp.where(row == 0, 1.0, 0.0).astype(BF16)
    zeros = jnp.zeros((64, SLOTS), BF16)
    q_0[64:, :], q_1[:64, :] = filler, filler
    do_0[64:, :], do_1[:64, :] = zeros, zeros
    for copy in loads[3:]:
        copy.wait()
    mg_val = val[:SLOTS, :].astype(BF16)
    for c in range(6):
        cols = slice(c * 128, c * 128 + 128)
        mg[:, cols] = mg[:, cols] * mg_val

    @pl.loop(0, 3)
    def _(c):
        cols = pl.ds(pl.multiple_of(c * BLOCK, BLOCK), BLOCK)
        d_heads = lax.dot_general(mg[...], wout[cols, :], NT, preferred_element_type=F32).astype(BF16)
        do_tok[:, cols] = d_heads
        do_t[cols, :] = d_heads.T

    row = lax.broadcasted_iota(jnp.int32, (96, 256), 0)
    pick = lax.broadcasted_iota(jnp.int32, (96, 256), 1) == (row % 16) * 16 + row // 16
    pick = pick.astype(BF16)
    for copy in first_copies:
        copy.wait_recv()
    rows = dot(pick, arrived[:256, :]).astype(BF16)
    for m in range(6):
        own_far[m] = rows[m * 16 : m * 16 + 16]

    up = (slide, lax.rem(z + 1, SIDE) * 2 + core)
    down = (slide, lax.rem(z + 3, SIDE) * 2 + core)
    across = lax.rem(z + 2, SIDE) * 2 + core
    to_up = begin(own_far, xd.at[:, seq], send_z.at[0], recv_z.at[0], up)
    to_down = begin(own_far, xd.at[:, seq], send_z.at[1], recv_z.at[1], down)
    to_side = [begin(own_far, xd.at[:, seq], send_s.at[0], recv_s.at[0], sibling)]
    xd[:, seq] = own_far[...]
    order = o_t
    order[...] = (lax.broadcasted_iota(jnp.int32, (SLOTS, SLOTS), 0) == place_ref[3][:1, :]).astype(BF16)
    for copy in far_copies:
        copy.wait_recv()
    for m in range(6):
        for j in range(8):
            first = SLOTS + m * 128 + j * 16
            val[first : first + 16, :] = jnp.where(far[j] > m * RATE, 1.0, 0.0)
    bias[...] = jnp.where(val[...] > 0.5, 0.0, MASKED).astype(BF16)
    to_up.wait_recv()
    relay_up = begin(xd.at[pl.ds(0, 3), down[1]], xd.at[pl.ds(0, 3), down[1]], send_z.at[2], recv_z.at[2], up)
    to_side.append(begin(xd.at[:, down[1]], xd.at[:, down[1]], send_s.at[1], recv_s.at[1], sibling))
    to_down.wait_recv()
    relay_down = begin(xd.at[pl.ds(3, 3), up[1]], xd.at[pl.ds(3, 3), up[1]], send_z.at[3], recv_z.at[3], down)
    to_side.append(begin(xd.at[:, up[1]], xd.at[:, up[1]], send_s.at[2], recv_s.at[2], sibling))
    relay_up.wait_recv()
    relay_down.wait_recv()
    to_side.append(begin(xd.at[:, across], xd.at[:, across], send_s.at[3], recv_s.at[3], sibling))

    def project(first, rows_of):
        @pl.loop(0, 3)
        def _(c):
            cols = pl.ds(pl.multiple_of(c * BLOCK, BLOCK), BLOCK)
            x_t[cols, first : first + SLOTS] = rows_of(cols).T
            for w, tok, turned in ((w_k, k_tok, k_t), (w_v, v_tok, v_t)):
                part = dot(rows_of(slice(None)), w[:, cols]).astype(BF16)
                tok[first : first + SLOTS, cols] = part
                turned[cols, first : first + SLOTS] = part.T

    for copy in to_side:
        copy.wait_recv()
    project(SLOTS, lambda cols: xd[:, :, :, cols].reshape(SLOTS, WIDTH if isinstance(cols, slice) else BLOCK))

    for copy in rest_copies:
        copy.wait_recv()

    @pl.loop(0, 3)
    def _(c):
        cols = pl.ds(pl.multiple_of(c * BLOCK, BLOCK), BLOCK)
        x[:, cols] = dot(order[...], arrived[:, cols]).astype(BF16)

    @pl.loop(0, 3)
    def _(c):
        cols = pl.ds(pl.multiple_of(c * BLOCK, BLOCK), BLOCK)
        query = dot(x[...], w_q[:, cols]).astype(BF16) * BF16(0.125)
        q_tok[:, cols] = query
        q_t[cols, :] = query.T

    project(0, lambda cols: x[:, cols])

    for copy in to_side + far_copies + near_copies + first_copies + rest_copies + [to_up, to_down, relay_up, relay_down]:
        copy.wait_send()

    def close_keys(pair, a, third):
        rows = slice(third * PART, third * PART + PART)
        mine = lax.broadcasted_iota(jnp.int32, (PART, 128), 1) // 64 == a
        slot = lax.rem(pair // 2, 2)
        for offset, left, right in ((0, grad[a], q_cat[a]), (BLOCK, prob[a], do_cat[a])):
            lanes = pl.ds(pl.multiple_of(lax.rem(pair, 2) * 128 + offset, 128), 128)
            part = dot(left[rows, :], right[...]).astype(BF16)
            dkv[slot, rows, lanes] = jnp.where(mine, part, dkv[slot, rows, lanes])

    own_half = pl.multiple_of(core * 384, 384)
    its_half = pl.multiple_of((1 - core) * 384, 384)

    def parity(r):
        return r % 2 if isinstance(r, int) else lax.rem(r, 2)

    def axis_copies(r, t, axis, source, landing, send, recv, height):
        copies = []
        for d in (2, 1, 3):
            moved = dict(at)
            moved[axis] = lax.rem(at[axis] + d, SIDE)
            device = (moved["y"] * SIDE + moved["x"], moved["z"] * 2 + core)
            if height:
                src = source.at[r, t, pl.ds(pl.multiple_of(moved[axis] * height, height), height), :]
            else:
                src = source.at[r, t, moved[axis]]
            copies.append(remote(src, landing.at[r, t, d - 1], send.at[r, t, d - 1], recv.at[r, t, d - 1], device))
        return copies

    def pair_copy(r, t):
        src = g.at[parity(r), t, pl.ds(its_half, 384), :]
        return remote(src, half.at[r, t], send0.at[r, t], recv0.at[r, t], sibling)

    def a_copies(r, t):
        return axis_copies(r, t, ORDERS[t][0], pair_sum, from_a, send_a, recv_a, 96)

    def b_copies(r, t):
        return axis_copies(r, t, ORDERS[t][1], owned, from_b, send_b, recv_b, 24)

    def c_copies(r, t):
        return axis_copies(r, t, ORDERS[t][2], spread, from_c, send_c, recv_c, 0)

    def stage_pair(r, parts):
        for t in range(3):
            g[parity(r), t] = dot(perm[t], parts(t).astype(BF16)).astype(BF16)
            pair_copy(r, t).start()

    def stage_qkv(r):
        slot = parity(r)

        def parts(t):
            if t == 0:
                return dot(x_t[:, :SLOTS], dq_round[slot])
            return dot(x_t[...], dkv[slot, :, (t - 1) * BLOCK : t * BLOCK])

        stage_pair(r, parts)

    def stage_a(r):
        for t in range(3):
            copy = pair_copy(r, t)
            copy.wait_recv()
            mine = g[parity(r), t, pl.ds(own_half, 384), :].astype(F32)
            pair_sum[r, t] = (mine + half[r, t].astype(F32)).astype(BF16)
            for copy in a_copies(r, t):
                copy.start()

    def stage_b(r):
        for t in range(3):
            mine = pl.multiple_of(at[ORDERS[t][0]] * 96, 96)
            total = g[parity(r), t, pl.ds(pl.multiple_of(own_half + mine, 96), 96), :].astype(F32)
            total = total + half[r, t, pl.ds(mine, 96), :].astype(F32)
            for copy in a_copies(r, t):
                copy.wait_recv()
            for d in range(3):
                total = total + from_a[r, t, d].astype(F32)
            owned[r, t] = total
            for copy in b_copies(r, t):
                copy.start()

    def stage_c(r):
        for t in range(3):
            total = owned[r, t, pl.ds(pl.multiple_of(at[ORDERS[t][1]] * 24, 24), 24), :]
            for copy in b_copies(r, t):
                copy.wait_recv()
            for d in range(3):
                total = total + from_b[r, t, d]
            for c in range(SIDE):
                spread[r, t, c, :6, :] = total[c * 6 : c * 6 + 6]
                spread[r, t, c, 6:, :] = jnp.zeros((2, BLOCK), F32)
            for copy in c_copies(r, t):
                copy.start()

    def stage_out(r):
        for t in range(3):
            total = spread[r, t, at[ORDERS[t][2]]]
            for copy in c_copies(r, t):
                copy.wait_recv()
            for d in range(3):
                total = total + from_c[r, t, d]
            total = total[:6] * factor
            if r < 3:
                first = t * WIDTH + r * BLOCK
                oq_ref[:, first : first + BLOCK] = total
            else:
                oo_ref[:, t * BLOCK : t * BLOCK + BLOCK] = total

    def sent(r):
        for t in range(3):
            for copy in a_copies(r, t) + b_copies(r, t) + c_copies(r, t):
                copy.wait_send()

    @pl.loop(0, HEADS // 2)
    def _(pair):
        lanes = pl.ds(pl.multiple_of(pair * 128, 128), 128)
        before = lax.max(pair - 1, 0)
        done = lax.max(pair // 2 - 1, 0)
        lane = lax.broadcasted_iota(jnp.int32, (KEYS, 128), 1)
        lane_q = lax.broadcasted_iota(jnp.int32, (SLOTS, 128), 1)
        nothing = jnp.zeros((SLOTS, 128), BF16)

        def head_rows(a):
            return pl.ds(pl.multiple_of(pair * 128 + a * 64, 64), 64)

        def open_head(a):
            own = slice(a * 64, a * 64 + 64)
            keys[a][...] = jnp.where(lane // 64 == a, k_tok[:, lanes], bias[...])
            q_rows[a][own, :] = q_t[head_rows(a), :]
            do_rows[a][own, :] = do_t[head_rows(a), :]

        def score_piece(step, piece):
            a, block = step // 3, step % 3
            rows = slice(piece * CHAIN, piece * CHAIN + CHAIN)
            s = dot(keys[a][rows, :], q_rows[a][:, block * BLOCK : block * BLOCK + BLOCK])
            peak = jnp.max(s, axis=0, keepdims=True)
            raw = jnp.exp(s - peak)
            scores[step % 2][rows, :] = raw
            return peak, jnp.sum(raw, axis=0, keepdims=True)

        def factors(parts):
            peak = functools.reduce(jnp.maximum, [p for p, _ in parts])
            weights = [jnp.exp(p - peak) for p, _ in parts]
            inverse = 1.0 / sum(w * total for w, (_, total) in zip(weights, parts))
            return [w * inverse for w in weights]

        open_head(0)
        parts = [score_piece(0, piece) for piece in range(PIECES)]
        open_head(1)
        for step in range(6):
            a, block = step // 3, step % 3
            cols = slice(block * BLOCK, block * BLOCK + BLOCK)
            score = scores[step % 2]
            factor_of = factors(parts)
            parts = []
            for piece in range(PIECES):
                rows = slice(piece * CHAIN, piece * CHAIN + CHAIN)
                prob[a][rows, cols] = (score[rows, :] * factor_of[piece]).astype(BF16)
                if step < 5:
                    parts.append(score_piece(step + 1, piece))
            out = dot(v_t[head_rows(a), :], prob[a][:, cols]).astype(BF16)
            o_t[head_rows(a), cols] = out
            if a == 0:
                close_keys(before, 1, block)
            else:
                close_keys(pair, 0, block)
            delta = jnp.sum(do_t[head_rows(a), cols].astype(F32) * out.astype(F32), axis=0, keepdims=True)
            for piece in range(PIECES):
                rows = slice(piece * CHAIN, piece * CHAIN + CHAIN)
                grad_p = dot(v_tok[rows, lanes], do_rows[a][:, cols])
                grad[a][rows, cols] = (score[rows, :] * ((grad_p - delta) * factor_of[piece])).astype(BF16)
            dq_t[a * 64 : a * 64 + 64, cols] = (dot(k_t[head_rows(a), :], grad[a][:, cols]) * 0.125).astype(BF16)
            if step == 2:
                @pl.when((pair == 2) | (pair == 4))
                def _():
                    stage_qkv(done)

                @pl.when((pair == 3) | (pair == 5))
                def _():
                    stage_b(done)

                @pl.when(pair == 4)
                def _():
                    stage_out(0)

            if block == 2:
                half_lanes = lane_q // 64 == a
                q_cat[a][...] = jnp.where(half_lanes, q_tok[:, lanes], nothing)
                do_cat[a][...] = jnp.where(half_lanes, do_tok[:, lanes], nothing)
        dq_round[lax.rem(pair // 2, 2), :, pl.ds(pl.multiple_of(lax.rem(pair, 2) * 128, 128), 128)] = dq_t[...].T

        @pl.when((pair == 2) | (pair == 4))
        def _():
            stage_a(done)

        @pl.when((pair == 3) | (pair == 5))
        def _():
            stage_c(done)

    for third in range(3):
        close_keys(HEADS // 2 - 1, 1, third)
    for t in range(3):
        pair_copy(0, t).wait_send()
    stage_qkv(2)
    for t in range(3):
        pair_copy(1, t).wait_send()
    stage_pair(3, lambda t: dot(o_t[...], mg[:, t * BLOCK : t * BLOCK + BLOCK]))
    stage_a(2)
    do_tok[...] = o_t[...].T
    stage_a(3)

    @pl.loop(0, 3)
    def _(c):
        cols = pl.ds(pl.multiple_of(c * BLOCK, BLOCK), BLOCK)
        mixed = x[:, cols].astype(F32) + dot(do_tok[...], wout[:, cols])
        q_tok[:, cols] = (mixed * val[:SLOTS, :1]).astype(BF16)

    store = pltpu.make_async_copy(q_tok, att_ref, load.at[0])
    store.start()
    stage_out(1)
    for stage in (stage_b, stage_c, stage_out):
        stage(2)
        stage(3)
    for r in range(4):
        sent(r)
    for r in (2, 3):
        for t in range(3):
            pair_copy(r, t).wait_send()
    store.wait()


def whole(feats, gain, w_embed, target, cot, w_qkv, w_out, factor):
    tall, wide, square = (KEYS, WIDTH), (WIDTH, KEYS), (SLOTS, WIDTH)
    vmem, anywhere = pl.BlockSpec(memory_space=pltpu.VMEM), pl.BlockSpec(memory_space=pl.ANY)
    dma = pltpu.SemaphoreType.DMA
    half16 = lambda *shapes: [pltpu.VMEM(shape, BF16) for shape in shapes]
    full32 = lambda *shapes: [pltpu.VMEM(shape, F32) for shape in shapes]
    scratch = half16(square, square, (6, 8, 16, WIDTH)) + full32((KEYS, 128)) + half16((KEYS, 128))
    scratch += half16(square, tall, tall, square, square, wide, wide, square, wide, square, square, square)
    scratch += half16((128, SLOTS), (2, SLOTS, BLOCK), (2, KEYS, 2 * BLOCK))
    scratch += full32((KEYS, BLOCK), (KEYS, BLOCK)) + half16(tall, tall, tall, tall)
    scratch += half16(*[(KEYS, 128)] * 2, *[(128, SLOTS)] * 4, *[(SLOTS, 128)] * 4, (3, WIDTH, WIDTH))
    scratch += full32((16, 8, 128), (16, 8, 128), (16, 128), (8, 16, 128)) + half16((6, 16, WIDTH))
    scratch += half16((2, 3, WIDTH, BLOCK), (4, 3, 384, BLOCK), (4, 3, 384, BLOCK), (4, 3, 3, 96, BLOCK))
    scratch += full32((4, 3, 96, BLOCK), (4, 3, 3, 24, BLOCK), (4, 3, SIDE, 8, BLOCK), (4, 3, 3, 8, BLOCK))
    scratch += [dma((8,)), dma((3, 15)), dma((3, 15)), dma((15,)), dma((15,)), dma((7,)), dma((7,))]
    scratch += [dma((4,))] * 4 + [dma((4, 3))] * 2 + [dma((4, 3, 3))] * 6
    return pl.pallas_call(
        functools.partial(whole_kernel, factor),
        out_shape=(
            jax.ShapeDtypeStruct(square, BF16),
            jax.ShapeDtypeStruct((6, 3 * WIDTH), F32),
            jax.ShapeDtypeStruct((6, WIDTH), F32),
        ),
        in_specs=[anywhere, vmem, anywhere, vmem, anywhere, anywhere, anywhere, vmem],
        out_specs=(anywhere, vmem, vmem),
        scratch_shapes=scratch,
        compiler_params=pltpu.CompilerParams(
            collective_id=1, has_side_effects=True, vmem_limit_bytes=63 * 1024 * 1024
        ),
        cost_estimate=pl.CostEstimate(flops=30_000_000_000, bytes_accessed=16_000_000, transcendentals=14_000_000),
        name="whole",
    )(feats, gain, w_embed, target, cot, w_qkv, w_out, jnp.asarray(row_orders()))


def hand_over_kernel(*refs):
    ins, outs, held, sem_in, sem_out = refs[:3], refs[3:6], refs[6:9], refs[9], refs[10]
    pieces = [(0, slice(first, first + 192)) for first in range(0, SLOTS, 192)] + [(1, slice(0, 6)), (2, slice(0, 6))]
    arriving, leaving = [], []
    for n, (which, rows) in enumerate(pieces):
        arriving.append(pltpu.make_async_copy(ins[which].at[rows], held[which].at[rows], sem_in.at[n]))
        leaving.append(pltpu.make_async_copy(held[which].at[rows], outs[which].at[rows], sem_out.at[n]))
    for copy in arriving:
        copy.start()
    for first, second in zip(arriving, leaving):
        first.wait()
        second.start()
    for copy in leaving:
        copy.wait()


def hand_over(*arrays):
    anywhere = pl.BlockSpec(memory_space=pl.ANY)
    return pl.pallas_call(
        hand_over_kernel,
        out_shape=tuple(jax.ShapeDtypeStruct(a.shape, a.dtype) for a in arrays),
        in_specs=[anywhere] * 3,
        out_specs=(anywhere,) * 3,
        scratch_shapes=[pltpu.VMEM(a.shape, a.dtype) for a in arrays] + [pltpu.SemaphoreType.DMA((6,))] * 2,
        compiler_params=pltpu.CompilerParams(vmem_limit_bytes=63 * 1024 * 1024),
        name="hand_over",
    )(*arrays)


def shards(tile_feats, norm_gain, w_embed, slide_of_tile, w_qkv, w_out, cotangent):
    factor = (lax.axis_size("slide") * lax.axis_size("seq") * SLOTS) ** (-0.5)
    output, grad_qkv, grad_out = hand_over(*whole(
        tile_feats, norm_gain, w_embed, slide_of_tile.reshape(1, TILES),
        cotangent[0], w_qkv, w_out, factor,
    ))
    return (output[None], grad_qkv, grad_out)


def solution(mesh):
    return jax.shard_map(
        shards,
        mesh=mesh,
        in_specs=(
            P(("slide", "seq"), None),
            P(),
            P(),
            P(("slide", "seq"), None),
            P(),
            P(),
            P("slide", "seq", None),
        ),
        out_specs=(P("slide", "seq", None), P(("slide", "seq"), None), P(("slide", "seq"), None)),
        check_vma=False,
    )
```

```python
import functools

import jax
import jax.numpy as jnp
import numpy as np
from jax import lax
from jax.experimental import pallas as pl
from jax.experimental.pallas import tpu as pltpu
from jax.sharding import PartitionSpec as P

HEADS = 12
CAP = 48
RATE = 8
WIDTH = 768
WIDE = 1536
TILES = 384
SLOTS = 768
KEYS = 1536
BLOCK = 256
CHAIN = 128
PIECES = KEYS // CHAIN
SIDE = 4
MASKED = -1e30
BF16 = jnp.bfloat16
F32 = jnp.float32
MESH = pl.DeviceIdType.MESH
ORDERS = (("x", "y", "z"), ("y", "z", "x"), ("z", "x", "y"))
NT = (((1,), (1,)), ((), ()))


def row_orders():
    feature = np.arange(WIDTH)
    device, inner = feature // 6, feature % 6
    at = {"core": device % 2, "z": device // 2 % 4, "x": device // 8 % 4, "y": device // 32}
    places = [
        at["core"] * 384 + at[a] * 96 + at[b] * 24 + at[c] * 6 + inner for a, b, c in ORDERS
    ]
    return np.broadcast_to(np.stack(places)[:, None, :], (3, 8, WIDTH)).astype(np.int32)


def dot(a, b):
    return jnp.dot(a, b, preferred_element_type=F32)


def whole_kernel(
    factor,
    feats_ref, gain_ref, we_ref, target_ref, cot_ref, wqkv_ref, wout_ref, place_ref,
    att_ref, oq_ref, oo_ref,
    x, xd, val, bias, q_tok, k_tok, v_tok, do_tok, q_t, k_t, v_t, do_t, x_t, mg, o_t, wout,
    dq_t, dq_round, dkv, score_0, score_1, prob_0, prob_1, grad_0, grad_1,
    key_0, key_1, q_0, q_1, do_0, do_1, qc_0, qc_1, dc_0, dc_1, perm,
    tally, near_all, near, far, own_far,
    g, half, pair_sum, from_a, owned, from_b, spread, from_c,
    load, send_x, recv_x, send_n, recv_n, send_f, recv_f, send_z, recv_z, send_s, recv_s,
    send0, recv0, send_a, recv_a, send_b, recv_b, send_c, recv_c,
):
    scores, prob, grad = (score_0, score_1), (prob_0, prob_1), (grad_0, grad_1)
    keys, q_rows, do_rows = (key_0, key_1), (q_0, q_1), (do_0, do_1)
    q_cat, do_cat = (qc_0, qc_1), (dc_0, dc_1)
    slide, seq = lax.axis_index("slide"), lax.axis_index("seq")
    at = {"y": slide // SIDE, "x": slide % SIDE, "z": seq // 2}
    z, core = at["z"], seq % 2
    sibling = (slide, z * 2 + 1 - core)
    slides = [(lax.rem(slide + k, 16), seq) for k in range(1, 16)]
    blocks = [(slide, lax.rem(seq + k, 8)) for k in range(1, 8)]

    barrier = pltpu.get_barrier_semaphore()
    for device in slides + blocks:
        pl.semaphore_signal(barrier, inc=1, device_id=device, device_id_type=MESH)

    def remote(src, dst, send, recv, device):
        return pltpu.make_async_remote_copy(
            src_ref=src, dst_ref=dst, send_sem=send, recv_sem=recv, device_id=device, device_id_type=MESH
        )

    def begin(*args):
        copy = remote(*args)
        copy.start()
        return copy

    feats, normed, placed, w_e, w_q, w_k, w_v = (
        grad_0.at[:SLOTS], grad_1.at[:SLOTS], grad_1.at[SLOTS:], prob_1,
        prob_0.at[:SLOTS], prob_0.at[SLOTS:], grad_0.at[SLOTS:],
    )
    sources = [
        (feats_ref.at[:, :WIDTH], feats.at[:TILES]), (feats_ref.at[:, WIDTH:], feats.at[TILES:]),
        (we_ref, w_e), (cot_ref, mg), (wout_ref, wout),
        (wqkv_ref.at[:, :WIDTH], w_q), (wqkv_ref.at[:, WIDTH : 2 * WIDTH], w_k), (wqkv_ref.at[:, 2 * WIDTH :], w_v),
    ]
    loads = [pltpu.make_async_copy(src, dst, load.at[n]) for n, (src, dst) in enumerate(sources)]
    for copy in loads:
        copy.start()

    target = target_ref[...]
    named = lax.broadcasted_iota(jnp.int32, (16, TILES), 0) == target
    one_hot = jnp.where(named, 1.0, 0.0)
    earlier = (
        lax.broadcasted_iota(jnp.int32, (TILES, TILES), 0) < lax.broadcasted_iota(jnp.int32, (TILES, TILES), 1)
    ).astype(BF16)
    before_it = dot(one_hot.astype(BF16), earlier)
    rank = jnp.sum(one_hot * before_it, axis=0, keepdims=True)
    slot = target * CAP + rank.astype(jnp.int32)
    placing = x_t.at[:, :TILES]
    placing[...] = (lax.broadcasted_iota(jnp.int32, (SLOTS, TILES), 0) == slot).astype(BF16)
    total = jnp.sum(one_hot, axis=1, keepdims=True)
    for d in range(16):
        tally[d] = jnp.broadcast_to(total[d : d + 1], (8, 128))
    loads[0].wait()
    loads[1].wait()

    @pl.loop(0, 4)
    def _(c):
        low = pl.ds(pl.multiple_of(c * 96, 96), 96)
        high = pl.ds(pl.multiple_of(c * 96 + TILES, 96), 96)
        values = [feats[low, :].astype(F32), feats[high, :].astype(F32)]
        center = sum(jnp.sum(v, axis=-1, keepdims=True) for v in values) * (1.0 / WIDE)
        moved = [v - center for v in values]
        spread_sq = sum(jnp.sum(v * v, axis=-1, keepdims=True) for v in moved) * (1.0 / WIDE)
        scale = lax.rsqrt(spread_sq + 1e-06)
        normed[low, :] = (moved[0] * scale * gain_ref[:WIDTH].reshape(1, WIDTH)).astype(BF16)
        normed[high, :] = (moved[1] * scale * gain_ref[WIDTH:].reshape(1, WIDTH)).astype(BF16)

    pl.semaphore_wait(barrier, 22)
    near_copies = [
        begin(tally.at[dev[0]], near_all.at[slide], send_n.at[k], recv_n.at[k], dev) for k, dev in enumerate(slides)
    ]
    near_all[slide] = tally[slide]
    loads[2].wait()
    x_copies = []
    for part in range(2):
        cols = slice(part * 384, part * 384 + 384)
        embedded = dot(normed[:TILES, :], w_e[:WIDTH, cols]) + dot(normed[TILES:, :], w_e[WIDTH:, cols])
        o_t[:TILES, cols] = embedded.astype(BF16)
        placed[:, cols] = dot(placing[...], o_t[:TILES, cols]).astype(BF16)
        for k in (7, 8, 6, 9, 5, 10, 4, 11, 3, 12, 2, 13, 1, 14, 0):
            dev = slides[k]
            src = placed.at[pl.ds(pl.multiple_of(dev[0] * CAP, CAP), CAP), cols]
            dst = x.at[pl.ds(pl.multiple_of(slide * CAP, CAP), CAP), cols]
            x_copies.append(begin(src, dst, send_x.at[part, k], recv_x.at[part, k], dev))
    own = pl.ds(pl.multiple_of(slide * CAP, CAP), CAP)
    x[own, :] = placed[own, :]

    for copy in near_copies:
        copy.wait_recv()
    for i in range(16):
        near[i : i + 1, :] = near_all[i][:1]
    far_copies = [begin(near, far.at[seq], send_f.at[k], recv_f.at[k], dev) for k, dev in enumerate(blocks)]
    far[seq] = near[...]
    place_in = lax.broadcasted_iota(jnp.int32, (CAP, 128), 0).astype(F32)
    for i in range(16):
        val[i * CAP : i * CAP + CAP, :] = jnp.where(place_in < near[i : i + 1, :], 1.0, 0.0)
    for t in range(3):
        perm[t] = (lax.broadcasted_iota(jnp.int32, (WIDTH, WIDTH), 0) == place_ref[t][:1, :]).astype(BF16)
    row = lax.broadcasted_iota(jnp.int32, (64, SLOTS), 0)
    filler = jnp.where(row == 0, 1.0, 0.0).astype(BF16)
    zeros = jnp.zeros((64, SLOTS), BF16)
    q_0[64:, :], q_1[:64, :] = filler, filler
    do_0[64:, :], do_1[:64, :] = zeros, zeros
    for copy in loads[3:]:
        copy.wait()
    mg_val = val[:SLOTS, :].astype(BF16)
    for c in range(6):
        cols = slice(c * 128, c * 128 + 128)
        mg[:, cols] = mg[:, cols] * mg_val

    @pl.loop(0, 3)
    def _(c):
        cols = pl.ds(pl.multiple_of(c * BLOCK, BLOCK), BLOCK)
        d_heads = lax.dot_general(mg[...], wout[cols, :], NT, preferred_element_type=F32).astype(BF16)
        do_tok[:, cols] = d_heads
        do_t[cols, :] = d_heads.T

    row = lax.broadcasted_iota(jnp.int32, (96, SLOTS), 0)
    pick = lax.broadcasted_iota(jnp.int32, (96, SLOTS), 1) == (row % 16) * CAP + (row // 16) * RATE
    pick = pick.astype(BF16)
    for copy in x_copies:
        copy.wait_recv()
    rows = dot(pick, x[...]).astype(BF16)
    for m in range(6):
        own_far[m] = rows[m * 16 : m * 16 + 16]

    up = (slide, lax.rem(z + 1, SIDE) * 2 + core)
    down = (slide, lax.rem(z + 3, SIDE) * 2 + core)
    across = lax.rem(z + 2, SIDE) * 2 + core
    to_up = begin(own_far, xd.at[:, seq], send_z.at[0], recv_z.at[0], up)
    to_down = begin(own_far, xd.at[:, seq], send_z.at[1], recv_z.at[1], down)
    to_side = [begin(own_far, xd.at[:, seq], send_s.at[0], recv_s.at[0], sibling)]
    xd[:, seq] = own_far[...]

    def project(first, rows_of):
        @pl.loop(0, 3)
        def _(c):
            cols = pl.ds(pl.multiple_of(c * BLOCK, BLOCK), BLOCK)
            x_t[cols, first : first + SLOTS] = rows_of(cols).T
            for w, tok, turned in ((w_k, k_tok, k_t), (w_v, v_tok, v_t)):
                part = dot(rows_of(slice(None)), w[:, cols]).astype(BF16)
                tok[first : first + SLOTS, cols] = part
                turned[cols, first : first + SLOTS] = part.T

    @pl.loop(0, 3)
    def _(c):
        cols = pl.ds(pl.multiple_of(c * BLOCK, BLOCK), BLOCK)
        query = dot(x[...], w_q[:, cols]).astype(BF16) * BF16(0.125)
        q_tok[:, cols] = query
        q_t[cols, :] = query.T

    to_up.wait_recv()
    relay_up = begin(xd.at[pl.ds(0, 3), down[1]], xd.at[pl.ds(0, 3), down[1]], send_z.at[2], recv_z.at[2], up)
    to_side.append(begin(xd.at[:, down[1]], xd.at[:, down[1]], send_s.at[1], recv_s.at[1], sibling))
    to_down.wait_recv()
    relay_down = begin(xd.at[pl.ds(3, 3), up[1]], xd.at[pl.ds(3, 3), up[1]], send_z.at[3], recv_z.at[3], down)
    to_side.append(begin(xd.at[:, up[1]], xd.at[:, up[1]], send_s.at[2], recv_s.at[2], sibling))

    project(0, lambda cols: x[:, cols])

    relay_up.wait_recv()
    relay_down.wait_recv()
    to_side.append(begin(xd.at[:, across], xd.at[:, across], send_s.at[3], recv_s.at[3], sibling))
    for copy in far_copies:
        copy.wait_recv()
    for m in range(6):
        for j in range(8):
            first = SLOTS + m * 128 + j * 16
            val[first : first + 16, :] = jnp.where(far[j] > m * RATE, 1.0, 0.0)
    bias[...] = jnp.where(val[...] > 0.5, 0.0, MASKED).astype(BF16)
    for copy in to_side:
        copy.wait_recv()

    project(SLOTS, lambda cols: xd[:, :, :, cols].reshape(SLOTS, WIDTH if isinstance(cols, slice) else BLOCK))

    for copy in to_side + far_copies + near_copies + x_copies + [to_up, to_down, relay_up, relay_down]:
        copy.wait_send()

    def close_keys(pair, a, which, half_of):
        rows = slice(half_of * SLOTS, half_of * SLOTS + SLOTS)
        mine = lax.broadcasted_iota(jnp.int32, (SLOTS, 128), 1) // 64 == a
        slot = lax.rem(pair // 2, 2)
        left, right, offset = ((prob[a], do_cat[a], BLOCK), (grad[a], q_cat[a], 0))[which]
        lanes = pl.ds(pl.multiple_of(lax.rem(pair, 2) * 128 + offset, 128), 128)
        part = dot(left[rows, :], right[...]).astype(BF16)
        dkv[slot, rows, lanes] = jnp.where(mine, part, dkv[slot, rows, lanes])

    own_half = pl.multiple_of(core * 384, 384)
    its_half = pl.multiple_of((1 - core) * 384, 384)

    def parity(r):
        return r % 2 if isinstance(r, int) else lax.rem(r, 2)

    def axis_copies(r, t, axis, source, landing, send, recv, height):
        copies = []
        for d in (2, 1, 3):
            moved = dict(at)
            moved[axis] = lax.rem(at[axis] + d, SIDE)
            device = (moved["y"] * SIDE + moved["x"], moved["z"] * 2 + core)
            if height:
                src = source.at[r, t, pl.ds(pl.multiple_of(moved[axis] * height, height), height), :]
            else:
                src = source.at[r, t, moved[axis]]
            copies.append(remote(src, landing.at[r, t, d - 1], send.at[r, t, d - 1], recv.at[r, t, d - 1], device))
        return copies

    def pair_copy(r, t):
        src = g.at[parity(r), t, pl.ds(its_half, 384), :]
        return remote(src, half.at[r, t], send0.at[r, t], recv0.at[r, t], sibling)

    def a_copies(r, t):
        return axis_copies(r, t, ORDERS[t][0], pair_sum, from_a, send_a, recv_a, 96)

    def b_copies(r, t):
        return axis_copies(r, t, ORDERS[t][1], owned, from_b, send_b, recv_b, 24)

    def c_copies(r, t):
        return axis_copies(r, t, ORDERS[t][2], spread, from_c, send_c, recv_c, 0)

    def stage_pair(r, parts):
        for t in range(3):
            g[parity(r), t] = dot(perm[t], parts(t).astype(BF16)).astype(BF16)
            pair_copy(r, t).start()

    def stage_qkv(r):
        slot = parity(r)

        query_part = dot(x_t[:, :SLOTS], dq_round[slot])

        def parts(t):
            if t == 0:
                return query_part
            if t == 1:
                both.append(dot(x_t[...], dkv[slot]))
            return both[0][:, (t - 1) * BLOCK : t * BLOCK]

        both = []
        stage_pair(r, parts)

    def stage_a(r):
        for t in range(3):
            copy = pair_copy(r, t)
            copy.wait_recv()
            mine = g[parity(r), t, pl.ds(own_half, 384), :].astype(F32)
            pair_sum[r, t] = (mine + half[r, t].astype(F32)).astype(BF16)
            for copy in a_copies(r, t):
                copy.start()

    def stage_b(r):
        for t in range(3):
            mine = pl.multiple_of(at[ORDERS[t][0]] * 96, 96)
            total = g[parity(r), t, pl.ds(pl.multiple_of(own_half + mine, 96), 96), :].astype(F32)
            total = total + half[r, t, pl.ds(mine, 96), :].astype(F32)
            for copy in a_copies(r, t):
                copy.wait_recv()
            for d in range(3):
                total = total + from_a[r, t, d].astype(F32)
            owned[r, t] = total
            for copy in b_copies(r, t):
                copy.start()

    def stage_c(r):
        for t in range(3):
            total = owned[r, t, pl.ds(pl.multiple_of(at[ORDERS[t][1]] * 24, 24), 24), :]
            for copy in b_copies(r, t):
                copy.wait_recv()
            for d in range(3):
                total = total + from_b[r, t, d]
            for c in range(SIDE):
                spread[r, t, c, :6, :] = total[c * 6 : c * 6 + 6]
                spread[r, t, c, 6:, :] = jnp.zeros((2, BLOCK), F32)
            for copy in c_copies(r, t):
                copy.start()

    def stage_out(r):
        for t in range(3):
            total = spread[r, t, at[ORDERS[t][2]]]
            for copy in c_copies(r, t):
                copy.wait_recv()
            for d in range(3):
                total = total + from_c[r, t, d]
            total = total[:6] * factor
            if r < 3:
                first = t * WIDTH + r * BLOCK
                oq_ref[:, first : first + BLOCK] = total
            else:
                oo_ref[:, t * BLOCK : t * BLOCK + BLOCK] = total

    def sent(r):
        for t in range(3):
            for copy in a_copies(r, t) + b_copies(r, t) + c_copies(r, t):
                copy.wait_send()

    @pl.loop(0, HEADS // 2)
    def _(pair):
        lanes = pl.ds(pl.multiple_of(pair * 128, 128), 128)
        before = lax.max(pair - 1, 0)
        done = lax.max(pair // 2 - 1, 0)
        lane = lax.broadcasted_iota(jnp.int32, (KEYS, 128), 1)
        lane_q = lax.broadcasted_iota(jnp.int32, (SLOTS, 128), 1)
        nothing = jnp.zeros((SLOTS, 128), BF16)

        def head_rows(a):
            return pl.ds(pl.multiple_of(pair * 128 + a * 64, 64), 64)

        def open_head(a):
            own = slice(a * 64, a * 64 + 64)
            keys[a][...] = jnp.where(lane // 64 == a, k_tok[:, lanes], bias[...])
            q_rows[a][own, :] = q_t[head_rows(a), :]
            do_rows[a][own, :] = do_t[head_rows(a), :]

        def score_piece(step, piece):
            a, block = step // 3, step % 3
            rows = slice(piece * CHAIN, piece * CHAIN + CHAIN)
            s = dot(keys[a][rows, :], q_rows[a][:, block * BLOCK : block * BLOCK + BLOCK])
            peak = jnp.max(s, axis=0, keepdims=True)
            raw = jnp.exp(s - peak)
            scores[step % 2][rows, :] = raw
            return peak, jnp.sum(raw, axis=0, keepdims=True)

        def factors(parts):
            peak = functools.reduce(jnp.maximum, [p for p, _ in parts])
            weights = [jnp.exp(p - peak) for p, _ in parts]
            inverse = 1.0 / sum(w * total for w, (_, total) in zip(weights, parts))
            return [w * inverse for w in weights]

        open_head(0)
        parts = [score_piece(0, piece) for piece in range(PIECES)]
        open_head(1)
        for step in range(6):
            a, block = step // 3, step % 3
            cols = slice(block * BLOCK, block * BLOCK + BLOCK)
            score = scores[step % 2]
            factor_of = factors(parts)
            parts = []
            for piece in range(PIECES):
                rows = slice(piece * CHAIN, piece * CHAIN + CHAIN)
                prob[a][rows, cols] = (score[rows, :] * factor_of[piece]).astype(BF16)
                if step < 5:
                    parts.append(score_piece(step + 1, piece))
            out = dot(v_t[head_rows(a), :], prob[a][:, cols]).astype(BF16)
            o_t[head_rows(a), cols] = out
            for which, half_of in (((0, 0),), ((0, 1), (1, 0)), ((1, 1),))[block]:
                close_keys(before if a == 0 else pair, 1 - a, which, half_of)
            delta = jnp.sum(do_t[head_rows(a), cols].astype(F32) * out.astype(F32), axis=0, keepdims=True)
            for piece in range(PIECES):
                rows = slice(piece * CHAIN, piece * CHAIN + CHAIN)
                grad_p = dot(v_tok[rows, lanes], do_rows[a][:, cols])
                grad[a][rows, cols] = (score[rows, :] * ((grad_p - delta) * factor_of[piece])).astype(BF16)
            dq_t[a * 64 : a * 64 + 64, cols] = (dot(k_t[head_rows(a), :], grad[a][:, cols]) * 0.125).astype(BF16)
            if step == 2:
                @pl.when((pair == 2) | (pair == 4))
                def _():
                    stage_qkv(done)

                @pl.when((pair == 3) | (pair == 5))
                def _():
                    stage_b(done)

                @pl.when(pair == 4)
                def _():
                    stage_out(0)

            if block == 2:
                half_lanes = lane_q // 64 == a
                q_cat[a][...] = jnp.where(half_lanes, q_tok[:, lanes], nothing)
                do_cat[a][...] = jnp.where(half_lanes, do_tok[:, lanes], nothing)
        dq_round[lax.rem(pair // 2, 2), :, pl.ds(pl.multiple_of(lax.rem(pair, 2) * 128, 128), 128)] = dq_t[...].T

        @pl.when((pair == 2) | (pair == 4))
        def _():
            stage_a(done)

        @pl.when((pair == 3) | (pair == 5))
        def _():
            stage_c(done)

    for which in range(2):
        for half_of in range(2):
            close_keys(HEADS // 2 - 1, 1, which, half_of)
    for t in range(3):
        pair_copy(0, t).wait_send()
    stage_qkv(2)
    for t in range(3):
        pair_copy(1, t).wait_send()
    stage_pair(3, lambda t: dot(o_t[...], mg[:, t * BLOCK : t * BLOCK + BLOCK]))
    stage_a(2)
    do_tok[...] = o_t[...].T
    stage_a(3)

    @pl.loop(0, 3)
    def _(c):
        cols = pl.ds(pl.multiple_of(c * BLOCK, BLOCK), BLOCK)
        mixed = x[:, cols].astype(F32) + dot(do_tok[...], wout[:, cols])
        q_tok[:, cols] = (mixed * val[:SLOTS, :1]).astype(BF16)

    store = pltpu.make_async_copy(q_tok, att_ref, load.at[0])
    store.start()
    stage_out(1)
    for stage in (stage_b, stage_c, stage_out):
        stage(2)
        stage(3)
    for r in range(4):
        sent(r)
    for r in (2, 3):
        for t in range(3):
            pair_copy(r, t).wait_send()
    store.wait()


def whole(feats, gain, w_embed, target, cot, w_qkv, w_out, factor):
    tall, wide, square = (KEYS, WIDTH), (WIDTH, KEYS), (SLOTS, WIDTH)
    vmem, anywhere = pl.BlockSpec(memory_space=pltpu.VMEM), pl.BlockSpec(memory_space=pl.ANY)
    dma = pltpu.SemaphoreType.DMA
    half16 = lambda *shapes: [pltpu.VMEM(shape, BF16) for shape in shapes]
    full32 = lambda *shapes: [pltpu.VMEM(shape, F32) for shape in shapes]
    scratch = half16(square, (6, 8, 16, WIDTH)) + full32((KEYS, 128)) + half16((KEYS, 128))
    scratch += half16(square, tall, tall, square, square, wide, wide, square, wide, square, square, square)
    scratch += half16((128, SLOTS), (2, SLOTS, BLOCK), (2, KEYS, 2 * BLOCK))
    scratch += full32((KEYS, BLOCK), (KEYS, BLOCK)) + half16(tall, tall, tall, tall)
    scratch += half16(*[(KEYS, 128)] * 2, *[(128, SLOTS)] * 4, *[(SLOTS, 128)] * 4, (3, WIDTH, WIDTH))
    scratch += full32((16, 8, 128), (16, 8, 128), (16, 128), (8, 16, 128)) + half16((6, 16, WIDTH))
    scratch += half16((2, 3, WIDTH, BLOCK), (4, 3, 384, BLOCK), (4, 3, 384, BLOCK), (4, 3, 3, 96, BLOCK))
    scratch += full32((4, 3, 96, BLOCK), (4, 3, 3, 24, BLOCK), (4, 3, SIDE, 8, BLOCK), (4, 3, 3, 8, BLOCK))
    scratch += [dma((8,)), dma((2, 15)), dma((2, 15)), dma((15,)), dma((15,)), dma((7,)), dma((7,))]
    scratch += [dma((4,))] * 4 + [dma((4, 3))] * 2 + [dma((4, 3, 3))] * 6
    return pl.pallas_call(
        functools.partial(whole_kernel, factor),
        out_shape=(
            jax.ShapeDtypeStruct(square, BF16),
            jax.ShapeDtypeStruct((6, 3 * WIDTH), F32),
            jax.ShapeDtypeStruct((6, WIDTH), F32),
        ),
        in_specs=[anywhere, vmem, anywhere, vmem, anywhere, anywhere, anywhere, vmem],
        out_specs=(anywhere, vmem, vmem),
        scratch_shapes=scratch,
        compiler_params=pltpu.CompilerParams(
            collective_id=1, has_side_effects=True, vmem_limit_bytes=63 * 1024 * 1024
        ),
        cost_estimate=pl.CostEstimate(flops=30_000_000_000, bytes_accessed=16_000_000, transcendentals=14_000_000),
        name="whole",
    )(feats, gain, w_embed, target, cot, w_qkv, w_out, jnp.asarray(row_orders()))


def hand_over_kernel(*refs):
    ins, outs, held, sem_in, sem_out = refs[:3], refs[3:6], refs[6:9], refs[9], refs[10]
    pieces = [(0, slice(first, first + 192)) for first in range(0, SLOTS, 192)] + [(1, slice(0, 6)), (2, slice(0, 6))]
    arriving, leaving = [], []
    for n, (which, rows) in enumerate(pieces):
        arriving.append(pltpu.make_async_copy(ins[which].at[rows], held[which].at[rows], sem_in.at[n]))
        leaving.append(pltpu.make_async_copy(held[which].at[rows], outs[which].at[rows], sem_out.at[n]))
    for copy in arriving:
        copy.start()
    for first, second in zip(arriving, leaving):
        first.wait()
        second.start()
    for copy in leaving:
        copy.wait()


def hand_over(*arrays):
    anywhere = pl.BlockSpec(memory_space=pl.ANY)
    return pl.pallas_call(
        hand_over_kernel,
        out_shape=tuple(jax.ShapeDtypeStruct(a.shape, a.dtype) for a in arrays),
        in_specs=[anywhere] * 3,
        out_specs=(anywhere,) * 3,
        scratch_shapes=[pltpu.VMEM(a.shape, a.dtype) for a in arrays] + [pltpu.SemaphoreType.DMA((6,))] * 2,
        compiler_params=pltpu.CompilerParams(vmem_limit_bytes=63 * 1024 * 1024),
        name="hand_over",
    )(*arrays)


def shards(tile_feats, norm_gain, w_embed, slide_of_tile, w_qkv, w_out, cotangent):
    factor = (lax.axis_size("slide") * lax.axis_size("seq") * SLOTS) ** (-0.5)
    output, grad_qkv, grad_out = hand_over(*whole(
        tile_feats, norm_gain, w_embed, slide_of_tile.reshape(1, TILES),
        cotangent[0], w_qkv, w_out, factor,
    ))
    return (output[None], grad_qkv, grad_out)


def solution(mesh):
    return jax.shard_map(
        shards,
        mesh=mesh,
        in_specs=(
            P(("slide", "seq"), None),
            P(),
            P(),
            P(("slide", "seq"), None),
            P(),
            P(),
            P("slide", "seq", None),
        ),
        out_specs=(P("slide", "seq", None), P(("slide", "seq"), None), P(("slide", "seq"), None)),
        check_vma=False,
    )
```

```python
import functools

import jax
import jax.numpy as jnp
import numpy as np
from jax import lax
from jax.experimental import pallas as pl
from jax.experimental.pallas import tpu as pltpu
from jax.sharding import PartitionSpec as P

HEADS = 12
CAP = 48
RATE = 8
WIDTH = 768
WIDE = 1536
TILES = 384
SLOTS = 768
KEYS = 1536
BLOCK = 256
CHAIN = 128
PIECES = KEYS // CHAIN
SIDE = 4
MASKED = -1e30
BF16 = jnp.bfloat16
F32 = jnp.float32
MESH = pl.DeviceIdType.MESH
ORDERS = (("x", "y", "z"), ("y", "z", "x"), ("z", "x", "y"))
NT = (((1,), (1,)), ((), ()))


def row_orders():
    feature = np.arange(WIDTH)
    device, inner = feature // 6, feature % 6
    at = {"core": device % 2, "z": device // 2 % 4, "x": device // 8 % 4, "y": device // 32}
    places = [
        at["core"] * 384 + at[a] * 96 + at[b] * 24 + at[c] * 6 + inner for a, b, c in ORDERS
    ]
    return np.broadcast_to(np.stack(places)[:, None, :], (3, 8, WIDTH)).astype(np.int32)


def dot(a, b):
    return jnp.dot(a, b, preferred_element_type=F32)


def whole_kernel(
    factor,
    feats_ref, gain_ref, we_ref, target_ref, cot_ref, wqkv_ref, wout_ref, place_ref,
    att_ref, oq_ref, oo_ref,
    x, xd, val, bias, q_tok, k_tok, v_tok, do_tok, q_t, k_t, v_t, do_t, x_t, mg, o_t, wout,
    dq_t, dq_round, dkv, score_0, score_1, prob_0, prob_1, grad_0, grad_1,
    key_0, key_1, q_0, q_1, do_0, do_1, qc_0, qc_1, dc_0, dc_1, perm,
    tally, near_all, near, far, own_far,
    g, half, pair_sum, from_a, owned, from_b, spread, from_c,
    load, send_x, recv_x, send_n, recv_n, send_f, recv_f, send_z, recv_z, send_s, recv_s,
    send0, recv0, send_a, recv_a, send_b, recv_b, send_c, recv_c,
):
    scores, prob, grad = (score_0, score_1), (prob_0, prob_1), (grad_0, grad_1)
    keys, q_rows, do_rows = (key_0, key_1), (q_0, q_1), (do_0, do_1)
    q_cat, do_cat = (qc_0, qc_1), (dc_0, dc_1)
    slide, seq = lax.axis_index("slide"), lax.axis_index("seq")
    at = {"y": slide // SIDE, "x": slide % SIDE, "z": seq // 2}
    z, core = at["z"], seq % 2
    sibling = (slide, z * 2 + 1 - core)
    slides = [(lax.rem(slide + k, 16), seq) for k in range(1, 16)]
    blocks = [(slide, lax.rem(seq + k, 8)) for k in range(1, 8)]

    barrier = pltpu.get_barrier_semaphore()
    for device in slides + blocks:
        pl.semaphore_signal(barrier, inc=1, device_id=device, device_id_type=MESH)

    def remote(src, dst, send, recv, device):
        return pltpu.make_async_remote_copy(
            src_ref=src, dst_ref=dst, send_sem=send, recv_sem=recv, device_id=device, device_id_type=MESH
        )

    def begin(*args):
        copy = remote(*args)
        copy.start()
        return copy

    feats, normed, placed, w_e, w_q, w_k, w_v = (
        grad_0.at[:SLOTS], grad_1.at[:SLOTS], grad_1.at[SLOTS:], prob_1,
        prob_0.at[:SLOTS], prob_0.at[SLOTS:], grad_0.at[SLOTS:],
    )
    sources = [
        (feats_ref.at[:, :WIDTH], feats.at[:TILES]), (feats_ref.at[:, WIDTH:], feats.at[TILES:]),
        (we_ref, w_e), (cot_ref, mg), (wout_ref, wout),
        (wqkv_ref.at[:, :WIDTH], w_q), (wqkv_ref.at[:, WIDTH : 2 * WIDTH], w_k), (wqkv_ref.at[:, 2 * WIDTH :], w_v),
    ]
    loads = [pltpu.make_async_copy(src, dst, load.at[n]) for n, (src, dst) in enumerate(sources)]
    for copy in loads:
        copy.start()

    target = target_ref[...]
    named = lax.broadcasted_iota(jnp.int32, (16, TILES), 0) == target
    one_hot = jnp.where(named, 1.0, 0.0)
    earlier = (
        lax.broadcasted_iota(jnp.int32, (TILES, TILES), 0) < lax.broadcasted_iota(jnp.int32, (TILES, TILES), 1)
    ).astype(BF16)
    before_it = dot(one_hot.astype(BF16), earlier)
    rank = jnp.sum(one_hot * before_it, axis=0, keepdims=True)
    slot = target * CAP + rank.astype(jnp.int32)
    placing = x_t.at[:, :TILES]
    placing[...] = (lax.broadcasted_iota(jnp.int32, (SLOTS, TILES), 0) == slot).astype(BF16)
    total = jnp.sum(one_hot, axis=1, keepdims=True)
    for d in range(16):
        tally[d] = jnp.broadcast_to(total[d : d + 1], (8, 128))
    loads[0].wait()
    loads[1].wait()

    @pl.loop(0, 4)
    def _(c):
        low = pl.ds(pl.multiple_of(c * 96, 96), 96)
        high = pl.ds(pl.multiple_of(c * 96 + TILES, 96), 96)
        values = [feats[low, :].astype(F32), feats[high, :].astype(F32)]
        center = sum(jnp.sum(v, axis=-1, keepdims=True) for v in values) * (1.0 / WIDE)
        moved = [v - center for v in values]
        spread_sq = sum(jnp.sum(v * v, axis=-1, keepdims=True) for v in moved) * (1.0 / WIDE)
        scale = lax.rsqrt(spread_sq + 1e-06)
        normed[low, :] = (moved[0] * scale * gain_ref[:WIDTH].reshape(1, WIDTH)).astype(BF16)
        normed[high, :] = (moved[1] * scale * gain_ref[WIDTH:].reshape(1, WIDTH)).astype(BF16)

    pl.semaphore_wait(barrier, 22)
    near_copies = [
        begin(tally.at[dev[0]], near_all.at[slide], send_n.at[k], recv_n.at[k], dev) for k, dev in enumerate(slides)
    ]
    near_all[slide] = tally[slide]
    loads[2].wait()
    x_copies = []
    for part in range(2):
        cols = slice(part * 384, part * 384 + 384)
        embedded = dot(normed[:TILES, :], w_e[:WIDTH, cols]) + dot(normed[TILES:, :], w_e[WIDTH:, cols])
        o_t[:TILES, cols] = embedded.astype(BF16)
        placed[:, cols] = dot(placing[...], o_t[:TILES, cols]).astype(BF16)
        for k in (7, 8, 6, 9, 5, 10, 4, 11, 3, 12, 2, 13, 1, 14, 0):
            dev = slides[k]
            src = placed.at[pl.ds(pl.multiple_of(dev[0] * CAP, CAP), CAP), cols]
            dst = x.at[pl.ds(pl.multiple_of(slide * CAP, CAP), CAP), cols]
            x_copies.append(begin(src, dst, send_x.at[part, k], recv_x.at[part, k], dev))
    own = pl.ds(pl.multiple_of(slide * CAP, CAP), CAP)
    x[own, :] = placed[own, :]

    for copy in near_copies:
        copy.wait_recv()
    for i in range(16):
        near[i : i + 1, :] = near_all[i][:1]
    far_copies = [begin(near, far.at[seq], send_f.at[k], recv_f.at[k], dev) for k, dev in enumerate(blocks)]
    far[seq] = near[...]
    place_in = lax.broadcasted_iota(jnp.int32, (CAP, 128), 0).astype(F32)
    for i in range(16):
        val[i * CAP : i * CAP + CAP, :] = jnp.where(place_in < near[i : i + 1, :], 1.0, 0.0)
    for t in range(3):
        perm[t] = (lax.broadcasted_iota(jnp.int32, (WIDTH, WIDTH), 0) == place_ref[t][:1, :]).astype(BF16)
    row = lax.broadcasted_iota(jnp.int32, (64, SLOTS), 0)
    filler = jnp.where(row == 0, 1.0, 0.0).astype(BF16)
    zeros = jnp.zeros((64, SLOTS), BF16)
    q_0[64:, :], q_1[:64, :] = filler, filler
    do_0[64:, :], do_1[:64, :] = zeros, zeros
    for copy in loads[3:]:
        copy.wait()
    mg_val = val[:SLOTS, :].astype(BF16)
    for c in range(6):
        cols = slice(c * 128, c * 128 + 128)
        mg[:, cols] = mg[:, cols] * mg_val

    @pl.loop(0, 3)
    def _(c):
        cols = pl.ds(pl.multiple_of(c * BLOCK, BLOCK), BLOCK)
        d_heads = lax.dot_general(mg[...], wout[cols, :], NT, preferred_element_type=F32).astype(BF16)
        do_tok[:, cols] = d_heads
        do_t[cols, :] = d_heads.T

    row = lax.broadcasted_iota(jnp.int32, (96, SLOTS), 0)
    pick = lax.broadcasted_iota(jnp.int32, (96, SLOTS), 1) == (row % 16) * CAP + (row // 16) * RATE
    pick = pick.astype(BF16)
    for copy in x_copies:
        copy.wait_recv()
    rows = dot(pick, x[...]).astype(BF16)
    for m in range(6):
        own_far[m] = rows[m * 16 : m * 16 + 16]

    up = (slide, lax.rem(z + 1, SIDE) * 2 + core)
    down = (slide, lax.rem(z + 3, SIDE) * 2 + core)
    across = lax.rem(z + 2, SIDE) * 2 + core
    to_up = begin(own_far, xd.at[:, seq], send_z.at[0], recv_z.at[0], up)
    to_down = begin(own_far, xd.at[:, seq], send_z.at[1], recv_z.at[1], down)
    to_side = [begin(own_far, xd.at[:, seq], send_s.at[0], recv_s.at[0], sibling)]
    xd[:, seq] = own_far[...]

    def project(first, rows_of):
        @pl.loop(0, 3)
        def _(c):
            cols = pl.ds(pl.multiple_of(c * BLOCK, BLOCK), BLOCK)
            x_t[cols, first : first + SLOTS] = rows_of(cols).T
            for w, tok, turned in ((w_k, k_tok, k_t), (w_v, v_tok, v_t)):
                part = dot(rows_of(slice(None)), w[:, cols]).astype(BF16)
                tok[first : first + SLOTS, cols] = part
                turned[cols, first : first + SLOTS] = part.T

    @pl.loop(0, 3)
    def _(c):
        cols = pl.ds(pl.multiple_of(c * BLOCK, BLOCK), BLOCK)
        query = dot(x[...], w_q[:, cols]).astype(BF16) * BF16(0.125)
        q_tok[:, cols] = query
        q_t[cols, :] = query.T

    to_up.wait_recv()
    relay_up = begin(xd.at[pl.ds(0, 3), down[1]], xd.at[pl.ds(0, 3), down[1]], send_z.at[2], recv_z.at[2], up)
    to_side.append(begin(xd.at[:, down[1]], xd.at[:, down[1]], send_s.at[1], recv_s.at[1], sibling))
    to_down.wait_recv()
    relay_down = begin(xd.at[pl.ds(3, 3), up[1]], xd.at[pl.ds(3, 3), up[1]], send_z.at[3], recv_z.at[3], down)
    to_side.append(begin(xd.at[:, up[1]], xd.at[:, up[1]], send_s.at[2], recv_s.at[2], sibling))

    project(0, lambda cols: x[:, cols])

    relay_up.wait_recv()
    relay_down.wait_recv()
    to_side.append(begin(xd.at[:, across], xd.at[:, across], send_s.at[3], recv_s.at[3], sibling))
    for copy in far_copies:
        copy.wait_recv()
    for m in range(6):
        for j in range(8):
            first = SLOTS + m * 128 + j * 16
            val[first : first + 16, :] = jnp.where(far[j] > m * RATE, 1.0, 0.0)
    bias[...] = jnp.where(val[...] > 0.5, 0.0, MASKED).astype(BF16)
    for copy in to_side:
        copy.wait_recv()

    project(SLOTS, lambda cols: xd[:, :, :, cols].reshape(SLOTS, WIDTH if isinstance(cols, slice) else BLOCK))

    for copy in to_side + far_copies + near_copies + x_copies + [to_up, to_down, relay_up, relay_down]:
        copy.wait_send()

    def close_keys(pair, a, which, half_of):
        rows = slice(half_of * SLOTS, half_of * SLOTS + SLOTS)
        mine = lax.broadcasted_iota(jnp.int32, (SLOTS, 128), 1) // 64 == a
        slot = lax.rem(pair // 2, 2)
        left, right, offset = ((prob[a], do_cat[a], BLOCK), (grad[a], q_cat[a], 0))[which]
        lanes = pl.ds(pl.multiple_of(lax.rem(pair, 2) * 128 + offset, 128), 128)
        part = dot(left[rows, :], right[...]).astype(BF16)
        dkv[slot, rows, lanes] = jnp.where(mine, part, dkv[slot, rows, lanes])

    own_half = pl.multiple_of(core * 384, 384)
    its_half = pl.multiple_of((1 - core) * 384, 384)

    def parity(r):
        return r % 2 if isinstance(r, int) else lax.rem(r, 2)

    def axis_copies(r, t, axis, source, landing, send, recv, height):
        copies = []
        for d in (2, 1, 3):
            moved = dict(at)
            moved[axis] = lax.rem(at[axis] + d, SIDE)
            device = (moved["y"] * SIDE + moved["x"], moved["z"] * 2 + core)
            if height:
                src = source.at[r, t, pl.ds(pl.multiple_of(moved[axis] * height, height), height), :]
            else:
                src = source.at[r, t, moved[axis]]
            copies.append(remote(src, landing.at[r, t, d - 1], send.at[r, t, d - 1], recv.at[r, t, d - 1], device))
        return copies

    def pair_copy(r, t):
        src = g.at[parity(r), t, pl.ds(its_half, 384), :]
        return remote(src, half.at[r, t], send0.at[r, t], recv0.at[r, t], sibling)

    def a_copies(r, t):
        return axis_copies(r, t, ORDERS[t][0], pair_sum, from_a, send_a, recv_a, 96)

    def b_copies(r, t):
        return axis_copies(r, t, ORDERS[t][1], owned, from_b, send_b, recv_b, 24)

    def c_copies(r, t):
        return axis_copies(r, t, ORDERS[t][2], spread, from_c, send_c, recv_c, 0)

    def stage_pair(r, parts):
        for t in range(3):
            g[parity(r), t] = dot(perm[t], parts(t).astype(BF16)).astype(BF16)
            pair_copy(r, t).start()

    def stage_qkv(r):
        slot = parity(r)

        query_part = dot(x_t[:, :SLOTS], dq_round[slot])

        def parts(t):
            if t == 0:
                return query_part
            if t == 1:
                both.append(dot(x_t[...], dkv[slot]))
            return both[0][:, (t - 1) * BLOCK : t * BLOCK]

        both = []
        stage_pair(r, parts)

    def stage_a(r):
        for t in range(3):
            copy = pair_copy(r, t)
            copy.wait_recv()
            mine = g[parity(r), t, pl.ds(own_half, 384), :].astype(F32)
            pair_sum[r, t] = (mine + half[r, t].astype(F32)).astype(BF16)
            for copy in a_copies(r, t):
                copy.start()

    def stage_b(r):
        for t in range(3):
            mine = pl.multiple_of(at[ORDERS[t][0]] * 96, 96)
            total = g[parity(r), t, pl.ds(pl.multiple_of(own_half + mine, 96), 96), :].astype(F32)
            total = total + half[r, t, pl.ds(mine, 96), :].astype(F32)
            for copy in a_copies(r, t):
                copy.wait_recv()
            for d in range(3):
                total = total + from_a[r, t, d].astype(F32)
            owned[r, t] = total
            for copy in b_copies(r, t):
                copy.start()

    def stage_c(r):
        for t in range(3):
            total = owned[r, t, pl.ds(pl.multiple_of(at[ORDERS[t][1]] * 24, 24), 24), :]
            for copy in b_copies(r, t):
                copy.wait_recv()
            for d in range(3):
                total = total + from_b[r, t, d]
            for c in range(SIDE):
                spread[r, t, c, :6, :] = total[c * 6 : c * 6 + 6]
                spread[r, t, c, 6:, :] = jnp.zeros((2, BLOCK), F32)
            for copy in c_copies(r, t):
                copy.start()

    def stage_out(r):
        for t in range(3):
            total = spread[r, t, at[ORDERS[t][2]]]
            for copy in c_copies(r, t):
                copy.wait_recv()
            for d in range(3):
                total = total + from_c[r, t, d]
            total = total[:6] * factor
            if r < 3:
                first = t * WIDTH + r * BLOCK
                oq_ref[:, first : first + BLOCK] = total
            else:
                oo_ref[:, t * BLOCK : t * BLOCK + BLOCK] = total

    def sent(r):
        for t in range(3):
            for copy in a_copies(r, t) + b_copies(r, t) + c_copies(r, t):
                copy.wait_send()

    @pl.loop(0, HEADS // 2)
    def _(pair):
        lanes = pl.ds(pl.multiple_of(pair * 128, 128), 128)
        before = lax.max(pair - 1, 0)
        done = lax.max(pair // 2 - 1, 0)
        lane = lax.broadcasted_iota(jnp.int32, (KEYS, 128), 1)
        lane_q = lax.broadcasted_iota(jnp.int32, (SLOTS, 128), 1)
        nothing = jnp.zeros((SLOTS, 128), BF16)

        def head_rows(a):
            return pl.ds(pl.multiple_of(pair * 128 + a * 64, 64), 64)

        def open_head(a):
            own = slice(a * 64, a * 64 + 64)
            keys[a][...] = jnp.where(lane // 64 == a, k_tok[:, lanes], bias[...])
            q_rows[a][own, :] = q_t[head_rows(a), :]
            do_rows[a][own, :] = do_t[head_rows(a), :]

        def score_piece(step, piece):
            a, block = step // 3, step % 3
            rows = slice(piece * CHAIN, piece * CHAIN + CHAIN)
            s = dot(keys[a][rows, :], q_rows[a][:, block * BLOCK : block * BLOCK + BLOCK])
            peak = jnp.max(s, axis=0, keepdims=True)
            raw = jnp.exp(s - peak)
            scores[step % 2][rows, :] = raw
            return peak, jnp.sum(raw, axis=0, keepdims=True)

        def factors(parts):
            peak = functools.reduce(jnp.maximum, [p for p, _ in parts])
            weights = [jnp.exp(p - peak) for p, _ in parts]
            inverse = 1.0 / sum(w * total for w, (_, total) in zip(weights, parts))
            return [w * inverse for w in weights]

        open_head(0)
        parts = [score_piece(0, piece) for piece in range(PIECES)]
        open_head(1)
        for step in range(6):
            a, block = step // 3, step % 3
            cols = slice(block * BLOCK, block * BLOCK + BLOCK)
            score = scores[step % 2]
            closing = (before if a == 0 else pair, 1 - a)
            factor_of = factors(parts)
            parts = []
            for piece in range(PIECES):
                rows = slice(piece * CHAIN, piece * CHAIN + CHAIN)
                prob[a][rows, cols] = (score[rows, :] * factor_of[piece]).astype(BF16)
                if step < 5:
                    parts.append(score_piece(step + 1, piece))
                if piece == PIECES // 2 - 1:
                    close_keys(*closing, block // 2, block % 2)
            out = dot(v_t[head_rows(a), :], prob[a][:, cols]).astype(BF16)
            o_t[head_rows(a), cols] = out
            delta = jnp.sum(do_t[head_rows(a), cols].astype(F32) * out.astype(F32), axis=0, keepdims=True)
            for piece in range(PIECES):
                rows = slice(piece * CHAIN, piece * CHAIN + CHAIN)
                grad_p = dot(v_tok[rows, lanes], do_rows[a][:, cols])
                grad[a][rows, cols] = (score[rows, :] * ((grad_p - delta) * factor_of[piece])).astype(BF16)
                if block == 1 and piece == PIECES // 2 - 1:
                    close_keys(*closing, 1, 1)
            dq_t[a * 64 : a * 64 + 64, cols] = (dot(k_t[head_rows(a), :], grad[a][:, cols]) * 0.125).astype(BF16)
            if step == 2:
                @pl.when((pair == 2) | (pair == 4))
                def _():
                    stage_qkv(done)

                @pl.when((pair == 3) | (pair == 5))
                def _():
                    stage_b(done)

                @pl.when(pair == 4)
                def _():
                    stage_out(0)

            if block == 2:
                half_lanes = lane_q // 64 == a
                q_cat[a][...] = jnp.where(half_lanes, q_tok[:, lanes], nothing)
                do_cat[a][...] = jnp.where(half_lanes, do_tok[:, lanes], nothing)
        dq_round[lax.rem(pair // 2, 2), :, pl.ds(pl.multiple_of(lax.rem(pair, 2) * 128, 128), 128)] = dq_t[...].T

        @pl.when((pair == 2) | (pair == 4))
        def _():
            stage_a(done)

        @pl.when((pair == 3) | (pair == 5))
        def _():
            stage_c(done)

    for which in range(2):
        for half_of in range(2):
            close_keys(HEADS // 2 - 1, 1, which, half_of)
    for t in range(3):
        pair_copy(0, t).wait_send()
    stage_qkv(2)
    for t in range(3):
        pair_copy(1, t).wait_send()
    stage_pair(3, lambda t: dot(o_t[...], mg[:, t * BLOCK : t * BLOCK + BLOCK]))
    stage_a(2)
    do_tok[...] = o_t[...].T
    stage_a(3)

    @pl.loop(0, 3)
    def _(c):
        cols = pl.ds(pl.multiple_of(c * BLOCK, BLOCK), BLOCK)
        mixed = x[:, cols].astype(F32) + dot(do_tok[...], wout[:, cols])
        q_tok[:, cols] = (mixed * val[:SLOTS, :1]).astype(BF16)

    store = pltpu.make_async_copy(q_tok, att_ref, load.at[0])
    store.start()
    stage_out(1)
    for stage in (stage_b, stage_c, stage_out):
        stage(2)
        stage(3)
    for r in range(4):
        sent(r)
    for r in (2, 3):
        for t in range(3):
            pair_copy(r, t).wait_send()
    store.wait()


def whole(feats, gain, w_embed, target, cot, w_qkv, w_out, factor):
    tall, wide, square = (KEYS, WIDTH), (WIDTH, KEYS), (SLOTS, WIDTH)
    vmem, anywhere = pl.BlockSpec(memory_space=pltpu.VMEM), pl.BlockSpec(memory_space=pl.ANY)
    dma = pltpu.SemaphoreType.DMA
    half16 = lambda *shapes: [pltpu.VMEM(shape, BF16) for shape in shapes]
    full32 = lambda *shapes: [pltpu.VMEM(shape, F32) for shape in shapes]
    scratch = half16(square, (6, 8, 16, WIDTH)) + full32((KEYS, 128)) + half16((KEYS, 128))
    scratch += half16(square, tall, tall, square, square, wide, wide, square, wide, square, square, square)
    scratch += half16((128, SLOTS), (2, SLOTS, BLOCK), (2, KEYS, 2 * BLOCK))
    scratch += full32((KEYS, BLOCK), (KEYS, BLOCK)) + half16(tall, tall, tall, tall)
    scratch += half16(*[(KEYS, 128)] * 2, *[(128, SLOTS)] * 4, *[(SLOTS, 128)] * 4, (3, WIDTH, WIDTH))
    scratch += full32((16, 8, 128), (16, 8, 128), (16, 128), (8, 16, 128)) + half16((6, 16, WIDTH))
    scratch += half16((2, 3, WIDTH, BLOCK), (4, 3, 384, BLOCK), (4, 3, 384, BLOCK), (4, 3, 3, 96, BLOCK))
    scratch += full32((4, 3, 96, BLOCK), (4, 3, 3, 24, BLOCK), (4, 3, SIDE, 8, BLOCK), (4, 3, 3, 8, BLOCK))
    scratch += [dma((8,)), dma((2, 15)), dma((2, 15)), dma((15,)), dma((15,)), dma((7,)), dma((7,))]
    scratch += [dma((4,))] * 4 + [dma((4, 3))] * 2 + [dma((4, 3, 3))] * 6
    return pl.pallas_call(
        functools.partial(whole_kernel, factor),
        out_shape=(
            jax.ShapeDtypeStruct(square, BF16),
            jax.ShapeDtypeStruct((6, 3 * WIDTH), F32),
            jax.ShapeDtypeStruct((6, WIDTH), F32),
        ),
        in_specs=[anywhere, vmem, anywhere, vmem, anywhere, anywhere, anywhere, vmem],
        out_specs=(anywhere, vmem, vmem),
        scratch_shapes=scratch,
        compiler_params=pltpu.CompilerParams(
            collective_id=1, has_side_effects=True, vmem_limit_bytes=63 * 1024 * 1024
        ),
        cost_estimate=pl.CostEstimate(flops=30_000_000_000, bytes_accessed=16_000_000, transcendentals=14_000_000),
        name="whole",
    )(feats, gain, w_embed, target, cot, w_qkv, w_out, jnp.asarray(row_orders()))


def hand_over_kernel(*refs):
    ins, outs, held, sem_in, sem_out = refs[:3], refs[3:6], refs[6:9], refs[9], refs[10]
    pieces = [(0, slice(first, first + 192)) for first in range(0, SLOTS, 192)] + [(1, slice(0, 6)), (2, slice(0, 6))]
    arriving, leaving = [], []
    for n, (which, rows) in enumerate(pieces):
        arriving.append(pltpu.make_async_copy(ins[which].at[rows], held[which].at[rows], sem_in.at[n]))
        leaving.append(pltpu.make_async_copy(held[which].at[rows], outs[which].at[rows], sem_out.at[n]))
    for copy in arriving:
        copy.start()
    for first, second in zip(arriving, leaving):
        first.wait()
        second.start()
    for copy in leaving:
        copy.wait()


def hand_over(*arrays):
    anywhere = pl.BlockSpec(memory_space=pl.ANY)
    return pl.pallas_call(
        hand_over_kernel,
        out_shape=tuple(jax.ShapeDtypeStruct(a.shape, a.dtype) for a in arrays),
        in_specs=[anywhere] * 3,
        out_specs=(anywhere,) * 3,
        scratch_shapes=[pltpu.VMEM(a.shape, a.dtype) for a in arrays] + [pltpu.SemaphoreType.DMA((6,))] * 2,
        compiler_params=pltpu.CompilerParams(vmem_limit_bytes=63 * 1024 * 1024),
        name="hand_over",
    )(*arrays)


def shards(tile_feats, norm_gain, w_embed, slide_of_tile, w_qkv, w_out, cotangent):
    factor = (lax.axis_size("slide") * lax.axis_size("seq") * SLOTS) ** (-0.5)
    output, grad_qkv, grad_out = hand_over(*whole(
        tile_feats, norm_gain, w_embed, slide_of_tile.reshape(1, TILES),
        cotangent[0], w_qkv, w_out, factor,
    ))
    return (output[None], grad_qkv, grad_out)


def solution(mesh):
    return jax.shard_map(
        shards,
        mesh=mesh,
        in_specs=(
            P(("slide", "seq"), None),
            P(),
            P(),
            P(("slide", "seq"), None),
            P(),
            P(),
            P("slide", "seq", None),
        ),
        out_specs=(P("slide", "seq", None), P(("slide", "seq"), None), P(("slide", "seq"), None)),
        check_vma=False,
    )
```
